32 devices in a mesh: dp: 8 (over z, y), mp: 4 (over x, core).
Axes of the slice: x: 2, y: 2, z: 4, core: 2. Of those that a mesh axis runs over, the one named last changes fastest.
Arguments:
- tokens: bfloat16 [8192, 1536], P(('dp', 'mp')), may hold values from -6 to 6
- gain_attn: float32 [1536], replicated, may hold values from 0.5 to 1.5
- w_query: bfloat16 [1536, 768], P(None, 'mp'), may hold values from -0.01953125 to 0.01953125
- w_key: bfloat16 [1536, 768], P(None, 'mp'), may hold values from -0.15625 to 0.15625
- w_value: bfloat16 [1536, 768], P(None, 'mp'), may hold values from -0.15625 to 0.15625
- w_out: bfloat16 [768, 1536], P('mp'), may hold values from -6 to 6
- bias_table: float32 [32, 12], P(None, 'mp'), may hold values from -4 to 4
- gain_ff: float32 [1536], replicated, may hold values from 0.5 to 1.5
- w_gate: bfloat16 [1536, 3968], P(None, 'mp'), may hold values from -0.15625 to 0.15625
- w_up: bfloat16 [1536, 3968], P(None, 'mp'), may hold values from -0.15625 to 0.15625
- w_down: bfloat16 [3968, 1536], P('mp'), may hold values from -0.09375 to 0.09375
- cotangent: bfloat16 [8192, 1536], P(('dp', 'mp')), may hold values from -6 to 6
- first_length: int32 [8], P('dp'), may hold values from 512 to 1024, as said below
- offset_bucket: int32 [2047], replicated, may hold values from 0 to 31
Outputs:
- output: bfloat16 [8192, 1536], P(('dp', 'mp'))
- grad_input: float32 [8192, 1536], P(('dp', 'mp'))
- grad_gain_attn: float32 [1536], replicated
- grad_query: float32 [1536, 768], P('dp', 'mp')
- grad_key: float32 [1536, 768], P('dp', 'mp')
- grad_value: float32 [1536, 768], P('dp', 'mp')
- grad_out: float32 [768, 1536], P('mp', 'dp')
- grad_table: float32 [32, 12], P(None, 'mp')
- grad_gain_ff: float32 [1536], replicated
- grad_gate: float32 [1536, 3968], P('dp', 'mp')
- grad_up: float32 [1536, 3968], P('dp', 'mp')
- grad_down: float32 [3968, 1536], P('mp', 'dp')
The draws below stay inside these ranges and needn't reach their ends.
Inputs may be any that keep to these rules, and one draw needn't show every extreme that they name: `first_length`: each group of 1024 tokens holds one row of 1024 tokens (this value 1024) or two rows of 1024 // 2 (this value 1024 // 2); both kinds occur in every draw.
All inputs are finite; a program needn't handle non-finite values.
Results may differ from the reference program's by a relative error of at most 0.013.
Values may be sent and summed in bfloat16 or wider, within the bound.
A program may use at most 192 MiB of HBM per device.

```python
import jax
import jax.numpy as jnp
from jax import lax

D = 1536
H = 12
DH = 64
FF = 3968
NB = 32
TOK_DEV = 1024
TOKENS = 8192
N_DP = 8


def draw_first_length(key, part):
    key = jax.random.fold_in(key, 7)
    pick_key, place_key = jax.random.split(key)
    long_rows = jax.random.randint(pick_key, (N_DP,), 0, 4) == 0
    chosen_spot = jax.random.randint(place_key, (), 0, N_DP)
    device_slots = jnp.arange(N_DP, dtype=jnp.int32)
    long_rows = jnp.where(device_slots == chosen_spot, True, long_rows)
    long_rows = jnp.where(device_slots == (chosen_spot + 1) % N_DP, False, long_rows)
    return jnp.where(long_rows, TOK_DEV, TOK_DEV // 2).astype(jnp.int32)


def place_ends(array, own_key, smallest, top_value):
    longest = array.shape.index(max(array.shape))
    spots = []
    for shift in (0, 1):
        where = [jax.random.randint(jax.random.fold_in(own_key, axis), (), 0, length) for axis, length in enumerate(array.shape)]
        where[longest] = (where[longest] + shift) % array.shape[longest]
        spots.append(tuple(where))
    return array.at[spots[0]].set(smallest).at[spots[1]].set(top_value)


def with_spikes(values, rng, source, target, shards_of, factor):
    def block_of(axis_at):
        return (jnp.arange(values.shape[axis_at]) // (values.shape[axis_at] // shards_of)).reshape((-1,) + (1,) * (values.ndim - 1 - axis_at))

    near = jax.random.permutation(rng, shards_of)[block_of(target)]
    far = (block_of(target) + shards_of // 2) % shards_of
    return jnp.where((block_of(source) == near) | (block_of(source) == far), factor * values, values)


def block_scale(key, shape, cuts, low, top_value):
    level, own = 1.0, jax.random.fold_in(key, 6)
    for axis_at, shards_of in cuts:
        draws = jnp.exp(jax.random.uniform(jax.random.fold_in(own, axis_at), (shards_of,), jnp.float32, low / len(cuts), top_value / len(cuts)))
        level = level * jnp.repeat(draws, shape[axis_at] // shards_of).reshape([-1 if axis == axis_at else 1 for axis in range(len(shape))])
    return level


def gaussian(rng, dims, deviation, reach, pieces=(), kind=jnp.bfloat16):
    values = deviation * jax.random.normal(rng, dims, jnp.float32)
    if pieces:
        values = values * block_scale(rng, dims, pieces, -0.22, 0.18)
    return jnp.clip(values, -reach, reach).astype(kind)


def heavy_noise(rng, extent, spread, reach, cuts, heavy, kind=jnp.bfloat16):
    entries = spread * jax.random.normal(rng, extent, jnp.float32)
    if cuts:
        entries = entries * block_scale(rng, extent, cuts, -0.22, 0.18)
    return jnp.clip(with_spikes(entries, jax.random.fold_in(rng, 3), *heavy), -reach, reach).astype(kind)


def setup_inputs(seed: int = 0) -> dict:
    splits = jax.random.split(jax.random.key(seed), 15)
    return {
        "tokens": heavy_noise(splits[0], (TOKENS, D), 1.0, 6.0, ((0, 32),), (0, 1, 32, 2.75)),
        "gain_attn": jnp.clip(1.0 + 0.1 * jax.random.normal(splits[1], (D,), jnp.float32), 0.5, 1.5),
        "w_query": gaussian(splits[2], (D, H * DH), (D * DH) ** -0.5, 0.01953125, ((1, 4),)),
        "w_key": gaussian(splits[3], (D, H * DH), D ** -0.5, 0.15625, ((1, 4),)),
        "w_value": gaussian(splits[4], (D, H * DH), D ** -0.5, 0.15625, ((1, 4),)),
        "w_out": gaussian(splits[5], (H * DH, D), 1 ** -0.5, 6.0, ((0, 4),)),
        "bias_table": gaussian(splits[6], (NB, H), 1.0, 4.0, ((1, 4),), jnp.float32),
        "gain_ff": jnp.clip(1.0 + 0.1 * jax.random.normal(splits[7], (D,), jnp.float32), 0.5, 1.5),
        "w_gate": gaussian(splits[8], (D, FF), D ** -0.5, 0.15625, ((1, 4),)),
        "w_up": gaussian(splits[9], (D, FF), D ** -0.5, 0.15625, ((1, 4),)),
        "w_down": gaussian(splits[10], (FF, D), FF ** -0.5, 0.09375, ((0, 4),)),
        "cotangent": heavy_noise(splits[11], (TOKENS, D), 1.0, 6.0, ((0, 32),), (0, 1, 32, 2.75)),
        "first_length": draw_first_length(jax.random.fold_in(splits[14], 71), 0),
        "offset_bucket": place_ends(jax.random.randint(splits[13], (2 * TOK_DEV - 1,), 0, NB), jax.random.fold_in(splits[13], 1), 0, NB - 1).astype(jnp.int32),
    }


@jax.custom_vjp
def low(v):
    return lax.optimization_barrier(v.astype(jnp.bfloat16)).astype(jnp.float32)

@jax.custom_vjp
def low_back(v):
    return v

def low_keep(v):
    return (low(v), None)

def low_pass(kept, grad):
    return (grad,)

def back_keep(v):
    return (v, None)

def back_low(kept, grad):
    return (low(grad),)
low.defvjp(low_keep, low_pass)
low_back.defvjp(back_keep, back_low)
epsilon = 1e-06
masked_score = -1000000000.0
highest = lax.Precision.HIGHEST

def normalize(values, gain):
    return values * lax.rsqrt(lax.optimization_barrier(jnp.mean(values * values, axis=-1, keepdims=True)) + epsilon) * gain

def matmul(left, right):
    return jnp.dot(left, right, precision=highest)

def attend(query_rows, key_rows, value_rows, first, bias_rows):
    length = query_rows.shape[0]
    places = jnp.arange(length, dtype=jnp.int32)
    offsets = places[None, :] - places[:, None] + (length - 1)
    bias_block = jnp.take(bias_rows, offsets, axis=1)
    row_side = (places >= first).astype(jnp.int32)
    visible = row_side[:, None] == row_side[None, :]
    scores = jnp.einsum('qhd,khd->hqk', query_rows, key_rows, precision=highest) + bias_block
    scores = low_back(jnp.where(visible[None], scores, masked_score))
    weights = low(jax.nn.softmax(scores, axis=-1))
    return jnp.einsum('hqk,khd->qhd', weights, value_rows, precision=highest)
attend_saved = jax.checkpoint(attend)

def layer(inputs, gain_attn, w_query, w_key, w_value, w_out, bias_table, gain_ff, w_gate, w_up, w_down, first_length, offset_bucket):
    total_rows = inputs.shape[0]
    normed = low(normalize(inputs, gain_attn))

    def project(weight):
        return low(low_back(matmul(normed, weight))).reshape(N_DP, TOK_DEV, H, DH)
    query_all, key_all, value_all = (project(w_query), project(w_key), project(w_value))
    bias_rows = jnp.take(bias_table, offset_bucket, axis=0).T

    def group_attend(items):
        query_rows, key_rows, value_rows, first = items
        return attend_saved(query_rows, key_rows, value_rows, first, bias_rows)
    mixed = lax.map(group_attend, (query_all, key_all, value_all, first_length))
    mixed = low(low_back(mixed.reshape(total_rows, H * DH)))
    attn_branch = low_back(matmul(mixed, w_out))
    residual = inputs + attn_branch
    normed_ff = low(normalize(residual, gain_ff))
    gate_val = low_back(matmul(normed_ff, w_gate))
    up_val = low_back(matmul(normed_ff, w_up))
    hidden = low(jax.nn.gelu(gate_val, approximate=True) * up_val)
    return residual + matmul(hidden, w_down)

def reference(tokens, gain_attn, w_query, w_key, w_value, w_out, bias_table, gain_ff, w_gate, w_up, w_down, cotangent, first_length, offset_bucket):
    floats = [tokens, gain_attn, w_query, w_key, w_value, w_out, bias_table, gain_ff, w_gate, w_up, w_down]
    floats = [item.astype(jnp.float32) for item in floats]

    def forward(*params):
        return layer(*params, first_length, offset_bucket)
    result, pullback = jax.vjp(forward, *floats)
    grads = pullback(cotangent.astype(jnp.float32))
    return (result.astype(jnp.bfloat16), grads[0], grads[1], grads[2], grads[3], grads[4], grads[5], grads[6], grads[7], grads[8], grads[9], grads[10])
```

```python
import functools

import jax
import jax.numpy as jnp
from jax import lax
from jax.experimental import pallas as pl
from jax.experimental.pallas import tpu as pltpu
from jax.sharding import PartitionSpec as P

MESH = pl.DeviceIdType.MESH
DH = 64
epsilon = 1e-06
masked_score = -1000000000.0
highest = lax.Precision.HIGHEST
bf16 = jnp.bfloat16
f32 = jnp.float32
VMEM_BYTES = 60 * 2**20


def mm(left, right):
    return jnp.dot(left, right, preferred_element_type=f32)


def contract_rows(left, right):
    return lax.dot_general(left, right, (((0,), (0,)), ((), ())), preferred_element_type=f32)


def contract_cols(left, right):
    return lax.dot_general(left, right, (((1,), (1,)), ((), ())), preferred_element_type=f32)


def rms(values):
    return values * lax.rsqrt(jnp.mean(values * values, axis=-1, keepdims=True) + epsilon)


class Links:
    def __init__(self, send, recv):
        self.send, self.recv, self.used = send, recv, 0

    def copy(self, src, dst, to):
        at = self.used
        self.used += 1
        return pltpu.make_async_remote_copy(
            src_ref=src,
            dst_ref=dst,
            send_sem=self.send.at[at],
            recv_sem=self.recv.at[at],
            device_id=to,
            device_id_type=MESH,
        )


class Group:
    def __init__(self):
        self.dp, self.me = lax.axis_index("dp"), lax.axis_index("mp")
        self.core = self.me + 1 - 2 * lax.rem(self.me, 2)
        self.far = lax.rem(self.me + 2, 4)
        self.diag = 3 - self.me

    def at(self, mp):
        return (self.dp, mp)


def greet(peers):
    barrier = pltpu.get_barrier_semaphore()
    for peer in peers:
        pl.semaphore_signal(barrier, inc=1, device_id=peer, device_id_type=MESH)
    pl.semaphore_wait(barrier, len(peers))


def block_rows(dev, rows, start=0, size=None):
    return pl.ds(pl.multiple_of(dev * rows + start, 16), rows if size is None else size)


class Gather:
    def __init__(self, links, group, full, rows, chunks, source=None):
        size = rows // chunks
        own = block_rows(group.me, rows)
        self.near = links.copy(full.at[own] if source is None else source, full.at[own], group.at(group.core))
        self.far, self.passed = [], []
        for i in range(chunks):
            mine = block_rows(group.me, rows, i * size, size)
            theirs = block_rows(group.far, rows, i * size, size)
            src = full.at[mine] if source is None else source.at[pl.ds(i * size, size)]
            self.far.append(links.copy(src, full.at[mine], group.at(group.far)))
            self.passed.append(links.copy(full.at[theirs], full.at[theirs], group.at(group.core)))

    def start(self):
        self.near.start()
        for copy in self.far:
            copy.start()

    def forward(self, i):
        self.far[i].wait_recv()
        self.passed[i].start()

    def wait_send(self):
        self.near.wait_send()
        for copy in self.far + self.passed:
            copy.wait_send()


def build_strips(strip, bucket, table):
    buckets, heads = table.shape
    index = bucket[...]
    width = index.shape[1]
    for h in range(heads):
        row = jnp.zeros(index.shape, f32)
        for b in range(buckets):
            row = jnp.where(index == b, table[b, h], row)
        strip[h] = pltpu.roll(
            jnp.broadcast_to(row, (128, width)), width - 127, 1, stride=1, stride_axis=0
        )


def add_bias(scores, strip, h, dev, length):
    parts = []
    count = length // 128
    for i in range(scores.shape[0] // 128):
        first = (count - 1 - i) * 128 - dev * scores.shape[0]
        parts.append(
            scores[i * 128 : (i + 1) * 128]
            + strip[h, :, pl.ds(pl.multiple_of(first, 128), length)]
        )
    return jnp.concatenate(parts, axis=0)


def visible_pairs(dev, rows, length, first):
    query = lax.broadcasted_iota(jnp.int32, (rows, length), 0) + dev * rows >= first
    key = lax.broadcasted_iota(jnp.int32, (rows, length), 1) >= first
    return query == key


def head_lanes(shape, h):
    lane = lax.broadcasted_iota(jnp.int32, shape, len(shape) - 1)
    return (lane >= h * DH) & (lane < (h + 1) * DH)


def attend_kernel(
    quarters,
    tokens,
    gain_attn,
    gain_ff,
    w_query,
    w_key,
    w_value,
    bucket,
    table,
    first,
    w_out,
    cot,
    qkv,
    mixed,
    lse,
    h1,
    normed_ff,
    normed_out,
    cot_full,
    normed,
    out_full,
    mixed_all,
    strip,
    key_heads,
    value_heads,
    mixed_sum,
    send,
    recv,
    local,
):
    group = Group()
    me, core, far, diag = group.me, group.core, group.far, group.diag
    rows, width = tokens.shape
    length = 4 * rows
    heads = table.shape[1]
    links = Links(send, recv)
    zs = []
    if quarters > 1:
        z = group.dp // 2
        zs = [lax.rem(z + t, 4) for t in (1, 2, 3)]
        z_peers = [(2 * other + lax.rem(group.dp, 2), me) for other in zs]
    peers = [group.at(core), group.at(far), group.at(diag)]
    if quarters > 1:
        peers += z_peers
    out_own = pltpu.make_async_copy(w_out, out_full.at[me], local.at[0])
    out_own.start()
    cot_own = pltpu.make_async_copy(cot, cot_full.at[block_rows(me, rows)], local.at[1])
    cot_own.start()
    greet(peers)

    x = tokens[...].astype(f32)
    normed[block_rows(me, rows), :] = (rms(x) * gain_attn[...]).astype(bf16)
    gather = Gather(links, group, normed, rows, 2)
    gather.start()
    out_own.wait()
    depth = w_out.shape[0]
    part = depth // quarters
    mine = pl.ds(pl.multiple_of((z if quarters > 1 else 0) * part, 16), part)
    out_near = links.copy(out_full.at[me], out_full.at[me], group.at(core))
    out_far = links.copy(out_full.at[me, mine], out_full.at[me, mine], group.at(far))
    out_near.start()
    out_z = []
    if quarters > 1:
        for peer in z_peers:
            out_z.append(links.copy(out_full.at[far, mine], out_full.at[far, mine], peer))
    out_pass = links.copy(out_full.at[far], out_full.at[far], group.at(core))
    cot_gather = Gather(links, group, cot_full, rows, 4, source=cot)
    cot_gather.near.start()
    mixed_near = links.copy(
        mixed.at[block_rows(core, rows)], mixed_all.at[me], group.at(core)
    )
    mixed_far = links.copy(mixed.at[block_rows(far, rows)], mixed_all.at[me], group.at(far))
    mixed_diag = links.copy(mixed.at[block_rows(diag, rows)], mixed_all.at[me], group.at(diag))

    build_strips(strip, bucket, table)

    def project(dev):
        block = normed[block_rows(dev, rows), :]
        at = block_rows(dev, rows)
        qkv[0, at, :] = mm(block, w_query[...]).astype(bf16)
        key = mm(block, w_key[...]).astype(bf16)
        value = mm(block, w_value[...]).astype(bf16)
        qkv[1, at, :] = key
        qkv[2, at, :] = value
        for h in range(heads):
            lanes = head_lanes(key.shape, h)
            key_heads[h, at, :] = jnp.where(lanes, key, jnp.zeros_like(key))
            value_heads[h, at, :] = jnp.where(lanes, value, jnp.zeros_like(value))

    project(me)
    gather.near.wait_recv()
    project(core)
    gather.forward(0)
    gather.forward(1)
    out_far.start()
    project(far)
    for copy in gather.passed:
        copy.wait_recv()
    normed_save = pltpu.make_async_copy(normed, normed_out, local.at[2])
    normed_save.start()
    project(diag)

    def attend(dev):
        at = block_rows(dev, rows)
        seen = visible_pairs(dev, rows, length, first[0])
        mixed_sum[...] = jnp.zeros_like(mixed_sum)
        lse[at, :] = jnp.zeros((rows, 128), f32)

        def one_head(h, carry):
            scores = contract_cols(qkv[0, at, :], key_heads[h])
            scores = jnp.where(seen, add_bias(scores, strip, h, dev, length), masked_score)
            top = jnp.max(scores, axis=-1, keepdims=True)
            expo = jnp.exp(scores - top)
            total = jnp.sum(expo, axis=-1, keepdims=True)
            weights = (expo * (1.0 / total)).astype(bf16)
            mixed_sum[...] += mm(weights, value_heads[h])
            lane = lax.broadcasted_iota(jnp.int32, (rows, 128), 1)
            lse[at, :] = jnp.where(lane == h, top + jnp.log(total), lse[at, :])
            return carry

        lax.fori_loop(0, heads, one_head, 0)
        mixed[at, :] = mixed_sum[...].astype(bf16)

    attend(far)
    mixed_far.start()
    out_far.wait_recv()
    for copy in out_z:
        copy.start()
    for copy in cot_gather.far:
        copy.start()
    attend(diag)
    mixed_diag.start()
    attend(core)
    mixed_near.start()
    for copy in out_z:
        copy.wait_recv()
    out_pass.start()
    cot_gather.forward(0)
    attend(me)
    mixed_all[me] = mixed[block_rows(me, rows), :]
    cot_gather.forward(1)
    out_near.wait_recv()
    attn = mm(mixed_all[me], out_full[me])
    mixed_near.wait_recv()
    attn = attn + mm(mixed_all[core], out_full[core])
    mixed_far.wait_recv()
    attn = attn + mm(mixed_all[far], out_full[far])
    mixed_diag.wait_recv()
    out_pass.wait_recv()
    attn = attn + mm(mixed_all[diag], out_full[diag])
    residual = x + attn
    h1[...] = residual
    normed_ff[...] = (rms(residual) * gain_ff[...]).astype(bf16)
    cot_gather.forward(2)
    cot_gather.forward(3)

    gather.wait_send()
    for copy in [out_near, out_far, out_pass, mixed_near, mixed_far, mixed_diag] + out_z:
        copy.wait_send()
    cot_gather.near.wait_recv()
    for copy in cot_gather.passed:
        copy.wait_recv()
    cot_gather.wait_send()
    normed_save.wait()
    cot_own.wait()


def in_vmem():
    return pl.BlockSpec(memory_space=pltpu.VMEM)


def anywhere():
    return pl.BlockSpec(memory_space=pl.ANY)


def in_smem():
    return pl.BlockSpec(memory_space=pltpu.SMEM)


def attention_forward(n_dp, tokens, gain_attn, gain_ff, w_query, w_key, w_value, bucket, table, first, w_out, cot):
    rows, width = tokens.shape
    length = 4 * rows
    cols = w_query.shape[1]
    heads = table.shape[1]
    shape = jax.ShapeDtypeStruct
    return pl.pallas_call(
        functools.partial(attend_kernel, 4 if n_dp == 8 else 1),
        out_shape=(
            shape((3, length, cols), bf16),
            shape((length, cols), bf16),
            shape((length, 128), f32),
            shape((rows, width), f32),
            shape((rows, width), bf16),
            shape((length, width), bf16),
            shape((length, width), bf16),
        ),
        in_specs=[in_vmem()] * 7 + [in_smem()] * 2 + [anywhere()] * 2,
        out_specs=[in_vmem()] * 5 + [anywhere()] * 2,
        scratch_shapes=[
            pltpu.VMEM((length, width), bf16),
            pltpu.VMEM((4, cols, width), bf16),
            pltpu.VMEM((4, rows, cols), bf16),
            pltpu.VMEM((heads, 128, 2 * length), f32),
            pltpu.VMEM((heads, length, cols), bf16),
            pltpu.VMEM((heads, length, cols), bf16),
            pltpu.VMEM((rows, cols), f32),
            pltpu.SemaphoreType.DMA((32,)),
            pltpu.SemaphoreType.DMA((32,)),
            pltpu.SemaphoreType.DMA((4,)),
        ],
        compiler_params=pltpu.CompilerParams(
            collective_id=0, has_side_effects=True, vmem_limit_bytes=VMEM_BYTES
        ),
    )(tokens, gain_attn, gain_ff, w_query, w_key, w_value, bucket, table, first, w_out, cot)


def normalize(values, gain):
    return values * lax.rsqrt(jnp.mean(values * values, axis=-1, keepdims=True) + epsilon) * gain


def gated(gate_val, up_val):
    return jax.nn.gelu(gate_val, approximate=True) * up_val


def skew_bias(bias_rows, start, block, length):
    heads = bias_rows.shape[0]
    span = length + block - 1
    window = lax.dynamic_slice_in_dim(bias_rows, length - block - start, span, 1)
    tiled = jnp.broadcast_to(window[:, None, :], (heads, block, span)).reshape(heads, block * span)
    tiled = jnp.pad(tiled, ((0, 0), (0, block))).reshape(heads, block, length + block)
    return tiled[:, ::-1, :length]


def unskew_sum(grads, block, length):
    heads = grads.shape[0]
    span = length + block - 1
    flipped = grads[:, ::-1, :]
    padded = jnp.pad(flipped, ((0, 0), (0, 0), (0, block))).reshape(heads, block * (length + block))
    return padded[:, : block * span].reshape(heads, block, span).sum(axis=1)


def shards(
    tokens,
    gain_attn,
    w_query,
    w_key,
    w_value,
    w_out,
    bias_table,
    gain_ff,
    w_gate,
    w_up,
    w_down,
    cotangent,
    first_length,
    offset_bucket,
):
    inputs = tokens.astype(jnp.float32)
    n_dp = lax.axis_size("dp")
    bucket = jnp.pad(offset_bucket, (0, 1), constant_values=-1)[None, :]
    qkv, mixed, lse, residual, normed_ff_part, normed, cot_full = attention_forward(
        n_dp, tokens, gain_attn[None], gain_ff[None], w_query, w_key, w_value, bucket, bias_table,
        first_length, w_out, cotangent)
    normed_ff = lax.all_gather(normed_ff_part, "mp", axis=0, tiled=True)
    length = normed.shape[0]
    heads = w_query.shape[1] // DH
    query_all, key_all, value_all = qkv[0], qkv[1], qkv[2]
    key_heads = key_all.reshape(length, heads, DH)
    value_heads = value_all.reshape(length, heads, DH)
    places = jnp.arange(length, dtype=jnp.int32)
    row_side = (places >= first_length[0]).astype(jnp.int32)
    onehot = (
        offset_bucket[:, None] == jnp.arange(bias_table.shape[0], dtype=jnp.int32)[None, :]
    ).astype(jnp.float32)
    bias_rows = lax.dot_general(
        bias_table,
        onehot,
        (((0,), (1,)), ((), ())),
        precision=highest,
        preferred_element_type=jnp.float32,
    )
    block = min(512, length)
    count = length // block
    starts = jnp.arange(count, dtype=jnp.int32) * block
    query_blocks = query_all.reshape(count, block, heads, DH)

    def block_scores(query_block, start):
        bias_block = skew_bias(bias_rows, start, block, length)
        block_side = lax.dynamic_slice_in_dim(row_side, start, block)
        visible = block_side[:, None] == row_side[None, :]
        scores = (
            jnp.einsum("qhd,khd->hqk", query_block, key_heads, preferred_element_type=jnp.float32)
            + bias_block
        )
        return jnp.where(visible[None], scores, masked_score)

    log_totals = lse[:, :heads].reshape(count, block, heads).transpose(0, 2, 1)
    gate_val = jnp.dot(normed_ff, w_gate, preferred_element_type=jnp.float32)
    up_val = jnp.dot(normed_ff, w_up, preferred_element_type=jnp.float32)
    hidden = gated(gate_val, up_val).astype(jnp.bfloat16)
    ff_terms = jnp.dot(hidden, w_down, preferred_element_type=jnp.float32)
    ff_part = lax.psum_scatter(
        ff_terms.astype(jnp.bfloat16), "mp", scatter_dimension=0, tiled=True
    ).astype(jnp.float32)
    output = (residual + ff_part).astype(jnp.bfloat16)
    grad_down_t = contract_rows(cot_full, hidden)
    grad_hidden = contract_cols(cot_full, w_down)
    _, gated_pull = jax.vjp(gated, gate_val, up_val)
    grad_gate_act, grad_up_act = gated_pull(grad_hidden)
    grad_gate_act = grad_gate_act.astype(jnp.bfloat16)
    grad_up_act = grad_up_act.astype(jnp.bfloat16)
    grad_gate = contract_rows(normed_ff, grad_gate_act)
    grad_up = contract_rows(normed_ff, grad_up_act)
    normed_ff_terms = contract_cols(grad_gate_act, w_gate) + contract_cols(grad_up_act, w_up)
    grad_normed_ff = lax.psum_scatter(normed_ff_terms, "mp", scatter_dimension=0, tiled=True)
    _, norm_ff_pull = jax.vjp(normalize, residual, gain_ff)
    residual_grad, gain_ff_grad = norm_ff_pull(grad_normed_ff)
    residual_grad = cotangent.astype(jnp.float32) + residual_grad
    attn_grad = lax.all_gather(residual_grad.astype(jnp.bfloat16), "mp", axis=0, tiled=True)
    grad_out_t = contract_rows(attn_grad, mixed)
    grad_mixed = (
        contract_cols(attn_grad, w_out).astype(jnp.bfloat16).reshape(count, block, heads, DH)
    )
    span = length + block - 1

    def backward_block(carry, items):
        key_acc, value_acc, bias_acc = carry
        query_block, grad_block, lse_block, start = items
        scores = block_scores(query_block, start)
        probs = jnp.exp(scores - lse_block[..., None])
        probs_low = probs.astype(jnp.bfloat16)
        value_acc = value_acc + jnp.einsum(
            "hqk,qhd->khd", probs_low, grad_block, preferred_element_type=jnp.float32
        )
        inner = jnp.einsum(
            "qhd,khd->hqk", grad_block, value_heads, preferred_element_type=jnp.float32
        )
        center = jnp.sum(probs * inner, axis=-1, keepdims=True)
        score_grad = (probs * (inner - center)).astype(jnp.bfloat16)
        query_grad = jnp.einsum(
            "hqk,khd->qhd", score_grad, key_heads, preferred_element_type=jnp.float32
        ).astype(jnp.bfloat16)
        key_acc = key_acc + jnp.einsum(
            "hqk,qhd->khd", score_grad, query_block, preferred_element_type=jnp.float32
        )
        diagonal_sums = unskew_sum(score_grad.astype(jnp.float32), block, length)
        begin = length - block - start
        current = lax.dynamic_slice_in_dim(bias_acc, begin, span, 1)
        bias_acc = lax.dynamic_update_slice_in_dim(bias_acc, current + diagonal_sums, begin, 1)
        return ((key_acc, value_acc, bias_acc), query_grad)

    empty_heads = jnp.zeros((length, heads, DH), jnp.float32)
    empty_bias = jnp.zeros((heads, 2 * length - 1), jnp.float32)
    carried, query_grads = lax.scan(
        backward_block,
        (empty_heads, empty_heads, empty_bias),
        (query_blocks, grad_mixed, log_totals, starts),
    )
    key_grads, value_grads, offset_grads = carried
    grad_q = query_grads.reshape(length, heads * DH)
    grad_k = key_grads.astype(jnp.bfloat16).reshape(length, heads * DH)
    grad_v = value_grads.astype(jnp.bfloat16).reshape(length, heads * DH)
    grad_query = contract_rows(normed, grad_q)
    grad_key = contract_rows(normed, grad_k)
    grad_value = contract_rows(normed, grad_v)
    normed_terms = (
        contract_cols(grad_q, w_query)
        + contract_cols(grad_k, w_key)
        + contract_cols(grad_v, w_value)
    )
    grad_normed = lax.psum_scatter(normed_terms, "mp", scatter_dimension=0, tiled=True)
    _, norm_pull = jax.vjp(normalize, inputs, gain_attn)
    input_grad, gain_attn_grad = norm_pull(grad_normed)
    grad_input = residual_grad + input_grad
    table_grad = lax.dot_general(
        onehot,
        offset_grads,
        (((0,), (1,)), ((), ())),
        precision=highest,
        preferred_element_type=jnp.float32,
    )
    grad_table = lax.psum(table_grad, "dp")
    grad_gain_attn, grad_gain_ff = lax.psum((gain_attn_grad, gain_ff_grad), ("dp", "mp"))
    sum_query, sum_key, sum_value, sum_out, sum_gate, sum_up, sum_down = (
        lax.psum_scatter(grad_query, "dp", scatter_dimension=0, tiled=True),
        lax.psum_scatter(grad_key, "dp", scatter_dimension=0, tiled=True),
        lax.psum_scatter(grad_value, "dp", scatter_dimension=0, tiled=True),
        lax.psum_scatter(grad_out_t, "dp", scatter_dimension=0, tiled=True),
        lax.psum_scatter(grad_gate, "dp", scatter_dimension=0, tiled=True),
        lax.psum_scatter(grad_up, "dp", scatter_dimension=0, tiled=True),
        lax.psum_scatter(grad_down_t, "dp", scatter_dimension=0, tiled=True),
    )
    return (
        output,
        grad_input,
        grad_gain_attn,
        sum_query,
        sum_key,
        sum_value,
        sum_out.T,
        grad_table,
        grad_gain_ff,
        sum_gate,
        sum_up,
        sum_down.T,
    )


def solution(mesh):
    placed = (
        P(("dp", "mp"), None),
        P(),
        P(None, "mp"),
        P(None, "mp"),
        P(None, "mp"),
        P("mp", None),
        P(None, "mp"),
        P(),
        P(None, "mp"),
        P(None, "mp"),
        P("mp", None),
        P(("dp", "mp"), None),
        P("dp"),
        P(),
    )
    return jax.shard_map(
        shards,
        mesh=mesh,
        in_specs=placed,
        out_specs=(
            P(("dp", "mp"), None),
            P(("dp", "mp"), None),
            P(),
            P("dp", "mp"),
            P("dp", "mp"),
            P("dp", "mp"),
            P("mp", "dp"),
            P(None, "mp"),
            P(),
            P("dp", "mp"),
            P("dp", "mp"),
            P("mp", "dp"),
        ),
        check_vma=False,
    )
```

```python
import functools

import jax
import jax.numpy as jnp
from jax import lax
from jax.experimental import pallas as pl
from jax.experimental.pallas import tpu as pltpu
from jax.sharding import PartitionSpec as P

MESH = pl.DeviceIdType.MESH
DH = 64
epsilon = 1e-06
masked_score = -1000000000.0
highest = lax.Precision.HIGHEST
bf16 = jnp.bfloat16
f32 = jnp.float32
VMEM_BYTES = 60 * 2**20


def mm(left, right):
    return jnp.dot(left, right, preferred_element_type=f32)


def contract_rows(left, right):
    return lax.dot_general(left, right, (((0,), (0,)), ((), ())), preferred_element_type=f32)


def contract_cols(left, right):
    return lax.dot_general(left, right, (((1,), (1,)), ((), ())), preferred_element_type=f32)


def rms(values):
    return values * lax.rsqrt(jnp.mean(values * values, axis=-1, keepdims=True) + epsilon)


class Links:
    def __init__(self, send, recv):
        self.send, self.recv, self.used = send, recv, 0

    def copy(self, src, dst, to):
        at = self.used
        self.used += 1
        return pltpu.make_async_remote_copy(
            src_ref=src,
            dst_ref=dst,
            send_sem=self.send.at[at],
            recv_sem=self.recv.at[at],
            device_id=to,
            device_id_type=MESH,
        )


class Group:
    def __init__(self):
        self.dp, self.me = lax.axis_index("dp"), lax.axis_index("mp")
        self.core = self.me + 1 - 2 * lax.rem(self.me, 2)
        self.far = lax.rem(self.me + 2, 4)
        self.diag = 3 - self.me

    def at(self, mp):
        return (self.dp, mp)


def greet(peers):
    barrier = pltpu.get_barrier_semaphore()
    for peer in peers:
        pl.semaphore_signal(barrier, inc=1, device_id=peer, device_id_type=MESH)
    pl.semaphore_wait(barrier, len(peers))


def block_rows(dev, rows, start=0, size=None):
    return pl.ds(pl.multiple_of(dev * rows + start, 16), rows if size is None else size)


class Gather:
    def __init__(self, links, group, full, rows, chunks, source=None):
        size = rows // chunks
        own = block_rows(group.me, rows)
        self.near = links.copy(full.at[own] if source is None else source, full.at[own], group.at(group.core))
        self.far, self.passed = [], []
        for i in range(chunks):
            mine = block_rows(group.me, rows, i * size, size)
            theirs = block_rows(group.far, rows, i * size, size)
            src = full.at[mine] if source is None else source.at[pl.ds(i * size, size)]
            self.far.append(links.copy(src, full.at[mine], group.at(group.far)))
            self.passed.append(links.copy(full.at[theirs], full.at[theirs], group.at(group.core)))

    def start(self):
        self.near.start()
        for copy in self.far:
            copy.start()

    def forward(self, i):
        self.far[i].wait_recv()
        self.passed[i].start()

    def wait_send(self):
        self.near.wait_send()
        for copy in self.far + self.passed:
            copy.wait_send()


def build_strips(strip, bucket, table):
    buckets, heads = table.shape
    index = bucket[...]
    width = index.shape[1]
    for h in range(heads):
        row = jnp.zeros(index.shape, f32)
        for b in range(buckets):
            row = jnp.where(index == b, table[b, h], row)
        strip[h] = pltpu.roll(
            jnp.broadcast_to(row, (128, width)), width - 127, 1, stride=1, stride_axis=0
        )


def add_bias(scores, strip, h, dev, length):
    parts = []
    count = length // 128
    for i in range(scores.shape[0] // 128):
        first = (count - 1 - i) * 128 - dev * scores.shape[0]
        parts.append(
            scores[i * 128 : (i + 1) * 128]
            + strip[h, :, pl.ds(pl.multiple_of(first, 128), length)]
        )
    return jnp.concatenate(parts, axis=0)


def visible_pairs(dev, rows, length, first):
    query = lax.broadcasted_iota(jnp.int32, (rows, length), 0) + dev * rows >= first
    key = lax.broadcasted_iota(jnp.int32, (rows, length), 1) >= first
    return query == key


def head_lanes(shape, h):
    lane = lax.broadcasted_iota(jnp.int32, shape, len(shape) - 1)
    return (lane >= h * DH) & (lane < (h + 1) * DH)


def attend_kernel(
    quarters,
    tokens,
    gain_attn,
    gain_ff,
    w_query,
    w_key,
    w_value,
    bucket,
    table,
    first,
    w_out,
    cot,
    qkv,
    mixed,
    lse,
    h1,
    normed_ff,
    normed_out,
    cot_full,
    normed,
    out_full,
    mixed_all,
    strip,
    key_heads,
    value_heads,
    mixed_sum,
    send,
    recv,
    local,
):
    group = Group()
    me, core, far, diag = group.me, group.core, group.far, group.diag
    rows, width = tokens.shape
    length = 4 * rows
    heads = table.shape[1]
    links = Links(send, recv)
    zs = []
    if quarters > 1:
        z = group.dp // 2
        zs = [lax.rem(z + t, 4) for t in (1, 2, 3)]
        z_peers = [(2 * other + lax.rem(group.dp, 2), me) for other in zs]
    peers = [group.at(core), group.at(far), group.at(diag)]
    if quarters > 1:
        peers += z_peers
    out_own = pltpu.make_async_copy(w_out, out_full.at[me], local.at[0])
    out_own.start()
    cot_own = pltpu.make_async_copy(cot, cot_full.at[block_rows(me, rows)], local.at[1])
    cot_own.start()
    greet(peers)

    x = tokens[...].astype(f32)
    normed[block_rows(me, rows), :] = (rms(x) * gain_attn[...]).astype(bf16)
    gather = Gather(links, group, normed, rows, 2)
    gather.start()
    out_own.wait()
    depth = w_out.shape[0]
    part = depth // quarters
    mine = pl.ds(pl.multiple_of((z if quarters > 1 else 0) * part, 16), part)
    out_near = links.copy(out_full.at[me], out_full.at[me], group.at(core))
    out_far = links.copy(out_full.at[me, mine], out_full.at[me, mine], group.at(far))
    out_near.start()
    out_z = []
    if quarters > 1:
        for peer in z_peers:
            out_z.append(links.copy(out_full.at[far, mine], out_full.at[far, mine], peer))
    out_pass = links.copy(out_full.at[far], out_full.at[far], group.at(core))
    cot_gather = Gather(links, group, cot_full, rows, 4, source=cot)
    cot_gather.near.start()
    mixed_near = links.copy(
        mixed.at[block_rows(core, rows)], mixed_all.at[me], group.at(core)
    )
    mixed_far = links.copy(mixed.at[block_rows(far, rows)], mixed_all.at[me], group.at(far))
    mixed_diag = links.copy(mixed.at[block_rows(diag, rows)], mixed_all.at[me], group.at(diag))

    build_strips(strip, bucket, table)

    def project(dev):
        block = normed[block_rows(dev, rows), :]
        at = block_rows(dev, rows)
        qkv[0, at, :] = contract_cols(block, w_query[...]).astype(bf16)
        key = contract_cols(block, w_key[...]).astype(bf16)
        value = contract_cols(block, w_value[...]).astype(bf16)
        qkv[1, at, :] = key
        qkv[2, at, :] = value
        for h in range(heads):
            lanes = head_lanes(key.shape, h)
            key_heads[h, at, :] = jnp.where(lanes, key, jnp.zeros_like(key))
            value_heads[h, at, :] = jnp.where(lanes, value, jnp.zeros_like(value))

    project(me)
    gather.near.wait_recv()
    project(core)
    gather.forward(0)
    gather.forward(1)
    out_far.start()
    project(far)
    for copy in gather.passed:
        copy.wait_recv()
    normed_save = pltpu.make_async_copy(normed, normed_out, local.at[2])
    normed_save.start()
    project(diag)

    def attend(dev):
        at = block_rows(dev, rows)
        seen = visible_pairs(dev, rows, length, first[0])
        mixed_sum[...] = jnp.zeros_like(mixed_sum)
        lse[at, :] = jnp.zeros((rows, 128), f32)

        def one_head(h, carry):
            scores = contract_cols(qkv[0, at, :], key_heads[h])
            scores = jnp.where(seen, add_bias(scores, strip, h, dev, length), masked_score)
            top = jnp.max(scores, axis=-1, keepdims=True)
            expo = jnp.exp(scores - top)
            total = jnp.sum(expo, axis=-1, keepdims=True)
            weights = (expo * (1.0 / total)).astype(bf16)
            mixed_sum[...] += mm(weights, value_heads[h])
            lane = lax.broadcasted_iota(jnp.int32, (rows, 128), 1)
            lse[at, :] = jnp.where(lane == h, top + jnp.log(total), lse[at, :])
            return carry

        lax.fori_loop(0, heads, one_head, 0)
        mixed[at, :] = mixed_sum[...].astype(bf16)

    attend(far)
    mixed_far.start()
    out_far.wait_recv()
    for copy in out_z:
        copy.start()
    for copy in cot_gather.far:
        copy.start()
    attend(diag)
    mixed_diag.start()
    attend(core)
    mixed_near.start()
    for copy in out_z:
        copy.wait_recv()
    out_pass.start()
    cot_gather.forward(0)
    attend(me)
    mixed_all[me] = mixed[block_rows(me, rows), :]
    cot_gather.forward(1)
    out_near.wait_recv()
    attn = mm(mixed_all[me], out_full[me])
    mixed_near.wait_recv()
    attn = attn + mm(mixed_all[core], out_full[core])
    mixed_far.wait_recv()
    attn = attn + mm(mixed_all[far], out_full[far])
    mixed_diag.wait_recv()
    out_pass.wait_recv()
    attn = attn + mm(mixed_all[diag], out_full[diag])
    residual = x + attn
    h1[...] = residual
    normed_ff[...] = (rms(residual) * gain_ff[...]).astype(bf16)
    cot_gather.forward(2)
    cot_gather.forward(3)

    gather.wait_send()
    for copy in [out_near, out_far, out_pass, mixed_near, mixed_far, mixed_diag] + out_z:
        copy.wait_send()
    cot_gather.near.wait_recv()
    for copy in cot_gather.passed:
        copy.wait_recv()
    cot_gather.wait_send()
    normed_save.wait()
    cot_own.wait()


def in_vmem():
    return pl.BlockSpec(memory_space=pltpu.VMEM)


def anywhere():
    return pl.BlockSpec(memory_space=pl.ANY)


def in_smem():
    return pl.BlockSpec(memory_space=pltpu.SMEM)


def attention_forward(n_dp, tokens, gain_attn, gain_ff, w_query, w_key, w_value, bucket, table, first, w_out, cot):
    rows, width = tokens.shape
    length = 4 * rows
    cols = w_query.shape[0]
    heads = table.shape[1]
    shape = jax.ShapeDtypeStruct
    return pl.pallas_call(
        functools.partial(attend_kernel, 4 if n_dp == 8 else 1),
        out_shape=(
            shape((3, length, cols), bf16),
            shape((length, cols), bf16),
            shape((length, 128), f32),
            shape((rows, width), f32),
            shape((rows, width), bf16),
            shape((length, width), bf16),
            shape((length, width), bf16),
        ),
        in_specs=[in_vmem()] * 7 + [in_smem()] * 2 + [anywhere()] * 2,
        out_specs=[in_vmem()] * 5 + [anywhere()] * 2,
        scratch_shapes=[
            pltpu.VMEM((length, width), bf16),
            pltpu.VMEM((4, cols, width), bf16),
            pltpu.VMEM((4, rows, cols), bf16),
            pltpu.VMEM((heads, 128, 2 * length), f32),
            pltpu.VMEM((heads, length, cols), bf16),
            pltpu.VMEM((heads, length, cols), bf16),
            pltpu.VMEM((rows, cols), f32),
            pltpu.SemaphoreType.DMA((32,)),
            pltpu.SemaphoreType.DMA((32,)),
            pltpu.SemaphoreType.DMA((4,)),
        ],
        compiler_params=pltpu.CompilerParams(
            collective_id=0, has_side_effects=True, vmem_limit_bytes=VMEM_BYTES
        ),
    )(tokens, gain_attn, gain_ff, w_query, w_key, w_value, bucket, table, first, w_out, cot)


def norm_pull(values, gain, grad):
    inverse = lax.rsqrt(jnp.mean(values * values, axis=-1, keepdims=True) + epsilon)
    scaled = grad * gain
    along = jnp.mean(values * scaled, axis=-1, keepdims=True)
    gain_grad = jnp.sum(grad * values * inverse, axis=0, keepdims=True)
    return inverse * scaled - values * (along * inverse * inverse * inverse), gain_grad


class Scatter:
    def __init__(self, links, group, tx, rx, rows, parts):
        self.tx, self.rx, self.size = tx, rx, rows // parts
        core, far = group.at(group.core), group.at(group.far)
        self.near = links.copy(tx.at[2], rx.at[2], core)
        self.diag, self.far = [], []
        for i in range(parts):
            at = pl.ds(i * self.size, self.size)
            self.diag.append(links.copy(tx.at[0, at], rx.at[0, at], core))
            self.far.append(links.copy(tx.at[1, at], rx.at[1, at], far))

    def send_diag(self, i, terms):
        self.tx[0, pl.ds(i * self.size, self.size), :] = terms.astype(bf16)
        self.diag[i].start()

    def send_near(self, terms):
        self.tx[2] = terms.astype(bf16)
        self.near.start()

    def send_far(self, i, terms):
        at = pl.ds(i * self.size, self.size)
        self.diag[i].wait_recv()
        self.tx[1, at, :] = (terms + self.rx[0, at, :].astype(f32)).astype(bf16)
        self.far[i].start()

    def total(self, own):
        self.near.wait_recv()
        for copy in self.far:
            copy.wait_recv()
        return own + self.rx[2].astype(f32) + self.rx[1].astype(f32)

    def wait_send(self):
        for copy in [self.near] + self.diag + self.far:
            copy.wait_send()


GELU_SLOPE = 0.7978845608028654
GELU_CUBE = 0.044715


def feed_kernel(
    exchange,
    normed_own,
    h1,
    gain,
    gate_w,
    up_w,
    down_w,
    cot_full,
    output,
    grad_h1,
    grad_attn,
    gain_grad,
    down_out,
    gate_out,
    up_out,
    normed,
    cot,
    wg,
    wu,
    wd,
    gate,
    up,
    back,
    hidden,
    gate_act,
    up_act,
    far_terms,
    own_terms,
    tx,
    rx,
    tx_ff,
    rx_ff,
    down_grad,
    weight_grad,
    y_recv,
    send,
    recv,
    local,
):
    group = Group()
    me, core, far, diag = group.me, group.core, group.far, group.diag
    rows, width = h1.shape
    half = rows // 2
    part = width // 4
    links = Links(send, recv)
    peers = [group.at(core), group.at(far)]
    if exchange:
        z, y = group.dp // 2, lax.rem(group.dp, 2)
        order = z_order(z)
        y_peer = (2 * z + 1 - y, me)
        peers.append(y_peer)
    else:
        order, y = [0, 1, 2, 3], 0

    def block_at(t):
        found = jnp.int32(order[3])
        for i in range(3):
            found = jnp.where(t == i, order[i], found)
        return found

    loads = [
        pltpu.make_async_copy(src, dst, local.at[i])
        for i, (src, dst) in enumerate(
            [(gate_w, wg), (up_w, wu), (cot_full, cot), (down_w, wd)]
        )
    ]
    for load in loads:
        load.start()
    normed[block_rows(me, rows), :] = normed_own[...]
    greet(peers)
    gather = Gather(links, group, normed, rows, 2)
    gather.start()
    scatter = Scatter(links, group, tx, rx, rows, 2)
    scatter_ff = Scatter(links, group, tx_ff, rx_ff, rows, 1)

    def pair(ref, first, second):
        return jnp.concatenate(
            [
                ref[pl.ds(pl.multiple_of(first, 128), half), :],
                ref[pl.ds(pl.multiple_of(second, 128), half), :],
            ],
            axis=0,
        )

    def unit(first, second):
        block = pair(normed, first, second)
        gate[...] = contract_cols(block, wg[...])
        up[...] = contract_cols(block, wu[...])
        back[...] = contract_cols(pair(cot, first, second), wd[...])

        def act(i, carry):
            at = pl.ds(pl.multiple_of(i * 16, 16), 16)
            start = jnp.where(i < half // 16, first, second - half)
            to = pl.ds(pl.multiple_of(start + i * 16, 16), 16)
            v, u, g = gate[at, :], up[at, :], back[at, :]
            square = v * v
            t = jnp.tanh(GELU_SLOPE * v * (1.0 + GELU_CUBE * square))
            lift = 0.5 * (1.0 + t)
            value = v * lift
            slope = lift + 0.5 * v * (1.0 - t * t) * (
                GELU_SLOPE * (1.0 + 3.0 * GELU_CUBE * square)
            )
            hidden[to, :] = (value * u).astype(bf16)
            gate_act[to, :] = (g * u * slope).astype(bf16)
            up_act[to, :] = (g * value).astype(bf16)
            return carry

        lax.fori_loop(0, rows // 16, act, 0)

    def terms(first, second):
        return mm(pair(gate_act, first, second), wg[...]) + mm(
            pair(up_act, first, second), wu[...]
        )

    def weight_blocks(left, right, store):
        def one(t, carry):
            block = block_at(t)
            store(
                t,
                block,
                contract_rows(
                    left[:, pl.ds(pl.multiple_of(block * part, 128), part)], right[...]
                ).astype(bf16),
            )
            return carry

        lax.fori_loop(0, 4, one, 0)

    loads[0].wait()
    loads[1].wait()
    loads[2].wait()
    loads[3].wait()
    unit(me * rows, me * rows + half)
    gather.near.wait_recv()
    unit(core * rows, core * rows + half)
    gather.forward(0)
    gather.passed[0].wait_recv()
    unit(far * rows, diag * rows)
    both = terms(far * rows, diag * rows)
    scatter.send_diag(0, both[half:])
    far_terms[pl.ds(0, half), :] = both[:half]
    gather.forward(1)
    own_terms[...] = terms(me * rows, me * rows + half)
    scatter.send_far(0, far_terms[pl.ds(0, half), :])
    gather.passed[1].wait_recv()
    unit(far * rows + half, diag * rows + half)

    def y_copy(t, block):
        return pltpu.make_async_remote_copy(
            src_ref=down_grad.at[block, 1 - y],
            dst_ref=y_recv.at[block],
            send_sem=send.at[16 + t],
            recv_sem=recv.at[16 + t],
            device_id=y_peer,
            device_id_type=MESH,
        )

    def store_down(t, block, value):
        down_grad[block, 0] = value[: part // 2]
        down_grad[block, 1] = value[part // 2 :]
        if exchange:
            y_copy(t, block).start()

    weight_blocks(cot, hidden, store_down)
    both = terms(far * rows + half, diag * rows + half)
    scatter.send_diag(1, both[half:])
    far_terms[pl.ds(half, half), :] = both[:half]
    scatter.send_near(terms(core * rows, core * rows + half))
    scatter.send_far(1, far_terms[pl.ds(half, half), :])

    def save(slot, block, to, sem):
        return pltpu.make_async_copy(weight_grad.at[slot], to.at[block], local.at[sem])

    def store_gate(t, block, value):
        weight_grad[block, 0] = value[: part // 2]
        weight_grad[block, 1] = value[part // 2 :]
        save(block, block, gate_out, 4 + t).start()

    def store_up(t, block, value):
        save(block, block, gate_out, 4 + t).wait()
        weight_grad[block, 0] = value[: part // 2]
        weight_grad[block, 1] = value[part // 2 :]
        save(block, block, up_out, 8 + t).start()

    weight_blocks(normed, gate_act, store_gate)

    def ff_terms(dev):
        return mm(hidden[block_rows(dev, rows), :], wd[...])

    scatter_ff.send_diag(0, ff_terms(diag))
    scatter_ff.send_near(ff_terms(core))
    scatter_ff.send_far(0, ff_terms(far))
    weight_blocks(normed, up_act, store_up)

    residual = h1[...]
    pulled, gain_part = norm_pull(residual, gain[...], scatter.total(own_terms[...]))
    gain_grad[...] = gain_part
    grad = cot[block_rows(me, rows), :].astype(f32) + pulled
    grad_h1[...] = grad
    grad_attn[...] = grad.astype(bf16)
    own_terms[...] = ff_terms(me)

    def sum_down(t, carry):
        block = block_at(t)
        y_copy(t, block).wait_recv()
        down_grad[block, y] = (
            down_grad[block, y].astype(f32) + y_recv[block].astype(f32)
        ).astype(bf16)
        pltpu.make_async_copy(
            down_grad.at[block, y], down_out.at[block], local.at[12 + t]
        ).start()
        return carry

    if exchange:
        lax.fori_loop(0, 4, sum_down, 0)
    else:
        save_down = pltpu.make_async_copy(down_grad, down_out, local.at[12])
        save_down.start()

    output[...] = (h1[...] + scatter_ff.total(own_terms[...])).astype(bf16)

    def finish(t, carry):
        block = block_at(t)
        save(block, block, up_out, 8 + t).wait()
        if exchange:
            y_copy(t, block).wait_send()
            pltpu.make_async_copy(
                down_grad.at[block, y], down_out.at[block], local.at[12 + t]
            ).wait()
        return carry

    lax.fori_loop(0, 4, finish, 0)
    if not exchange:
        save_down.wait()
    gather.wait_send()
    scatter.wait_send()
    scatter_ff.wait_send()


def feed_forward(exchange, normed_own, h1, gain, gate_w, up_w, down_w, cot_full):
    rows, width = h1.shape
    length = 4 * rows
    cols = gate_w.shape[0]
    part = width // 8
    shape = jax.ShapeDtypeStruct
    halves = (4, 2, part, cols)
    return pl.pallas_call(
        functools.partial(feed_kernel, exchange),
        out_shape=(
            shape((rows, width), bf16),
            shape((rows, width), f32),
            shape((rows, width), bf16),
            shape((1, width), f32),
            shape((4, part, cols) if exchange else halves, bf16),
            shape(halves, bf16),
            shape(halves, bf16),
        ),
        in_specs=[in_vmem()] * 3 + [anywhere()] * 4,
        out_specs=[in_vmem()] * 4 + [anywhere()] * 3,
        scratch_shapes=[
            pltpu.VMEM((length, width), bf16),
            pltpu.VMEM((length, width), bf16),
            pltpu.VMEM((cols, width), bf16),
            pltpu.VMEM((cols, width), bf16),
            pltpu.VMEM((cols, width), bf16),
            pltpu.VMEM((rows, cols), f32),
            pltpu.VMEM((rows, cols), f32),
            pltpu.VMEM((rows, cols), f32),
            pltpu.VMEM((length, cols), bf16),
            pltpu.VMEM((length, cols), bf16),
            pltpu.VMEM((length, cols), bf16),
            pltpu.VMEM((rows, width), f32),
            pltpu.VMEM((rows, width), f32),
            pltpu.VMEM((3, rows, width), bf16),
            pltpu.VMEM((3, rows, width), bf16),
            pltpu.VMEM((3, rows, width), bf16),
            pltpu.VMEM((3, rows, width), bf16),
            pltpu.VMEM(halves, bf16),
            pltpu.VMEM(halves, bf16),
            pltpu.VMEM((4, part, cols), bf16),
            pltpu.SemaphoreType.DMA((20,)),
            pltpu.SemaphoreType.DMA((20,)),
            pltpu.SemaphoreType.DMA((16,)),
        ],
        compiler_params=pltpu.CompilerParams(
            collective_id=1, has_side_effects=True, vmem_limit_bytes=VMEM_BYTES
        ),
    )(normed_own, h1, gain, gate_w, up_w, down_w, cot_full)


class Halving:
    def __init__(self, links, dp, mp, own, y_recv, z_recv):
        self.own, self.y_recv, self.z_recv = own, y_recv, z_recv
        z, y = dp // 2, lax.rem(dp, 2)
        near = z + 1 - 2 * lax.rem(z, 2)
        across = lax.rem(z + 2, 4)
        self.y_peer = (2 * z + 1 - y, mp)
        self.near, self.across = (2 * near + y, mp), (2 * across + y, mp)
        self.links = links
        self.z_copies = [None] * 3

    def plan_y(self, sources):
        self.y_copies = [
            self.links.copy(src, self.y_recv.at[i], self.y_peer) for i, src in enumerate(sources)
        ]

    def plan_z(self, first=None, third=None):
        own, to = self.own, self.z_recv
        self.z_copies = [
            self.links.copy(own.at[0] if first is None else first, to.at[0], self.near),
            self.links.copy(own.at[1], to.at[2], self.across),
            self.links.copy(own.at[2] if third is None else third, to.at[1], self.near),
        ]

    def add(self, i, other):
        self.own[i] = (self.own[i].astype(f32) + other.astype(f32)).astype(bf16)

    def take_y(self, i):
        self.y_copies[i].wait_recv()
        self.add(i, self.y_recv[i])
        if i == 0 or i == 2:
            self.z_copies[i].start()

    def take_near(self):
        self.z_copies[0].wait_recv()
        self.add(1, self.z_recv[0])
        self.z_copies[1].start()

    def total(self):
        self.z_copies[2].wait_recv()
        self.z_copies[1].wait_recv()
        return self.own[3].astype(f32) + self.z_recv[1].astype(f32) + self.z_recv[2].astype(f32)

    def wait_send(self, with_y=True):
        for copy in (self.y_copies if with_y else []) + self.z_copies:
            copy.wait_send()


def z_order(z):
    near = z + 1 - 2 * lax.rem(z, 2)
    return [lax.rem(near + 2, 4), lax.rem(z + 2, 4), near, z]


def back_kernel(
    exchange,
    grad_attn_own,
    tokens,
    gain,
    grad_h1,
    qkv,
    mixed,
    lse,
    w_query,
    w_key,
    w_value,
    w_out,
    bucket,
    gain_ff_part,
    table,
    first,
    normed_in,
    down_in,
    gate_in,
    up_in,
    grad_input,
    stats_out,
    attn_out,
    gate_out,
    up_out,
    down_out,
    grad_attn,
    normed,
    strip,
    strip_grad,
    key_head,
    value_head,
    grad_mixed,
    query_sum,
    key_sum,
    value_sum,
    grad_qkv,
    own_terms,
    tx,
    rx,
    down_own,
    down_z,
    gate_own,
    gate_y,
    gate_z,
    up_own,
    up_y,
    up_z,
    attn_own,
    attn_send,
    attn_y,
    attn_z,
    stats,
    stats_recv,
    send,
    recv,
    local,
):
    group = Group()
    me, core, far, diag = group.me, group.core, group.far, group.diag
    rows, width = grad_h1.shape
    half = rows // 2
    length = 4 * rows
    part = width // 4
    heads = table.shape[1]
    span = 2 * length
    links = Links(send, recv)
    dp = group.dp
    peers = [group.at(core), group.at(far)]
    copies = []

    def load(src, dst):
        copy = pltpu.make_async_copy(src, dst, local.at[len(copies)])
        copies.append(copy)
        return copy

    save_normed = load(normed_in, normed)
    save_normed.start()
    if exchange:
        z, y = dp // 2, lax.rem(dp, 2)
        order = z_order(z)
        sums = [
            Halving(links, dp, me, own, y_recv, z_recv)
            for own, y_recv, z_recv in (
                (down_own, None, down_z),
                (gate_own, gate_y, gate_z),
                (up_own, up_y, up_z),
                (attn_own, attn_y, attn_z),
            )
        ]
        down, gate, up, attn = sums
        peers += [down.y_peer, down.near, down.across]
        loads = [load(down_in.at[order[i]], down_own.at[i]) for i in (1, 3)]
        gate_loads = [load(gate_in.at[order[i], y], gate_own.at[i]) for i in range(4)]
        up_loads = [load(up_in.at[order[i], y], up_own.at[i]) for i in range(4)]
        for copy in loads + gate_loads + up_loads:
            copy.start()
        down.plan_z(down_in.at[order[0]], down_in.at[order[2]])
        gate.plan_y([gate_in.at[order[i], 1 - y] for i in range(4)])
        gate.plan_z()
        up.plan_y([up_in.at[order[i], 1 - y] for i in range(4)])
        up.plan_z()
        attn.plan_y([attn_send.at[i] for i in range(4)])
        attn.plan_z()
    else:
        order = [0, 1, 2, 3]
    grad_attn[block_rows(me, rows), :] = grad_attn_own[...]
    greet(peers)
    gather = Gather(links, group, grad_attn, rows, 2)
    gather.start()
    if exchange:
        for copy in gate.y_copies:
            copy.start()
        down.z_copies[0].start()
        down.z_copies[2].start()
    scatter = Scatter(links, group, tx, rx, rows, 1)
    stages = []
    for i, to in enumerate([group.at(core), group.at(far)] + peers[2:]):
        stages.append(links.copy(stats.at[i], stats_recv.at[i], to))

    build_strips(strip, bucket, table)
    strip_grad[...] = jnp.zeros_like(strip_grad)
    query_sum[...] = jnp.zeros_like(query_sum)
    key_sum[...] = jnp.zeros_like(key_sum)
    value_sum[...] = jnp.zeros_like(value_sum)

    def mix_back(dev):
        at = block_rows(dev, rows)
        grad_mixed[at, :] = contract_cols(grad_attn[at, :], w_out[...]).astype(bf16)

    mix_back(me)
    gather.near.wait_recv()
    mix_back(core)

    def attend_back(dev, h):
        at = block_rows(dev, rows)
        seen = visible_pairs(dev, rows, length, first[0])
        query, grad = qkv[0, at, :], grad_mixed[at, :]
        lanes = head_lanes(query.shape, h)
        zero = jnp.zeros_like(query)
        scores = contract_cols(query, key_head[...])
        scores = jnp.where(seen, add_bias(scores, strip, h, dev, length), masked_score)
        probs = jnp.exp(scores - lse[at, h : h + 1])
        inner = contract_cols(grad, value_head[...])
        center = jnp.sum(probs * inner, axis=-1, keepdims=True)
        score_grad = (probs * (inner - center)).astype(bf16)
        query_sum[at, :] += mm(score_grad, key_head[...])
        key_sum[...] += contract_rows(score_grad, jnp.where(lanes, query, zero))
        value_sum[...] += contract_rows(probs.astype(bf16), jnp.where(lanes, grad, zero))
        count = length // 128
        for i in range(rows // 128):
            start = (count - 1 - i) * 128 - dev * rows
            to = pl.ds(pl.multiple_of(start, 128), length)
            strip_grad[h, :, to] += score_grad[i * 128 : (i + 1) * 128].astype(f32)

    def head_keys(h):
        key, value = qkv[1], qkv[2]
        lanes = head_lanes(key.shape, h)
        key_head[...] = jnp.where(lanes, key, jnp.zeros_like(key))
        value_head[...] = jnp.where(lanes, value, jnp.zeros_like(value))

    def take_gate(i):
        gate_loads[i].wait()
        gate.take_y(i)
        if i == 0:
            up.y_copies[0].start()
            up.y_copies[1].start()
        if i == 1:
            up.y_copies[2].start()
            up.y_copies[3].start()

    def take_up(i):
        up_loads[i].wait()
        up.take_y(i)

    def down_near():
        loads[0].wait()
        loads[1].wait()
        down.take_near()

    def down_total():
        down_out[...] = down.total()

    def gate_total():
        gate_out[...] = gate.total()

    def up_total():
        up_out[...] = up.total()

    head_keys(0)
    if exchange:
        take_gate(0)
    gather.forward(0)
    gather.forward(1)
    mix_back(far)
    for copy in gather.passed:
        copy.wait_recv()
    mix_back(diag)
    between = {
        (0, 1): [lambda: take_gate(1), down_near],
        (1, 1): [lambda: take_gate(2)],
        (2, 0): [down_total],
        (2, 2): [lambda: take_gate(3), gate.take_near],
    } if exchange else {}
    for h in range(heads):
        if h:
            head_keys(h)
        for j, dev in enumerate((diag, far, core, me)):
            attend_back(dev, h)
            for step in between.get((h, j), []):
                step()

    grad_qkv[0] = query_sum[...].astype(bf16)
    grad_qkv[1] = key_sum[...].astype(bf16)
    grad_qkv[2] = value_sum[...].astype(bf16)

    def terms(dev):
        at = block_rows(dev, rows)
        return (
            mm(grad_qkv[0, at, :], w_query[...])
            + mm(grad_qkv[1, at, :], w_key[...])
            + mm(grad_qkv[2, at, :], w_value[...])
        )

    scatter.send_diag(0, terms(diag))
    scatter.send_near(terms(core))
    scatter.send_far(0, terms(far))
    own_terms[...] = terms(me)
    save_normed.wait()

    cols = mixed.shape[1]
    for i in range(4):
        at = pl.ds(pl.multiple_of(order[i] * part, 128), part)
        for m in range(4):
            if m < 3:
                block = contract_rows(normed[:, at], grad_qkv[m]).astype(bf16)
            else:
                block = contract_rows(grad_attn[:, at], mixed[...]).astype(bf16)
            if exchange:
                low, high = block[: part // 2], block[part // 2 :]
                attn_send[i, m] = jnp.where(y == 0, high, low)
                attn_own[i, m] = jnp.where(y == 0, low, high)
            else:
                attn_out[m, at, :] = block
        if exchange:
            attn.y_copies[i].start()
        if exchange and i == 1:
            take_up(0)

    index = bucket[...]
    lines = []
    for h in range(heads):
        fold = strip_grad[h]
        count = 128
        while count > 1:
            count //= 2
            fold = fold[:count] + pltpu.roll(fold[count:], span - count, 1)
        lines.append(pltpu.roll(fold, 127, 1))
    diagonals = jnp.concatenate(lines + [jnp.zeros((8 - heads, span), f32)], axis=0)
    buckets = table.shape[0]
    onehot = (lax.broadcasted_iota(jnp.int32, (buckets, span), 0) == index).astype(f32)
    table_part = lax.dot_general(
        diagonals, onehot, (((1,), (1,)), ((), ())), precision=highest, preferred_element_type=f32
    )
    if exchange:
        take_up(1)

    value = tokens[...].astype(f32)
    pulled, gain_part = norm_pull(value, gain[...], scatter.total(own_terms[...]))
    grad_input[...] = grad_h1[...] + pulled
    stats[0] = jnp.zeros_like(stats[0])
    stats[0, 0:1, :] = gain_part
    stats[0, 1:2, :] = gain_ff_part[...]
    last = len(stages)
    for i, stage in enumerate(stages):
        stage.start()
        if exchange and i == 2:
            take_up(2)
            up.take_near()
        stage.wait_recv()
        total = stats[i] + stats_recv[i]
        if i + 1 < last:
            stats[i + 1] = total
            if i == 1:
                stats[i + 1, 2 : 2 + heads, 0:buckets] = table_part[0:heads]
        else:
            stats_out[...] = total
            if i == 1:
                stats_out[2 : 2 + heads, 0:buckets] = table_part[0:heads]
    if exchange:
        gate_total()
        take_up(3)
        for i in range(3):
            attn.take_y(i)
        attn.take_near()
        attn.take_y(3)
        up_total()
        attn_out[...] = attn.total()
        down.wait_send(with_y=False)
        gate.wait_send()
        up.wait_send()
        attn.wait_send()
    gather.wait_send()
    scatter.wait_send()
    for stage in stages:
        stage.wait_send()


def attention_backward(
    exchange, grad_attn, tokens, gain, grad_h1, qkv, mixed, lse, w_query, w_key, w_value, w_out, bucket, gain_ff_part,
    table, first, normed, down_in, gate_in, up_in,
):
    rows, width = grad_h1.shape
    length = 4 * rows
    cols = w_query.shape[0]
    ff = down_in.shape[-1]
    heads = table.shape[1]
    part = width // 8
    shape = jax.ShapeDtypeStruct
    small = (1,) if not exchange else None
    scratch = [
        pltpu.VMEM((length, width), bf16),
        pltpu.VMEM((length, width), bf16),
        pltpu.VMEM((heads, 128, 2 * length), f32),
        pltpu.VMEM((heads, 128, 2 * length), f32),
        pltpu.VMEM((length, cols), bf16),
        pltpu.VMEM((length, cols), bf16),
        pltpu.VMEM((length, cols), bf16),
        pltpu.VMEM((length, cols), f32),
        pltpu.VMEM((length, cols), f32),
        pltpu.VMEM((length, cols), f32),
        pltpu.VMEM((3, length, cols), bf16),
        pltpu.VMEM((rows, width), f32),
        pltpu.VMEM((3, rows, width), bf16),
        pltpu.VMEM((3, rows, width), bf16),
    ]
    for count in (4, 3, 4, 4, 3, 4, 4, 3):
        scratch.append(pltpu.VMEM((count, part, ff) if exchange else (8, 128), bf16))
    for count in (4, 4, 4, 3):
        scratch.append(pltpu.VMEM((count, 4, part, cols) if exchange else (8, 128), bf16))
    stages = 5 if exchange else 2
    scratch += [
        pltpu.VMEM((stages, 8, width), f32),
        pltpu.VMEM((stages, 8, width), f32),
        pltpu.SemaphoreType.DMA((40,)),
        pltpu.SemaphoreType.DMA((40,)),
        pltpu.SemaphoreType.DMA((12,)),
    ]
    ff_out = shape((part, ff) if exchange else (8, 128), f32)
    return pl.pallas_call(
        functools.partial(back_kernel, exchange),
        out_shape=(
            shape((rows, width), f32),
            shape((8, width), f32),
            shape((4, part, cols), f32) if exchange else shape((4, width, cols), bf16),
            ff_out,
            ff_out,
            ff_out,
        ),
        in_specs=[in_vmem()] * 13 + [in_smem()] * 2 + [anywhere()] * 4,
        out_specs=[in_vmem()] * 6,
        scratch_shapes=scratch,
        compiler_params=pltpu.CompilerParams(
            collective_id=2, has_side_effects=True, vmem_limit_bytes=VMEM_BYTES
        ),
    )(
        grad_attn, tokens, gain, grad_h1, qkv, mixed, lse, w_query, w_key, w_value, w_out, bucket, gain_ff_part,
        table, first, normed, down_in, gate_in, up_in,
    )


def shards(
    tokens,
    gain_attn,
    w_query,
    w_key,
    w_value,
    w_out,
    bias_table,
    gain_ff,
    w_gate,
    w_up,
    w_down,
    cotangent,
    first_length,
    offset_bucket,
):
    n_dp = lax.axis_size("dp")
    exchange = n_dp == 8
    buckets, heads = bias_table.shape
    width = tokens.shape[1]
    bucket = jnp.pad(offset_bucket, (0, 1), constant_values=-1)[None, :]
    gain_first, gain_second = gain_attn[None], gain_ff[None]
    turned = [w_query.T, w_key.T, w_value.T]
    qkv, mixed, lse, h1, normed_ff, normed, cot_full = attention_forward(
        n_dp, tokens, gain_first, gain_second, *turned, bucket, bias_table, first_length, w_out, cotangent
    )
    output, grad_h1, grad_attn, gain_ff_part, down, gate, up = feed_forward(
        exchange, normed_ff, h1, gain_second, w_gate.T, w_up.T, w_down, cot_full
    )
    grad_input, stats, attn, gate_sum, up_sum, down_sum = attention_backward(
        exchange, grad_attn, tokens, gain_first, grad_h1, qkv, mixed, lse, *turned, w_out, bucket, gain_ff_part,
        bias_table, first_length, normed, down, gate, up,
    )
    if not exchange:
        def scatter(value):
            value = value.reshape(width, -1).astype(f32)
            return lax.psum_scatter(value, "dp", scatter_dimension=0, tiled=True)

        stats = lax.psum(stats, "dp")
        gate_sum, up_sum, down_sum = scatter(gate), scatter(up), scatter(down)
        attn = [scatter(attn[i]) for i in range(4)]
    return (
        output,
        grad_input,
        stats[0],
        attn[0],
        attn[1],
        attn[2],
        attn[3].T,
        stats[2 : 2 + heads, :buckets].T,
        stats[1],
        gate_sum,
        up_sum,
        down_sum.T,
    )


def solution(mesh):
    placed = (
        P(("dp", "mp"), None),
        P(),
        P(None, "mp"),
        P(None, "mp"),
        P(None, "mp"),
        P("mp", None),
        P(None, "mp"),
        P(),
        P(None, "mp"),
        P(None, "mp"),
        P("mp", None),
        P(("dp", "mp"), None),
        P("dp"),
        P(),
    )
    return jax.shard_map(
        shards,
        mesh=mesh,
        in_specs=placed,
        out_specs=(
            P(("dp", "mp"), None),
            P(("dp", "mp"), None),
            P(),
            P("dp", "mp"),
            P("dp", "mp"),
            P("dp", "mp"),
            P("mp", "dp"),
            P(None, "mp"),
            P(),
            P("dp", "mp"),
            P("dp", "mp"),
            P("mp", "dp"),
        ),
        check_vma=False,
    )
```

```python
import functools

import jax
import jax.numpy as jnp
from jax import lax
from jax.experimental import pallas as pl
from jax.experimental.pallas import tpu as pltpu
from jax.sharding import PartitionSpec as P

MESH = pl.DeviceIdType.MESH
DH = 64
epsilon = 1e-06
masked_score = -1000000000.0
highest = lax.Precision.HIGHEST
bf16 = jnp.bfloat16
f32 = jnp.float32
VMEM_BYTES = 62 * 2**20


def mm(left, right):
    return jnp.dot(left, right, preferred_element_type=f32)


def contract_rows(left, right):
    return lax.dot_general(left, right, (((0,), (0,)), ((), ())), preferred_element_type=f32)


def contract_cols(left, right):
    return lax.dot_general(left, right, (((1,), (1,)), ((), ())), preferred_element_type=f32)


def rms(values):
    return values * lax.rsqrt(jnp.mean(values * values, axis=-1, keepdims=True) + epsilon)


class Links:
    def __init__(self, send, recv):
        self.send, self.recv, self.used = send, recv, 0

    def copy(self, src, dst, to):
        at = self.used
        self.used += 1
        return pltpu.make_async_remote_copy(
            src_ref=src,
            dst_ref=dst,
            send_sem=self.send.at[at],
            recv_sem=self.recv.at[at],
            device_id=to,
            device_id_type=MESH,
        )


class Group:
    def __init__(self):
        self.dp, self.me = lax.axis_index("dp"), lax.axis_index("mp")
        self.core = self.me + 1 - 2 * lax.rem(self.me, 2)
        self.far = lax.rem(self.me + 2, 4)
        self.diag = 3 - self.me

    def at(self, mp):
        return (self.dp, mp)


def greet(peers):
    barrier = pltpu.get_barrier_semaphore()
    for peer in peers:
        pl.semaphore_signal(barrier, inc=1, device_id=peer, device_id_type=MESH)
    pl.semaphore_wait(barrier, len(peers))


def block_rows(dev, rows, start=0, size=None):
    return pl.ds(pl.multiple_of(dev * rows + start, 16), rows if size is None else size)


class Gather:
    def __init__(self, links, group, full, rows, chunks, source=None):
        size = rows // chunks
        own = block_rows(group.me, rows)
        self.near = links.copy(full.at[own] if source is None else source, full.at[own], group.at(group.core))
        self.far, self.passed = [], []
        for i in range(chunks):
            mine = block_rows(group.me, rows, i * size, size)
            theirs = block_rows(group.far, rows, i * size, size)
            src = full.at[mine] if source is None else source.at[pl.ds(i * size, size)]
            self.far.append(links.copy(src, full.at[mine], group.at(group.far)))
            self.passed.append(links.copy(full.at[theirs], full.at[theirs], group.at(group.core)))

    def start(self):
        self.near.start()
        for copy in self.far:
            copy.start()

    def forward(self, i):
        self.far[i].wait_recv()
        self.passed[i].start()

    def wait_send(self):
        self.near.wait_send()
        for copy in self.far + self.passed:
            copy.wait_send()


def pack_small(gain_attn, gain_ff, offset_bucket, table):
    width = offset_bucket.shape[0] + 1

    def row(values, fill=0.0):
        values = values.astype(f32).reshape(-1, values.shape[-1])
        return jnp.pad(values, ((0, 0), (0, width - values.shape[1])), constant_values=fill)

    return jnp.concatenate([row(gain_attn), row(gain_ff), row(offset_bucket, -1.0), row(table.T)])


def build_strips(strip, small, buckets):
    index = small[2:3, :]
    heads, _, width = strip.shape
    for h in range(heads):
        row = jnp.zeros(index.shape, f32)
        for b in range(buckets):
            row = jnp.where(index == float(b), small[3 + h : 4 + h, b : b + 1], row)
        strip[h] = pltpu.roll(
            jnp.broadcast_to(row, (128, width)), width - 127, 1, stride=1, stride_axis=0
        )


def add_bias(scores, strip, h, dev, length):
    parts = []
    count = length // 128
    for i in range(scores.shape[0] // 128):
        first = (count - 1 - i) * 128 - dev * scores.shape[0]
        parts.append(
            scores[i * 128 : (i + 1) * 128]
            + strip[h, :, pl.ds(pl.multiple_of(first, 128), length)]
        )
    return jnp.concatenate(parts, axis=0)


def visible_pairs(dev, rows, length, first):
    query = lax.broadcasted_iota(jnp.int32, (rows, length), 0) + dev * rows >= first
    key = lax.broadcasted_iota(jnp.int32, (rows, length), 1) >= first
    return query == key


def head_lanes(shape, h):
    lane = lax.broadcasted_iota(jnp.int32, shape, len(shape) - 1)
    return (lane >= h * DH) & (lane < (h + 1) * DH)


def norm_pull(values, gain, grad):
    inverse = lax.rsqrt(jnp.mean(values * values, axis=-1, keepdims=True) + epsilon)
    scaled = grad * gain
    along = jnp.mean(values * scaled, axis=-1, keepdims=True)
    gain_grad = jnp.sum(grad * values * inverse, axis=0, keepdims=True)
    return inverse * scaled - values * (along * inverse * inverse * inverse), gain_grad


class Scatter:
    def __init__(self, links, group, tx, rx, rows, parts):
        self.tx, self.rx, self.size = tx, rx, rows // parts
        core, far = group.at(group.core), group.at(group.far)
        self.near = links.copy(tx.at[2], rx.at[2], core)
        self.diag, self.far = [], []
        for i in range(parts):
            at = pl.ds(i * self.size, self.size)
            self.diag.append(links.copy(tx.at[0, at], rx.at[0, at], core))
            self.far.append(links.copy(tx.at[1, at], rx.at[1, at], far))

    def send_diag(self, i, terms):
        self.tx[0, pl.ds(i * self.size, self.size), :] = terms.astype(bf16)
        self.diag[i].start()

    def send_near(self, terms):
        self.tx[2] = terms.astype(bf16)
        self.near.start()

    def send_far(self, i, terms):
        at = pl.ds(i * self.size, self.size)
        self.diag[i].wait_recv()
        self.tx[1, at, :] = (terms + self.rx[0, at, :].astype(f32)).astype(bf16)
        self.far[i].start()

    def total(self, own):
        self.near.wait_recv()
        for copy in self.far:
            copy.wait_recv()
        return own + self.rx[2].astype(f32) + self.rx[1].astype(f32)

    def wait_send(self):
        for copy in [self.near] + self.diag + self.far:
            copy.wait_send()


GELU_SLOPE = 0.7978845608028654
GELU_CUBE = 0.044715


def z_order(z):
    near = z + 1 - 2 * lax.rem(z, 2)
    return [lax.rem(near + 2, 4), lax.rem(z + 2, 4), near, z]


def forward_kernel(
    exchange,
    buckets,
    tokens,
    small,
    first,
    w_query,
    w_key,
    w_value,
    w_out,
    gate_w,
    up_w,
    down_w,
    cot_in,
    qkv,
    mixed,
    lse,
    output,
    grad_h1,
    grad_attn,
    gain_grad,
    normed_out,
    down_out,
    gate_out,
    up_out,
    normed,
    cot,
    wg,
    wu,
    wd,
    strip,
    hidden,
    gate_act,
    up_act,
    mixed_all,
    mixed_sum,
    far_terms,
    own_terms,
    tx,
    rx,
    tx_ff,
    rx_ff,
    down_grad,
    gate_grad,
    up_grad,
    y_recv,
    z_recv,
    send,
    recv,
    local,
):
    group = Group()
    me, core, far, diag = group.me, group.core, group.far, group.diag
    rows, width = tokens.shape
    half = rows // 2
    length = 4 * rows
    heads = strip.shape[0]
    depth = w_out.shape[0]
    ff = wg.shape[0]
    part = width // 4
    gain_attn, gain_ff = small[0:1, 0:width], small[1:2, 0:width]
    links = Links(send, recv)
    peers = [group.at(core), group.at(far), group.at(diag)]
    z_peers = []
    if exchange:
        z, y = group.dp // 2, lax.rem(group.dp, 2)
        order = z_order(z)
        y_peer = (2 * z + 1 - y, me)
        near_peer = (2 * order[2] + y, me)
        z_peers = [(2 * lax.rem(z + t, 4) + y, me) for t in (1, 2, 3)]
        peers += [y_peer] + z_peers
    else:
        order, y = [0, 1, 2, 3], 0

    def block_at(t):
        found = jnp.int32(order[3])
        for i in range(3):
            found = jnp.where(t == i, order[i], found)
        return found

    started = []

    def load(src, dst):
        copy = pltpu.make_async_copy(src, dst, local.at[len(started)])
        started.append(copy)
        return copy

    def depth_rows(i):
        return pl.ds(pl.multiple_of(i * depth, 16), depth)

    own = block_rows(me, rows)
    out_own = load(w_out, wu.at[depth_rows(me)])
    out_own.start()
    proj_loads = [load(w, wg.at[depth_rows(i)]) for i, w in enumerate((w_query, w_key, w_value))]
    for copy in proj_loads:
        copy.start()
    cot_own = load(cot_in, cot.at[own])
    cot_own.start()
    down_load = load(down_w, wd)
    down_load.start()
    greet(peers)

    x = tokens[...].astype(f32)
    normed[own, :] = (rms(x) * gain_attn).astype(bf16)
    gather = Gather(links, group, normed, rows, 2)
    gather.start()
    out_own.wait()
    parts = 4 if exchange else 1
    piece = depth // parts

    def out_rows(dev):
        start = dev * depth + (z * piece if exchange else 0)
        return pl.ds(pl.multiple_of(start, 16), piece)

    out_near = links.copy(wu.at[depth_rows(me)], wu.at[depth_rows(me)], group.at(core))
    out_far = links.copy(wu.at[out_rows(me)], wu.at[out_rows(me)], group.at(far))
    out_near.start()
    out_z = [links.copy(wu.at[out_rows(far)], wu.at[out_rows(far)], peer) for peer in z_peers]
    out_pass = links.copy(wu.at[depth_rows(far)], wu.at[depth_rows(far)], group.at(core))
    cot_gather = Gather(links, group, cot, rows, 4, source=cot_in)
    cot_gather.near.start()
    mixed_near = links.copy(mixed.at[block_rows(core, rows)], mixed_all.at[me], group.at(core))
    mixed_far = links.copy(mixed.at[block_rows(far, rows)], mixed_all.at[me], group.at(far))
    mixed_diag = links.copy(mixed.at[block_rows(diag, rows)], mixed_all.at[me], group.at(diag))

    build_strips(strip, small, buckets)
    for copy in proj_loads:
        copy.wait()

    def project(dev):
        at = block_rows(dev, rows)
        block = normed[at, :]
        for i in range(3):
            qkv[i, at, :] = contract_cols(block, wg[i * depth : (i + 1) * depth, :]).astype(bf16)

    project(me)
    gather.near.wait_recv()
    project(core)
    gather.forward(0)
    gather.forward(1)
    out_far.start()
    cot_gather.far[0].start()
    project(far)
    for copy in gather.passed:
        copy.wait_recv()
    normed_save = load(normed, normed_out)
    normed_save.start()
    project(diag)
    gate_load = load(gate_w, wg)
    gate_load.start()

    def attend(dev):
        at = block_rows(dev, rows)
        seen = visible_pairs(dev, rows, length, first[0])
        mixed_sum[...] = jnp.zeros_like(mixed_sum)
        lse[at, :] = jnp.zeros((rows, 128), f32)

        def one_head(h, carry):
            query = qkv[0, at, :]
            lanes = head_lanes(query.shape, h)
            scores = contract_cols(jnp.where(lanes, query, jnp.zeros_like(query)), qkv[1])
            scores = jnp.where(seen, add_bias(scores, strip, h, dev, length), masked_score)
            top = jnp.max(scores, axis=-1, keepdims=True)
            expo = jnp.exp(scores - top)
            total = jnp.sum(expo, axis=-1, keepdims=True)
            weights = (expo * (1.0 / total)).astype(bf16)
            mixed_sum[...] = jnp.where(lanes, mm(weights, qkv[2]), mixed_sum[...])
            lane = lax.broadcasted_iota(jnp.int32, (rows, 128), 1)
            lse[at, :] = jnp.where(lane == h, top + jnp.log(total), lse[at, :])
            return carry

        lax.fori_loop(0, heads, one_head, 0)
        mixed[at, :] = mixed_sum[...].astype(bf16)

    attend(far)
    gather.wait_send()
    normed_save.wait()
    mixed_far.start()
    cot_gather.far[1].start()
    out_far.wait_recv()
    for copy in out_z:
        copy.start()
    attend(diag)
    mixed_diag.start()
    cot_gather.far[2].start()
    attend(core)
    mixed_near.start()
    for copy in out_z:
        copy.wait_recv()
    out_pass.start()
    cot_gather.forward(0)
    attend(me)
    mixed_all[me] = mixed[own, :]
    out_near.wait_recv()
    attn = mm(mixed_all[me], wu[depth_rows(me), :])
    mixed_near.wait_recv()
    attn = attn + mm(mixed_all[core], wu[depth_rows(core), :])
    mixed_far.wait_recv()
    attn = attn + mm(mixed_all[far], wu[depth_rows(far), :])
    mixed_diag.wait_recv()
    out_pass.wait_recv()
    attn = attn + mm(mixed_all[diag], wu[depth_rows(diag), :])
    residual = x + attn
    grad_h1[...] = residual
    normed[own, :] = (rms(residual) * gain_ff).astype(bf16)
    second = Gather(links, group, normed, rows, 2)
    second.near.start()
    second.far[0].start()
    cot_gather.far[3].start()
    second.far[1].start()
    for copy in [out_near, out_far, out_pass] + out_z:
        copy.wait_send()
    up_load = load(up_w, wu)
    up_load.start()

    scatter = Scatter(links, group, tx, rx, rows, 2)
    scatter_ff = Scatter(links, group, tx_ff, rx_ff, rows, 1)

    def pair(ref, start, after):
        return jnp.concatenate(
            [
                ref[pl.ds(pl.multiple_of(start, 128), half), :],
                ref[pl.ds(pl.multiple_of(after, 128), half), :],
            ],
            axis=0,
        )

    def keep(i, value):
        strip[i, :, 0:ff] = value[:half]
        strip[i, :, length : length + ff] = value[half:]

    def unit(start, after):
        block = pair(normed, start, after)
        keep(0, contract_cols(block, wg[...]))
        keep(1, contract_cols(block, wu[...]))
        keep(2, contract_cols(pair(cot, start, after), wd[...]))
        for offset, lane in ((start, 0), (after, length)):

            def act(i, carry):
                at = pl.ds(pl.multiple_of(i * 16, 16), 16)
                to = pl.ds(pl.multiple_of(offset + i * 16, 16), 16)
                v, u, g = (strip[k, at, lane : lane + ff] for k in range(3))
                square = v * v
                t = jnp.tanh(GELU_SLOPE * v * (1.0 + GELU_CUBE * square))
                lift = 0.5 * (1.0 + t)
                value = v * lift
                slope = lift + 0.5 * v * (1.0 - t * t) * (
                    GELU_SLOPE * (1.0 + 3.0 * GELU_CUBE * square)
                )
                hidden[to, :] = (value * u).astype(bf16)
                gate_act[to, :] = (g * u * slope).astype(bf16)
                up_act[to, :] = (g * value).astype(bf16)
                return carry

            lax.fori_loop(0, half // 16, act, 0)

    def terms(start, after):
        return mm(pair(gate_act, start, after), wg[...]) + mm(
            pair(up_act, start, after), wu[...]
        )

    def weight_blocks(left, right, store):
        def one(t, carry):
            at = pl.ds(pl.multiple_of(block_at(t) * part, 128), part)
            value = contract_rows(left[:, at], right[...]).astype(bf16)
            store(t, value[: part // 2], value[part // 2 :])
            return carry

        lax.fori_loop(0, 4, one, 0)

    cot_own.wait()
    down_load.wait()
    gate_load.wait()
    up_load.wait()
    unit(me * rows, me * rows + half)
    cot_gather.forward(1)
    cot_gather.near.wait_recv()
    second.near.wait_recv()
    unit(core * rows, core * rows + half)
    second.forward(0)
    second.passed[0].wait_recv()
    for i in (0, 1):
        cot_gather.passed[i].wait_recv()
    unit(far * rows, diag * rows)
    both = terms(far * rows, diag * rows)
    scatter.send_diag(0, both[half:])
    far_terms[pl.ds(0, half), :] = both[:half]
    cot_gather.forward(2)
    cot_gather.forward(3)
    scatter.send_far(0, far_terms[pl.ds(0, half), :])
    second.forward(1)
    own_terms[...] = terms(me * rows, me * rows + half)
    for i in (2, 3):
        cot_gather.passed[i].wait_recv()
    second.passed[1].wait_recv()
    unit(far * rows + half, diag * rows + half)

    base = links.used
    links.used += 8

    def y_copy(t):
        return pltpu.make_async_remote_copy(
            src_ref=down_grad.at[t, 1 - y],
            dst_ref=y_recv.at[t],
            send_sem=send.at[base + t],
            recv_sem=recv.at[base + t],
            device_id=y_peer,
            device_id_type=MESH,
        )

    def z_copy(i, side):
        return pltpu.make_async_remote_copy(
            src_ref=gate_grad.at[2 * i, side],
            dst_ref=z_recv.at[i, side],
            send_sem=send.at[base + 4 + 2 * i + side],
            recv_sem=recv.at[base + 4 + 2 * i + side],
            device_id=near_peer,
            device_id_type=MESH,
        )

    spots = len(started)

    def save(src, dst, at):
        return pltpu.make_async_copy(src, dst, local.at[spots + at])

    def store_down(t, low, high):
        down_grad[t, 0] = low
        down_grad[t, 1] = high
        if exchange:
            y_copy(t).start()
        else:
            save(down_grad.at[t], down_out.at[t], t).start()

    def store_gate(t, low, high):
        gate_grad[t, 0] = low
        gate_grad[t, 1] = high
        if exchange:

            @pl.when(lax.rem(t, 2) == 0)
            def _():
                z_copy(t // 2, 0).start()
                z_copy(t // 2, 1).start()
        else:
            save(gate_grad.at[t], gate_out.at[t], 4 + t).start()

    def store_up(t, low, high):
        slot = lax.rem(t, 2)

        @pl.when(t >= 2)
        def _():
            save(up_grad.at[slot], up_out.at[t - 2], 8 + t - 2).wait()

        up_grad[slot, 0] = low
        up_grad[slot, 1] = high
        save(up_grad.at[slot], up_out.at[t], 8 + t).start()

    weight_blocks(cot, hidden, store_down)
    both = terms(far * rows + half, diag * rows + half)
    scatter.send_diag(1, both[half:])
    far_terms[pl.ds(half, half), :] = both[:half]
    scatter.send_near(terms(core * rows, core * rows + half))
    scatter.send_far(1, far_terms[pl.ds(half, half), :])
    weight_blocks(normed, gate_act, store_gate)

    def ff_terms(dev):
        return mm(hidden[block_rows(dev, rows), :], wd[...])

    scatter_ff.send_diag(0, ff_terms(diag))
    scatter_ff.send_near(ff_terms(core))
    scatter_ff.send_far(0, ff_terms(far))
    weight_blocks(normed, up_act, store_up)

    residual = grad_h1[...]
    pulled, gain_part = norm_pull(residual, gain_ff, scatter.total(own_terms[...]))
    gain_grad[...] = gain_part
    grad = cot[own, :].astype(f32) + pulled
    own_terms[...] = residual + ff_terms(me)
    grad_h1[...] = grad
    grad_attn[...] = grad.astype(bf16)

    if exchange:

        def sum_down(t, carry):
            y_copy(t).wait_recv()
            down_grad[t, y] = (
                down_grad[t, y].astype(f32) + y_recv[t].astype(f32)
            ).astype(bf16)
            save(down_grad.at[t, y], down_out.at[t], t).start()
            return carry

        lax.fori_loop(0, 4, sum_down, 0)
        for i in range(2):
            for side in range(2):
                z_copy(i, side).wait_recv()
                kept = gate_grad.at[2 * i + 1, side]
                kept[...] = (kept[...].astype(f32) + z_recv[i, side].astype(f32)).astype(bf16)
                save(kept, gate_out.at[i, side], 4 + 2 * i + side).start()

    output[...] = scatter_ff.total(own_terms[...]).astype(bf16)

    for t in range(4):
        if exchange:
            save(down_grad.at[t, y], down_out.at[t], t).wait()
            save(gate_grad.at[t // 2 * 2 + 1, t % 2], gate_out.at[t // 2, t % 2], 4 + t).wait()
            y_copy(t).wait_send()
            z_copy(t // 2, t % 2).wait_send()
        else:
            save(down_grad.at[t], down_out.at[t], t).wait()
            save(gate_grad.at[t], gate_out.at[t], 4 + t).wait()
        if t >= 2:
            save(up_grad.at[t % 2], up_out.at[t], 8 + t).wait()
    for copy in (mixed_near, mixed_far, mixed_diag):
        copy.wait_send()
    cot_gather.wait_send()
    second.wait_send()
    scatter.wait_send()
    scatter_ff.wait_send()


def in_vmem():
    return pl.BlockSpec(memory_space=pltpu.VMEM)


def anywhere():
    return pl.BlockSpec(memory_space=pl.ANY)


def in_smem():
    return pl.BlockSpec(memory_space=pltpu.SMEM)


def forward(exchange, table_shape, tokens, small, first, w_query, w_key, w_value, w_out, gate_w, up_w, down_w, cot):
    rows, width = tokens.shape
    length = 4 * rows
    cols = w_query.shape[0]
    ff = gate_w.shape[0]
    buckets, heads = table_shape
    part = width // 8
    shape = jax.ShapeDtypeStruct
    halves = (4, 2, part, ff)
    return pl.pallas_call(
        functools.partial(forward_kernel, exchange, buckets),
        out_shape=(
            shape((3, length, cols), bf16),
            shape((length, cols), bf16),
            shape((length, 128), f32),
            shape((rows, width), bf16),
            shape((rows, width), f32),
            shape((rows, width), bf16),
            shape((1, width), f32),
            shape((length, width), bf16),
            shape((4, part, ff) if exchange else halves, bf16),
            shape((2, 2, part, ff) if exchange else halves, bf16),
            shape(halves, bf16),
        ),
        in_specs=[in_vmem()] * 2 + [in_smem()] + [anywhere()] * 8,
        out_specs=[in_vmem()] * 7 + [anywhere()] * 4,
        scratch_shapes=[
            pltpu.VMEM((length, width), bf16),
            pltpu.VMEM((length, width), bf16),
            pltpu.VMEM((ff, width), bf16),
            pltpu.VMEM((ff, width), bf16),
            pltpu.VMEM((ff, width), bf16),
            pltpu.VMEM((heads, 128, 2 * length), f32),
            pltpu.VMEM((length, ff), bf16),
            pltpu.VMEM((length, ff), bf16),
            pltpu.VMEM((length, ff), bf16),
            pltpu.VMEM((4, rows, cols), bf16),
            pltpu.VMEM((rows, cols), f32),
            pltpu.VMEM((rows, width), f32),
            pltpu.VMEM((rows, width), f32),
            pltpu.VMEM((3, rows, width), bf16),
            pltpu.VMEM((3, rows, width), bf16),
            pltpu.VMEM((3, rows, width), bf16),
            pltpu.VMEM((3, rows, width), bf16),
            pltpu.VMEM(halves, bf16),
            pltpu.VMEM(halves, bf16),
            pltpu.VMEM((2, 2, part, ff), bf16),
            pltpu.VMEM((4, part, ff) if exchange else (8, 128), bf16),
            pltpu.VMEM((2, 2, part, ff) if exchange else (8, 128), bf16),
            pltpu.SemaphoreType.DMA((48,)),
            pltpu.SemaphoreType.DMA((48,)),
            pltpu.SemaphoreType.DMA((24,)),
        ],
        compiler_params=pltpu.CompilerParams(
            collective_id=0, has_side_effects=True, vmem_limit_bytes=VMEM_BYTES
        ),
    )(tokens, small, first, w_query, w_key, w_value, w_out, gate_w, up_w, down_w, cot)


class Halving:
    def __init__(self, links, dp, mp, own, y_recv, z_recv):
        self.own, self.y_recv, self.z_recv = own, y_recv, z_recv
        z, y = dp // 2, lax.rem(dp, 2)
        near = z + 1 - 2 * lax.rem(z, 2)
        across = lax.rem(z + 2, 4)
        self.y_peer = (2 * z + 1 - y, mp)
        self.near, self.across = (2 * near + y, mp), (2 * across + y, mp)
        self.links = links
        self.z_copies = [None] * 3

    def plan_y(self, sources):
        self.y_copies = [
            self.links.copy(src, self.y_recv.at[i], self.y_peer) for i, src in enumerate(sources)
        ]

    def plan_z(self, first=None, third=None):
        own, to = self.own, self.z_recv
        self.z_copies = [
            self.links.copy(own.at[0] if first is None else first, to.at[0], self.near),
            self.links.copy(own.at[1], to.at[2], self.across),
            self.links.copy(own.at[2] if third is None else third, to.at[1], self.near),
        ]

    def add(self, i, other):
        self.own[i] = (self.own[i].astype(f32) + other.astype(f32)).astype(bf16)

    def take_y(self, i):
        self.y_copies[i].wait_recv()
        self.add(i, self.y_recv[i])
        if i == 0 or i == 2:
            self.z_copies[i].start()

    def take_near(self):
        self.z_copies[0].wait_recv()
        self.add(1, self.z_recv[0])
        self.z_copies[1].start()

    def total(self):
        self.z_copies[2].wait_recv()
        self.z_copies[1].wait_recv()
        return self.own[3].astype(f32) + self.z_recv[1].astype(f32) + self.z_recv[2].astype(f32)

    def wait_send(self, with_y=True):
        for copy in (self.y_copies if with_y else []) + self.z_copies:
            copy.wait_send()


class LastHalvings:
    def __init__(self, links, halving, own, y_recv, z_recv, sources):
        self.own, self.y_recv, self.z_recv = own, y_recv, z_recv
        self.y_copies = [
            links.copy(src, y_recv.at[i], halving.y_peer) for i, src in enumerate(sources)
        ]
        self.across = links.copy(own.at[0], z_recv.at[0], halving.across)

    def take_y(self, i):
        self.y_copies[i].wait_recv()
        self.own[i] = (self.own[i].astype(f32) + self.y_recv[i].astype(f32)).astype(bf16)
        if i == 0:
            self.across.start()

    def total(self):
        self.across.wait_recv()
        return self.own[1].astype(f32) + self.z_recv[0].astype(f32)

    def wait_send(self):
        for copy in self.y_copies + [self.across]:
            copy.wait_send()


def back_kernel(
    exchange,
    buckets,
    grad_attn_own,
    tokens,
    small,
    grad_h1,
    qkv,
    mixed,
    lse,
    w_query,
    w_key,
    w_value,
    w_out,
    gain_ff_part,
    first,
    normed_in,
    down_in,
    gate_in,
    up_in,
    grad_input,
    stats_out,
    attn_out,
    gate_out,
    up_out,
    down_out,
    grad_attn,
    normed,
    strip,
    strip_grad,
    key_head,
    value_head,
    grad_mixed,
    query_sum,
    key_sum,
    value_sum,
    grad_qkv,
    own_terms,
    tx,
    rx,
    down_own,
    down_z,
    gate_own,
    gate_y,
    gate_z,
    up_own,
    up_y,
    up_z,
    attn_own,
    attn_send,
    attn_y,
    attn_z,
    stats,
    stats_recv,
    send,
    recv,
    local,
):
    group = Group()
    me, core, far, diag = group.me, group.core, group.far, group.diag
    rows, width = grad_h1.shape
    half = rows // 2
    length = 4 * rows
    part = width // 4
    heads = strip.shape[0]
    span = 2 * length
    links = Links(send, recv)
    dp = group.dp
    peers = [group.at(core), group.at(far)]
    copies = []

    def load(src, dst):
        copy = pltpu.make_async_copy(src, dst, local.at[len(copies)])
        copies.append(copy)
        return copy

    save_normed = load(normed_in, normed)
    save_normed.start()
    if exchange:
        z, y = dp // 2, lax.rem(dp, 2)
        order = z_order(z)
        sums = [
            Halving(links, dp, me, own, y_recv, z_recv)
            for own, y_recv, z_recv in (
                (down_own, None, down_z),
                (up_own, up_y, up_z),
                (attn_own, attn_y, attn_z),
            )
        ]
        down, up, attn = sums
        peers += [down.y_peer, down.near, down.across]
        loads = [load(down_in.at[i], down_own.at[i]) for i in (1, 3)]
        gate_loads = [load(gate_in.at[i, y], gate_own.at[i]) for i in range(2)]
        up_loads = [load(up_in.at[i, y], up_own.at[i]) for i in range(4)]
        for copy in loads + gate_loads + up_loads:
            copy.start()
        down.plan_z(down_in.at[0], down_in.at[2])
        gate = LastHalvings(links, down, gate_own, gate_y, gate_z, [gate_in.at[i, 1 - y] for i in range(2)])
        up.plan_y([up_in.at[i, 1 - y] for i in range(4)])
        up.plan_z()
        attn.plan_y([attn_send.at[i] for i in range(4)])
        attn.plan_z()
    else:
        order = [0, 1, 2, 3]
    grad_attn[block_rows(me, rows), :] = grad_attn_own[...]
    greet(peers)
    gather = Gather(links, group, grad_attn, rows, 2)
    gather.start()
    if exchange:
        for copy in gate.y_copies:
            copy.start()
        down.z_copies[0].start()
        down.z_copies[2].start()
    scatter = Scatter(links, group, tx, rx, rows, 1)
    stages = []
    for i, to in enumerate([group.at(core), group.at(far)] + peers[2:]):
        stages.append(links.copy(stats.at[i], stats_recv.at[i], to))

    build_strips(strip, small, buckets)
    strip_grad[...] = jnp.zeros_like(strip_grad)
    query_sum[...] = jnp.zeros_like(query_sum)
    key_sum[...] = jnp.zeros_like(key_sum)
    value_sum[...] = jnp.zeros_like(value_sum)

    def mix_back(dev):
        at = block_rows(dev, rows)
        grad_mixed[at, :] = contract_cols(grad_attn[at, :], w_out[...]).astype(bf16)

    mix_back(me)
    gather.near.wait_recv()
    mix_back(core)

    def attend_back(dev, h):
        at = block_rows(dev, rows)
        seen = visible_pairs(dev, rows, length, first[0])
        query, grad = qkv[0, at, :], grad_mixed[at, :]
        lanes = head_lanes(query.shape, h)
        zero = jnp.zeros_like(query)
        scores = contract_cols(query, key_head[...])
        scores = jnp.where(seen, add_bias(scores, strip, h, dev, length), masked_score)
        probs = jnp.exp(scores - lse[at, h : h + 1])
        inner = contract_cols(grad, value_head[...])
        center = jnp.sum(probs * inner, axis=-1, keepdims=True)
        score_grad = (probs * (inner - center)).astype(bf16)
        query_sum[at, :] += mm(score_grad, key_head[...])
        key_sum[...] += contract_rows(score_grad, jnp.where(lanes, query, zero))
        value_sum[...] += contract_rows(probs.astype(bf16), jnp.where(lanes, grad, zero))
        count = length // 128
        for i in range(rows // 128):
            start = (count - 1 - i) * 128 - dev * rows
            to = pl.ds(pl.multiple_of(start, 128), length)
            strip_grad[h, :, to] += score_grad[i * 128 : (i + 1) * 128].astype(f32)

    def head_keys(h):
        key, value = qkv[1], qkv[2]
        lanes = head_lanes(key.shape, h)
        key_head[...] = jnp.where(lanes, key, jnp.zeros_like(key))
        value_head[...] = jnp.where(lanes, value, jnp.zeros_like(value))

    def take_gate(i):
        gate_loads[i].wait()
        gate.take_y(i)
        if i == 0:
            up.y_copies[0].start()
            up.y_copies[1].start()
        if i == 1:
            up.y_copies[2].start()
            up.y_copies[3].start()

    def take_up(i):
        up_loads[i].wait()
        up.take_y(i)

    def down_near():
        loads[0].wait()
        loads[1].wait()
        down.take_near()

    def down_total():
        down_out[...] = down.total()

    def gate_total():
        gate_out[...] = gate.total()

    def up_total():
        up_out[...] = up.total()

    head_keys(0)
    if exchange:
        take_gate(0)
    gather.forward(0)
    gather.forward(1)
    mix_back(far)
    for copy in gather.passed:
        copy.wait_recv()
    mix_back(diag)
    between = {
        (0, 1): [lambda: take_gate(1), down_near],
        (1, 1): [lambda: take_up(0)],
        (2, 0): [down_total],
        (2, 1): [lambda: take_up(1)],
        (2, 3): [gate_total],
    } if exchange else {}
    for h in range(heads):
        if h:
            head_keys(h)
        for j, dev in enumerate((diag, far, core, me)):
            attend_back(dev, h)
            for step in between.get((h, j), []):
                step()

    grad_qkv[0] = query_sum[...].astype(bf16)
    grad_qkv[1] = key_sum[...].astype(bf16)
    grad_qkv[2] = value_sum[...].astype(bf16)

    def terms(dev):
        at = block_rows(dev, rows)
        return (
            mm(grad_qkv[0, at, :], w_query[...])
            + mm(grad_qkv[1, at, :], w_key[...])
            + mm(grad_qkv[2, at, :], w_value[...])
        )

    scatter.send_diag(0, terms(diag))
    scatter.send_near(terms(core))
    scatter.send_far(0, terms(far))
    own_terms[...] = terms(me)
    save_normed.wait()

    cols = mixed.shape[1]
    for i in range(4):
        at = pl.ds(pl.multiple_of(order[i] * part, 128), part)
        for m in range(4):
            if m < 3:
                block = contract_rows(normed[:, at], grad_qkv[m]).astype(bf16)
            else:
                block = contract_rows(grad_attn[:, at], mixed[...]).astype(bf16)
            if exchange:
                low, high = block[: part // 2], block[part // 2 :]
                lanes = slice(m * cols, (m + 1) * cols)
                attn_send[i, :, lanes] = jnp.where(y == 0, high, low)
                attn_own[i, :, lanes] = jnp.where(y == 0, low, high)
            else:
                attn_out[m, at, :] = block
        if exchange:
            attn.y_copies[i].start()

    index = small[2:3, :]
    lines = []
    for h in range(heads):
        fold = strip_grad[h]
        count = 128
        while count > 1:
            count //= 2
            fold = fold[:count] + pltpu.roll(fold[count:], span - count, 1)
        lines.append(pltpu.roll(fold, 127, 1))
    diagonals = jnp.concatenate(lines + [jnp.zeros((8 - heads, span), f32)], axis=0)
    onehot = (lax.broadcasted_iota(jnp.int32, (buckets, span), 0).astype(f32) == index).astype(f32)
    table_part = lax.dot_general(
        diagonals, onehot, (((1,), (1,)), ((), ())), precision=highest, preferred_element_type=f32
    )
    if exchange:
        take_up(2)
        up.take_near()

    value = tokens[...].astype(f32)
    pulled, gain_part = norm_pull(value, small[0:1, 0:width], scatter.total(own_terms[...]))
    grad_input[...] = grad_h1[...] + pulled
    stats[0] = jnp.zeros_like(stats[0])
    stats[0, 0:1, :] = gain_part
    stats[0, 1:2, :] = gain_ff_part[...]
    stages[0].start()

    def next_stage(i):
        stages[i].wait_recv()
        total = stats[i] + stats_recv[i]
        to = stats.at[i + 1] if i + 1 < len(stages) else stats_out
        to[...] = total
        if i == 1:
            to[2 : 2 + heads, 0:buckets] = table_part[0:heads]
        if i + 1 < len(stages):
            stages[i + 1].start()

    next_stage(0)
    if exchange:
        take_up(3)
    next_stage(1)
    if exchange:
        attn.take_y(0)
        attn.take_y(1)
        attn.take_near()
        attn.take_y(2)
        up_total()
        attn.take_y(3)
        next_stage(2)
        next_stage(3)
        total = attn.total()
        for m in range(3):
            attn_out[m] = total[:, m * cols : (m + 1) * cols]
        attn_out[3] = total[:, 3 * cols :].T
        next_stage(4)
        down.wait_send(with_y=False)
        gate.wait_send()
        up.wait_send()
        attn.wait_send()
    gather.wait_send()
    scatter.wait_send()
    for stage in stages:
        stage.wait_send()


def attention_backward(
    exchange, table_shape, grad_attn, tokens, small, grad_h1, qkv, mixed, lse, w_query, w_key, w_value, w_out,
    gain_ff_part, first, normed, down_in, gate_in, up_in,
):
    rows, width = grad_h1.shape
    length = 4 * rows
    cols = w_query.shape[0]
    ff = down_in.shape[-1]
    buckets, heads = table_shape
    part = width // 8
    shape = jax.ShapeDtypeStruct
    scratch = [
        pltpu.VMEM((length, width), bf16),
        pltpu.VMEM((length, width), bf16),
        pltpu.VMEM((heads, 128, 2 * length), f32),
        pltpu.VMEM((heads, 128, 2 * length), f32),
        pltpu.VMEM((length, cols), bf16),
        pltpu.VMEM((length, cols), bf16),
        pltpu.VMEM((length, cols), bf16),
        pltpu.VMEM((length, cols), f32),
        pltpu.VMEM((length, cols), f32),
        pltpu.VMEM((length, cols), f32),
        pltpu.VMEM((3, length, cols), bf16),
        pltpu.VMEM((rows, width), f32),
        pltpu.VMEM((3, rows, width), bf16),
        pltpu.VMEM((3, rows, width), bf16),
    ]
    for count in (4, 3, 2, 2, 1, 4, 4, 3):
        scratch.append(pltpu.VMEM((count, part, ff) if exchange else (8, 128), bf16))
    for count in (4, 4, 4, 3):
        scratch.append(pltpu.VMEM((count, part, 4 * cols) if exchange else (8, 128), bf16))
    stages = 5 if exchange else 2
    scratch += [
        pltpu.VMEM((stages, 8, width), f32),
        pltpu.VMEM((stages, 8, width), f32),
        pltpu.SemaphoreType.DMA((40,)),
        pltpu.SemaphoreType.DMA((40,)),
        pltpu.SemaphoreType.DMA((12,)),
    ]
    ff_out = shape((part, ff) if exchange else (8, 128), f32)
    return pl.pallas_call(
        functools.partial(back_kernel, exchange, buckets),
        out_shape=(
            shape((rows, width), f32),
            shape((8, width), f32),
            shape((4, part, cols), f32) if exchange else shape((4, width, cols), bf16),
            ff_out,
            ff_out,
            ff_out,
        ),
        in_specs=[in_vmem()] * 12 + [in_smem()] + [anywhere()] * 4,
        out_specs=[in_vmem()] * 6,
        scratch_shapes=scratch,
        compiler_params=pltpu.CompilerParams(
            collective_id=1, has_side_effects=True, vmem_limit_bytes=VMEM_BYTES
        ),
    )(
        grad_attn, tokens, small, grad_h1, qkv, mixed, lse, w_query, w_key, w_value, w_out, gain_ff_part, first,
        normed, down_in, gate_in, up_in,
    )


def finish_kernel(heads, *refs):
    ins, outs, (attn_held, *held, load, save) = refs[:7], refs[7:19], refs[19:]
    stats, attn = ins[0], ins[1]
    sources = list(ins[2:]) + [attn.at[i] for i in range(4)]
    slots = held + [attn_held.at[i] for i in range(4)]
    targets = list(outs[4:9]) + list(outs[:4])
    loads = [pltpu.make_async_copy(a, b, load.at[i]) for i, (a, b) in enumerate(zip(sources, slots))]
    saves = [pltpu.make_async_copy(a, b, save.at[i]) for i, (a, b) in enumerate(zip(slots, targets))]
    for copy in loads:
        copy.start()
    gain_attn, gain_ff, table = outs[9:]
    gain_attn[...] = stats[0]
    gain_ff[...] = stats[1]
    table[...] = stats[2 : 2 + heads, 0 : table.shape[1]]
    for before, after in zip(loads, saves):
        before.wait()
        after.start()
    for copy in saves:
        copy.wait()


def finish(table_shape, stats, attn, *whole):
    buckets, heads = table_shape
    shape = jax.ShapeDtypeStruct
    outs = [shape(attn.shape[1:], f32)] * 4 + [shape(v.shape, v.dtype) for v in whole]
    small = [shape(stats.shape[1:], f32)] * 2 + [shape((heads, buckets), f32)]
    return pl.pallas_call(
        functools.partial(finish_kernel, heads),
        out_shape=outs + small,
        in_specs=[in_vmem()] + [anywhere()] * 6,
        out_specs=[anywhere()] * 9 + [in_vmem()] * 3,
        scratch_shapes=[pltpu.VMEM(v.shape, v.dtype) for v in (attn, *whole)]
        + [pltpu.SemaphoreType.DMA((9,))] * 2,
        compiler_params=pltpu.CompilerParams(vmem_limit_bytes=VMEM_BYTES),
    )(stats, attn, *whole)


def shards(
    tokens,
    gain_attn,
    w_query,
    w_key,
    w_value,
    w_out,
    bias_table,
    gain_ff,
    w_gate,
    w_up,
    w_down,
    cotangent,
    first_length,
    offset_bucket,
):
    n_dp = lax.axis_size("dp")
    exchange = n_dp == 8
    buckets, heads = bias_table.shape
    width = tokens.shape[1]
    small = pack_small(gain_attn, gain_ff, offset_bucket, bias_table)
    turned = [w_query.T, w_key.T, w_value.T]
    qkv, mixed, lse, output, grad_h1, grad_attn, gain_ff_part, normed, down, gate, up = forward(
        exchange, bias_table.shape, tokens, small, first_length, *turned, w_out, w_gate.T, w_up.T, w_down, cotangent
    )
    grad_input, stats, attn, gate_sum, up_sum, down_sum = attention_backward(
        exchange, bias_table.shape, grad_attn, tokens, small, grad_h1, qkv, mixed, lse, *turned, w_out, gain_ff_part,
        first_length, normed, down, gate, up,
    )
    if exchange:
        *attn, output, grad_input, gate_sum, up_sum, down_sum, gain_first, gain_second, table = finish(
            bias_table.shape, stats, attn, output, grad_input, gate_sum, up_sum, down_sum
        )
    else:
        def scatter(value):
            value = value.reshape(width, -1).astype(f32)
            return lax.psum_scatter(value, "dp", scatter_dimension=0, tiled=True)

        stats = lax.psum(stats, "dp")
        gate_sum, up_sum, down_sum = scatter(gate), scatter(up), scatter(down)
        attn = [scatter(attn[i]) for i in range(4)]
        attn[3] = attn[3].T
        gain_first, gain_second, table = stats[0], stats[1], stats[2 : 2 + heads, :buckets]
    return (
        output,
        grad_input,
        gain_first,
        attn[0],
        attn[1],
        attn[2],
        attn[3],
        table.T,
        gain_second,
        gate_sum,
        up_sum,
        down_sum.T,
    )


def solution(mesh):
    placed = (
        P(("dp", "mp"), None),
        P(),
        P(None, "mp"),
        P(None, "mp"),
        P(None, "mp"),
        P("mp", None),
        P(None, "mp"),
        P(),
        P(None, "mp"),
        P(None, "mp"),
        P("mp", None),
        P(("dp", "mp"), None),
        P("dp"),
        P(),
    )
    return jax.shard_map(
        shards,
        mesh=mesh,
        in_specs=placed,
        out_specs=(
            P(("dp", "mp"), None),
            P(("dp", "mp"), None),
            P(),
            P("dp", "mp"),
            P("dp", "mp"),
            P("dp", "mp"),
            P("mp", "dp"),
            P(None, "mp"),
            P(),
            P("dp", "mp"),
            P("dp", "mp"),
            P("mp", "dp"),
        ),
        check_vma=False,
    )
```

```python
import functools

import jax
import jax.numpy as jnp
from jax import lax
from jax.experimental import pallas as pl
from jax.experimental.pallas import tpu as pltpu
from jax.sharding import PartitionSpec as P

MESH = pl.DeviceIdType.MESH
DH = 64
epsilon = 1e-06
masked_score = -1000000000.0
highest = lax.Precision.HIGHEST
bf16 = jnp.bfloat16
f32 = jnp.float32
VMEM_BYTES = 62 * 2**20


def mm(left, right):
    return jnp.dot(left, right, preferred_element_type=f32)


def contract_rows(left, right):
    return lax.dot_general(left, right, (((0,), (0,)), ((), ())), preferred_element_type=f32)


def contract_cols(left, right):
    return lax.dot_general(left, right, (((1,), (1,)), ((), ())), preferred_element_type=f32)


def rms(values):
    return values * lax.rsqrt(jnp.mean(values * values, axis=-1, keepdims=True) + epsilon)


class Links:
    def __init__(self, send, recv):
        self.send, self.recv, self.used = send, recv, 0

    def copy(self, src, dst, to):
        at = self.used
        self.used += 1
        return pltpu.make_async_remote_copy(
            src_ref=src,
            dst_ref=dst,
            send_sem=self.send.at[at],
            recv_sem=self.recv.at[at],
            device_id=to,
            device_id_type=MESH,
        )


class Group:
    def __init__(self):
        self.dp, self.me = lax.axis_index("dp"), lax.axis_index("mp")
        self.core = self.me + 1 - 2 * lax.rem(self.me, 2)
        self.far = lax.rem(self.me + 2, 4)
        self.diag = 3 - self.me

    def at(self, mp):
        return (self.dp, mp)


def greet(peers):
    barrier = pltpu.get_barrier_semaphore()
    for peer in peers:
        pl.semaphore_signal(barrier, inc=1, device_id=peer, device_id_type=MESH)
    pl.semaphore_wait(barrier, len(peers))


def block_rows(dev, rows, start=0, size=None):
    return pl.ds(pl.multiple_of(dev * rows + start, 16), rows if size is None else size)


class Gather:
    def __init__(self, links, group, full, rows, chunks, source=None):
        size = rows // chunks
        own = block_rows(group.me, rows)
        self.near = links.copy(full.at[own] if source is None else source, full.at[own], group.at(group.core))
        self.far, self.passed = [], []
        for i in range(chunks):
            mine = block_rows(group.me, rows, i * size, size)
            theirs = block_rows(group.far, rows, i * size, size)
            src = full.at[mine] if source is None else source.at[pl.ds(i * size, size)]
            self.far.append(links.copy(src, full.at[mine], group.at(group.far)))
            self.passed.append(links.copy(full.at[theirs], full.at[theirs], group.at(group.core)))

    def start(self):
        self.near.start()
        for copy in self.far:
            copy.start()

    def forward(self, i):
        self.far[i].wait_recv()
        self.passed[i].start()

    def wait_send(self):
        self.near.wait_send()
        for copy in self.far + self.passed:
            copy.wait_send()


def pack_small(gain_attn, gain_ff, offset_bucket, table):
    width = offset_bucket.shape[0] + 1

    def row(values, fill=0.0):
        values = values.astype(f32).reshape(-1, values.shape[-1])
        return jnp.pad(values, ((0, 0), (0, width - values.shape[1])), constant_values=fill)

    return jnp.concatenate([row(gain_attn), row(gain_ff), row(offset_bucket, -1.0), row(table.T)])


def build_strips(strip, small, buckets):
    index = small[2:3, :]
    heads, _, width = strip.shape
    for h in range(heads):
        row = jnp.zeros(index.shape, f32)
        for b in range(buckets):
            row = jnp.where(index == float(b), small[3 + h : 4 + h, b : b + 1], row)
        strip[h] = pltpu.roll(
            jnp.broadcast_to(row, (128, width)), width - 127, 1, stride=1, stride_axis=0
        )


def add_bias(scores, strip, h, dev, length):
    parts = []
    count = length // 128
    for i in range(scores.shape[0] // 128):
        first = (count - 1 - i) * 128 - dev * scores.shape[0]
        parts.append(
            scores[i * 128 : (i + 1) * 128]
            + strip[h, :, pl.ds(pl.multiple_of(first, 128), length)]
        )
    return jnp.concatenate(parts, axis=0)


def visible_pairs(dev, rows, length, first):
    query = lax.broadcasted_iota(jnp.int32, (rows, length), 0) + dev * rows >= first
    key = lax.broadcasted_iota(jnp.int32, (rows, length), 1) >= first
    return query == key


def head_lanes(shape, h):
    lane = lax.broadcasted_iota(jnp.int32, shape, len(shape) - 1)
    return (lane >= h * DH) & (lane < (h + 1) * DH)


def norm_pull(values, gain, grad):
    inverse = lax.rsqrt(jnp.mean(values * values, axis=-1, keepdims=True) + epsilon)
    scaled = grad * gain
    along = jnp.mean(values * scaled, axis=-1, keepdims=True)
    gain_grad = jnp.sum(grad * values * inverse, axis=0, keepdims=True)
    return inverse * scaled - values * (along * inverse * inverse * inverse), gain_grad


class Scatter:
    def __init__(self, links, group, tx, rx, rows, parts):
        self.tx, self.rx, self.size = tx, rx, rows // parts
        core, far = group.at(group.core), group.at(group.far)
        self.near = links.copy(tx.at[2], rx.at[2], core)
        self.diag, self.far = [], []
        for i in range(parts):
            at = pl.ds(i * self.size, self.size)
            self.diag.append(links.copy(tx.at[0, at], rx.at[0, at], core))
            self.far.append(links.copy(tx.at[1, at], rx.at[1, at], far))

    def send_diag(self, i, terms):
        self.tx[0, pl.ds(i * self.size, self.size), :] = terms.astype(bf16)
        self.diag[i].start()

    def send_near(self, terms):
        self.tx[2] = terms.astype(bf16)
        self.near.start()

    def send_far(self, i, terms):
        at = pl.ds(i * self.size, self.size)
        self.diag[i].wait_recv()
        self.tx[1, at, :] = (terms + self.rx[0, at, :].astype(f32)).astype(bf16)
        self.far[i].start()

    def total(self, own):
        self.near.wait_recv()
        for copy in self.far:
            copy.wait_recv()
        return own + self.rx[2].astype(f32) + self.rx[1].astype(f32)

    def wait_send(self):
        for copy in [self.near] + self.diag + self.far:
            copy.wait_send()


GELU_SLOPE = 0.7978845608028654
GELU_CUBE = 0.044715


def z_order(z):
    near = z + 1 - 2 * lax.rem(z, 2)
    return [lax.rem(near + 2, 4), lax.rem(z + 2, 4), near, z]


def line_order(z):
    return [
        jnp.where(z < 2, 3, 0),
        jnp.where(z < 2, 2, 1),
        jnp.where(z == 0, 1, jnp.where(z == 1, 0, jnp.where(z == 2, 3, 2))),
        z,
    ]


def forward_kernel(
    exchange,
    buckets,
    tokens,
    small,
    first,
    w_query,
    w_key,
    w_value,
    w_out,
    gate_w,
    up_w,
    down_w,
    cot_in,
    qkv,
    mixed,
    lse,
    ff_far,
    own_terms,
    grad_h1,
    grad_mixed,
    out_grad,
    gain_grad,
    normed_out,
    down_out,
    gate_out,
    up_out,
    normed,
    cot,
    wg,
    wu,
    wd,
    strip,
    hidden,
    gate_act,
    up_act,
    mixed_all,
    mixed_sum,
    far_terms,
    tx,
    rx,
    tx_ff,
    rx_ff,
    down_grad,
    gate_grad,
    up_grad,
    y_recv,
    z_recv,
    send,
    recv,
    local,
    free,
):
    group = Group()
    me, core, far, diag = group.me, group.core, group.far, group.diag
    rows, width = tokens.shape
    half = rows // 2
    length = 4 * rows
    heads = strip.shape[0]
    depth = w_out.shape[0]
    ff = wg.shape[0]
    part = width // 4
    gain_attn, gain_ff = small[0:1, 0:width], small[1:2, 0:width]
    links = Links(send, recv)
    peers = [group.at(core), group.at(far), group.at(diag)]
    z_peers = []
    if exchange:
        z, y = group.dp // 2, lax.rem(group.dp, 2)
        line, order = line_order(z), z_order(z)
        y_peer = (2 * z + 1 - y, me)
        near_peer = (2 * order[2] + y, me)
        z_peers = [(2 * lax.rem(z + t, 4) + y, me) for t in (1, 2, 3)]
        peers += [y_peer] + z_peers
    else:
        line, order, y = [0, 1, 2, 3], [0, 1, 2, 3], 0

    def place(order, t):
        found = jnp.int32(order[3])
        for i in range(3):
            found = jnp.where(t == i, order[i], found)
        return found

    started = []

    def load(src, dst):
        copy = pltpu.make_async_copy(src, dst, local.at[len(started)])
        started.append(copy)
        return copy

    def depth_rows(i):
        return pl.ds(pl.multiple_of(i * depth, 16), depth)

    own = block_rows(me, rows)
    out_own = load(w_out, wu.at[depth_rows(me)])
    out_own.start()
    proj_loads = [load(w, wg.at[depth_rows(i)]) for i, w in enumerate((w_query, w_key, w_value))]
    for copy in proj_loads:
        copy.start()
    cot_own = load(cot_in, cot.at[own])
    cot_own.start()
    down_load = load(down_w, wd)
    down_load.start()
    greet(peers)

    x = tokens[...].astype(f32)
    normed[own, :] = (rms(x) * gain_attn).astype(bf16)
    gather = Gather(links, group, normed, rows, 2)
    gather.start()
    out_own.wait()
    parts = 4 if exchange else 1
    piece = depth // parts

    def out_rows(dev):
        start = dev * depth + (z * piece if exchange else 0)
        return pl.ds(pl.multiple_of(start, 16), piece)

    out_near = links.copy(wu.at[depth_rows(me)], wu.at[depth_rows(me)], group.at(core))
    out_far = links.copy(wu.at[out_rows(me)], wu.at[out_rows(me)], group.at(far))
    out_near.start()
    out_z = [links.copy(wu.at[out_rows(far)], wu.at[out_rows(far)], peer) for peer in z_peers]
    out_pass = links.copy(wu.at[depth_rows(far)], wu.at[depth_rows(far)], group.at(core))
    cot_gather = Gather(links, group, cot, rows, 4, source=cot_in)
    cot_gather.near.start()
    mixed_near = links.copy(mixed.at[block_rows(core, rows)], mixed_all.at[me], group.at(core))
    mixed_far = links.copy(mixed.at[block_rows(far, rows)], mixed_all.at[me], group.at(far))
    mixed_diag = links.copy(mixed.at[block_rows(diag, rows)], mixed_all.at[me], group.at(diag))

    build_strips(strip, small, buckets)
    for copy in proj_loads:
        copy.wait()

    def project(dev):
        at = block_rows(dev, rows)
        block = normed[at, :]
        for i in range(3):
            qkv[i, at, :] = contract_cols(block, wg[i * depth : (i + 1) * depth, :]).astype(bf16)

    project(me)
    gather.near.wait_recv()
    project(core)
    gather.forward(0)
    gather.forward(1)
    out_far.start()
    cot_gather.far[0].start()
    project(far)
    for copy in gather.passed:
        copy.wait_recv()
    normed_save = load(normed, normed_out)
    normed_save.start()
    project(diag)
    gate_load = load(gate_w, wg)
    gate_load.start()

    def attend(dev):
        at = block_rows(dev, rows)
        seen = visible_pairs(dev, rows, length, first[0])
        mixed_sum[...] = jnp.zeros_like(mixed_sum)
        lse[at, :] = jnp.zeros((rows, 128), f32)

        def one_head(h, carry):
            query = qkv[0, at, :]
            lanes = head_lanes(query.shape, h)
            scores = contract_cols(jnp.where(lanes, query, jnp.zeros_like(query)), qkv[1])
            scores = jnp.where(seen, add_bias(scores, strip, h, dev, length), masked_score)
            top = jnp.max(scores, axis=-1, keepdims=True)
            expo = jnp.exp(scores - top)
            total = jnp.sum(expo, axis=-1, keepdims=True)
            weights = (expo * (1.0 / total)).astype(bf16)
            mixed_sum[...] = jnp.where(lanes, mm(weights, qkv[2]), mixed_sum[...])
            lane = lax.broadcasted_iota(jnp.int32, (rows, 128), 1)
            lse[at, :] = jnp.where(lane == h, top + jnp.log(total), lse[at, :])
            return carry

        lax.fori_loop(0, heads, one_head, 0)
        mixed[at, :] = mixed_sum[...].astype(bf16)

    attend(far)
    gather.wait_send()
    normed_save.wait()
    mixed_far.start()
    cot_gather.far[1].start()
    out_far.wait_recv()
    for copy in out_z:
        copy.start()
    attend(diag)
    mixed_diag.start()
    cot_gather.far[2].start()
    attend(core)
    mixed_near.start()
    cot_gather.far[3].start()
    for copy in out_z:
        copy.wait_recv()
    out_pass.start()
    cot_gather.forward(0)
    attend(me)
    mixed_all[me] = mixed[own, :]
    out_near.wait_recv()
    attn = mm(mixed_all[me], wu[depth_rows(me), :])
    mixed_near.wait_recv()
    attn = attn + mm(mixed_all[core], wu[depth_rows(core), :])
    mixed_far.wait_recv()
    attn = attn + mm(mixed_all[far], wu[depth_rows(far), :])
    mixed_diag.wait_recv()
    out_pass.wait_recv()
    attn = attn + mm(mixed_all[diag], wu[depth_rows(diag), :])
    residual = x + attn
    grad_h1[...] = residual
    normed[own, :] = (rms(residual) * gain_ff).astype(bf16)
    second = Gather(links, group, normed, rows, 2)
    second.near.start()
    for copy in second.far:
        copy.start()
    for copy in [out_near, out_far, out_pass] + out_z:
        copy.wait_send()
    up_load = load(up_w, wu)
    up_load.start()

    scatter = Scatter(links, group, tx, rx, rows, 2)
    ff_diag = links.copy(tx_ff.at[0], rx_ff.at[0], group.at(core))
    ff_near = links.copy(tx_ff.at[1], rx_ff.at[1], group.at(core))

    def pair(ref, start, after):
        return jnp.concatenate(
            [
                ref[pl.ds(pl.multiple_of(start, 128), half), :],
                ref[pl.ds(pl.multiple_of(after, 128), half), :],
            ],
            axis=0,
        )

    def keep(i, value):
        strip[i, :, 0:ff] = value[:half]
        strip[i, :, length : length + ff] = value[half:]

    def unit(start, after):
        block = pair(normed, start, after)
        keep(0, contract_cols(block, wg[...]))
        keep(1, contract_cols(block, wu[...]))
        keep(2, contract_cols(pair(cot, start, after), wd[...]))
        for offset, lane in ((start, 0), (after, length)):

            def act(i, carry):
                at = pl.ds(pl.multiple_of(i * 16, 16), 16)
                to = pl.ds(pl.multiple_of(offset + i * 16, 16), 16)
                v, u, g = (strip[k, at, lane : lane + ff] for k in range(3))
                square = v * v
                t = jnp.tanh(GELU_SLOPE * v * (1.0 + GELU_CUBE * square))
                lift = 0.5 * (1.0 + t)
                value = v * lift
                slope = lift + 0.5 * v * (1.0 - t * t) * (
                    GELU_SLOPE * (1.0 + 3.0 * GELU_CUBE * square)
                )
                hidden[to, :] = (value * u).astype(bf16)
                gate_act[to, :] = (g * u * slope).astype(bf16)
                up_act[to, :] = (g * value).astype(bf16)
                return carry

            lax.fori_loop(0, half // 16, act, 0)

    def terms(start, after):
        return mm(pair(gate_act, start, after), wg[...]) + mm(
            pair(up_act, start, after), wu[...]
        )

    def weight_block(order, left, right, store, t):
        at = pl.ds(pl.multiple_of(place(order, t) * part, 128), part)
        value = contract_rows(left[:, at], right[...]).astype(bf16)
        store(t, value[: part // 2], value[part // 2 :])

    def weight_blocks(order, left, right, store):
        def one(t, carry):
            weight_block(order, left, right, store, t)
            return carry

        lax.fori_loop(0, 4, one, 0)

    cot_own.wait()
    down_load.wait()
    gate_load.wait()
    up_load.wait()
    unit(me * rows, me * rows + half)
    cot_gather.forward(1)
    cot_gather.near.wait_recv()
    second.near.wait_recv()
    unit(core * rows, core * rows + half)
    second.forward(0)
    second.passed[0].wait_recv()
    for i in (0, 1):
        cot_gather.passed[i].wait_recv()
    unit(far * rows, diag * rows)
    both = terms(far * rows, diag * rows)
    scatter.send_diag(0, both[half:])
    far_terms[pl.ds(0, half), :] = both[:half]
    cot_gather.forward(2)
    cot_gather.forward(3)
    scatter.send_far(0, far_terms[pl.ds(0, half), :])
    second.forward(1)
    own_terms[...] = terms(me * rows, me * rows + half)
    for i in (2, 3):
        cot_gather.passed[i].wait_recv()
    second.passed[1].wait_recv()
    unit(far * rows + half, diag * rows + half)

    base = links.used
    links.used += 8

    def y_copy(t):
        return pltpu.make_async_remote_copy(
            src_ref=down_grad.at[t, 1 - y],
            dst_ref=y_recv.at[t],
            send_sem=send.at[base + t],
            recv_sem=recv.at[base + t],
            device_id=y_peer,
            device_id_type=MESH,
        )

    def z_copy(i, side):
        return pltpu.make_async_remote_copy(
            src_ref=gate_grad.at[2 * i, side],
            dst_ref=z_recv.at[i, side],
            send_sem=send.at[base + 4 + 2 * i + side],
            recv_sem=recv.at[base + 4 + 2 * i + side],
            device_id=near_peer,
            device_id_type=MESH,
        )

    spots = len(started) + 1

    def save(src, dst, at):
        return pltpu.make_async_copy(src, dst, local.at[spots + at])

    def store_down(t, low, high):
        down_grad[t, 0] = low
        down_grad[t, 1] = high
        if exchange:
            y_copy(t).start()
        else:
            save(down_grad.at[t], down_out.at[t], t).start()

    def store_gate(t, low, high):
        gate_grad[t, 0] = low
        gate_grad[t, 1] = high
        if exchange:

            if t % 2 == 0:
                z_copy(t // 2, 0).start()
                z_copy(t // 2, 1).start()
        else:
            save(gate_grad.at[t], gate_out.at[t], 4 + t).start()

    def store_up(t, low, high):
        slot = lax.rem(t, 2)

        @pl.when(t >= 2)
        def _():
            save(up_grad.at[slot], up_out.at[t - 2], 8 + t - 2).wait()

        up_grad[slot, 0] = low
        up_grad[slot, 1] = high
        save(up_grad.at[slot], up_out.at[t], 8 + t).start()

    def down_block(t):
        weight_block(line, cot, hidden, store_down, t)

    def gate_block(t):
        weight_block(order, normed, gate_act, store_gate, t)

    down_block(0)
    gate_block(0)
    both = terms(far * rows + half, diag * rows + half)
    scatter.send_diag(1, both[half:])
    far_terms[pl.ds(half, half), :] = both[:half]
    scatter.send_near(terms(core * rows, core * rows + half))
    scatter.send_far(1, far_terms[pl.ds(half, half), :])
    for block in (1, 2):
        down_block(block)
    gate_block(2)
    down_block(3)
    cot_gather.wait_send()
    for peer in (core, far):
        pl.semaphore_signal(free, inc=1, device_id=group.at(peer), device_id_type=MESH)
    gate_block(1)
    gate_block(3)

    def ff_terms(dev):
        return mm(hidden[block_rows(dev, rows), :], wd[...])

    tx_ff[0] = ff_terms(diag).astype(bf16)
    ff_diag.start()
    tx_ff[1] = ff_terms(core).astype(bf16)
    ff_near.start()
    own_part = ff_terms(far)
    ff_diag.wait_recv()
    ff_far[...] = (own_part + rx_ff[0].astype(f32)).astype(bf16)
    residual = grad_h1[...]
    own_part = residual + ff_terms(me)
    pulled, gain_part = norm_pull(residual, gain_ff, scatter.total(own_terms[...]))
    gain_grad[...] = gain_part
    grad = cot[own, :].astype(f32) + pulled
    grad_h1[...] = grad
    cot[own, :] = grad.astype(bf16)
    third = Gather(links, group, cot, rows, 2)
    pl.semaphore_wait(free, 2)
    third.start()
    scatter.wait_send()
    out_again = load(w_out, tx.at[0, 0:depth])
    out_again.start()
    ff_near.wait_recv()
    own_terms[...] = own_part + rx_ff[1].astype(f32)

    def mix_back(dev):
        at = block_rows(dev, rows)
        grad_mixed[at, :] = contract_cols(cot[at, :], tx[0, 0:depth, :]).astype(bf16)

    weight_blocks(line, normed, up_act, store_up)
    out_again.wait()
    mix_back(me)
    third.near.wait_recv()
    mix_back(core)
    third.forward(0)
    if exchange:

        def sum_down(t, carry):
            y_copy(t).wait_recv()
            down_grad[t, y] = (
                down_grad[t, y].astype(f32) + y_recv[t].astype(f32)
            ).astype(bf16)
            save(down_grad.at[t, y], down_out.at[t], t).start()
            return carry

        lax.fori_loop(0, 3, sum_down, 0)
    third.forward(1)
    mix_back(far)
    for copy in third.passed:
        copy.wait_recv()
    mix_back(diag)

    def store_out(t, low, high):
        out_grad[t, 0] = low
        out_grad[t, 1] = high

    weight_blocks(line, cot, mixed, store_out)
    if exchange:
        sum_down(3, 0)
        for i in range(2):
            for side in range(2):
                z_copy(i, side).wait_recv()
                kept = gate_grad.at[2 * i + 1, side]
                kept[...] = (kept[...].astype(f32) + z_recv[i, side].astype(f32)).astype(bf16)
                save(kept, gate_out.at[i, side], 4 + 2 * i + side).start()

    for t in range(4):
        if exchange:
            save(down_grad.at[t, y], down_out.at[t], t).wait()
            save(gate_grad.at[t // 2 * 2 + 1, t % 2], gate_out.at[t // 2, t % 2], 4 + t).wait()
            y_copy(t).wait_send()
            z_copy(t // 2, t % 2).wait_send()
        else:
            save(down_grad.at[t], down_out.at[t], t).wait()
            save(gate_grad.at[t], gate_out.at[t], 4 + t).wait()
        if t >= 2:
            save(up_grad.at[t % 2], up_out.at[t], 8 + t).wait()
    for copy in (mixed_near, mixed_far, mixed_diag):
        copy.wait_send()
    second.wait_send()
    third.wait_send()
    ff_diag.wait_send()
    ff_near.wait_send()


def in_vmem():
    return pl.BlockSpec(memory_space=pltpu.VMEM)


def anywhere():
    return pl.BlockSpec(memory_space=pl.ANY)


def in_smem():
    return pl.BlockSpec(memory_space=pltpu.SMEM)


def forward(exchange, table_shape, tokens, small, first, w_query, w_key, w_value, w_out, gate_w, up_w, down_w, cot):
    rows, width = tokens.shape
    length = 4 * rows
    cols = w_query.shape[0]
    ff = gate_w.shape[0]
    buckets, heads = table_shape
    part = width // 8
    shape = jax.ShapeDtypeStruct
    halves = (4, 2, part, ff)
    return pl.pallas_call(
        functools.partial(forward_kernel, exchange, buckets),
        out_shape=(
            shape((3, length, cols), bf16),
            shape((length, cols), bf16),
            shape((length, 128), f32),
            shape((rows, width), bf16),
            shape((rows, width), f32),
            shape((rows, width), f32),
            shape((length, cols), bf16),
            shape((4, 2, part, cols), bf16),
            shape((1, width), f32),
            shape((length, width), bf16),
            shape((4, part, ff) if exchange else halves, bf16),
            shape((2, 2, part, ff) if exchange else halves, bf16),
            shape(halves, bf16),
        ),
        in_specs=[in_vmem()] * 2 + [in_smem()] + [anywhere()] * 8,
        out_specs=[in_vmem()] * 9 + [anywhere()] * 4,
        scratch_shapes=[
            pltpu.VMEM((length, width), bf16),
            pltpu.VMEM((length, width), bf16),
            pltpu.VMEM((ff, width), bf16),
            pltpu.VMEM((ff, width), bf16),
            pltpu.VMEM((ff, width), bf16),
            pltpu.VMEM((heads, 128, 2 * length), f32),
            pltpu.VMEM((length, ff), bf16),
            pltpu.VMEM((length, ff), bf16),
            pltpu.VMEM((length, ff), bf16),
            pltpu.VMEM((4, rows, cols), bf16),
            pltpu.VMEM((rows, cols), f32),
            pltpu.VMEM((rows, width), f32),
            pltpu.VMEM((3, rows, width), bf16),
            pltpu.VMEM((3, rows, width), bf16),
            pltpu.VMEM((2, rows, width), bf16),
            pltpu.VMEM((2, rows, width), bf16),
            pltpu.VMEM(halves, bf16),
            pltpu.VMEM(halves, bf16),
            pltpu.VMEM((2, 2, part, ff), bf16),
            pltpu.VMEM((4, part, ff) if exchange else (8, 128), bf16),
            pltpu.VMEM((2, 2, part, ff) if exchange else (8, 128), bf16),
            pltpu.SemaphoreType.DMA((56,)),
            pltpu.SemaphoreType.DMA((56,)),
            pltpu.SemaphoreType.DMA((24,)),
            pltpu.SemaphoreType.REGULAR,
        ],
        compiler_params=pltpu.CompilerParams(
            collective_id=0, has_side_effects=True, vmem_limit_bytes=VMEM_BYTES
        ),
    )(tokens, small, first, w_query, w_key, w_value, w_out, gate_w, up_w, down_w, cot)


class Line:
    def __init__(self, links, dp, mp, own, y_recv, z_recv, sources=()):
        z, y = dp // 2, lax.rem(dp, 2)
        near = z + 1 - 2 * lax.rem(z, 2)
        self.own, self.y_recv, self.z_recv = own, y_recv, z_recv
        self.inner = (z == 1) | (z == 2)
        self.y_peer, self.near, self.across = (2 * z + 1 - y, mp), (2 * near + y, mp), (2 * lax.rem(z + 2, 4) + y, mp)
        self.middle = (2 * (3 - z) + y, mp)
        self.y_copies = [links.copy(src, y_recv.at[i], self.y_peer) for i, src in enumerate(sources)]
        base = links.used
        links.used += 5
        forth = jnp.where(self.inner, self.middle[0], self.near[0])
        step = jnp.where(self.inner, 3, 0)
        self.copies = [
            pltpu.make_async_remote_copy(
                src_ref=own.at[i],
                dst_ref=z_recv.at[slot],
                send_sem=links.send.at[base + i],
                recv_sem=links.recv.at[base + slot],
                device_id=(to, mp),
                device_id_type=MESH,
            )
            for i, (slot, to) in enumerate(((step, forth), (step + 1, forth), (2, self.near[0])))
        ]
        self.arrivals = [
            pltpu.make_async_remote_copy(
                src_ref=own.at[0],
                dst_ref=z_recv.at[slot],
                send_sem=links.send.at[base],
                recv_sem=links.recv.at[base + slot],
                device_id=self.near,
                device_id_type=MESH,
            )
            for slot in range(5)
        ]

    def add(self, i, other):
        self.own[i] = (self.own[i].astype(f32) + other.astype(f32)).astype(bf16)

    def begin(self, i):
        @pl.when(jnp.logical_not(self.inner))
        def _():
            self.copies[i].start()

    def take_y(self, i):
        self.y_copies[i].wait_recv()
        self.add(i, self.y_recv[i])
        if i < 3:
            self.begin(i)

    def relay(self, i):
        slot = (0, 1, 3)[i]

        @pl.when(self.inner)
        def _():
            self.arrivals[slot].wait_recv()
            self.add(i, self.z_recv[slot])
            self.copies[i].start()

    def total(self, out):
        self.arrivals[2].wait_recv()
        out[...] = self.own[3].astype(f32) + self.z_recv[2].astype(f32)

        @pl.when(self.inner)
        def _():
            self.arrivals[4].wait_recv()
            out[...] += self.z_recv[4].astype(f32)

    def wait_send(self):
        for copy in self.y_copies + self.copies:
            copy.wait_send()


class LastHalvings:
    def __init__(self, links, line, own, y_recv, z_recv, sources):
        self.own, self.y_recv, self.z_recv, self.inner = own, y_recv, z_recv, line.inner
        self.y_copies = [
            links.copy(src, y_recv.at[i], line.y_peer) for i, src in enumerate(sources)
        ]
        base = links.used
        links.used += 3

        def copy(i, src, slot, to):
            return pltpu.make_async_remote_copy(
                src_ref=src,
                dst_ref=z_recv.at[slot],
                send_sem=links.send.at[base + i],
                recv_sem=links.recv.at[base + slot],
                device_id=to,
                device_id_type=MESH,
            )

        mp = line.near[1]
        forth = (jnp.where(self.inner, line.middle[0], line.near[0]), mp)
        self.first = copy(0, own.at[0], jnp.where(self.inner, 1, 0), forth)
        self.inwards = copy(1, z_recv.at[0], 2, line.middle)
        self.outwards = copy(2, z_recv.at[1], 2, line.near)
        self.arrivals = [copy(0, own.at[0], slot, line.near) for slot in range(3)]

    def take_y(self, i):
        self.y_copies[i].wait_recv()
        self.own[i] = (self.own[i].astype(f32) + self.y_recv[i].astype(f32)).astype(bf16)
        if i == 0:
            self.first.start()

    def hand_on(self):
        @pl.when(self.inner)
        def _():
            self.arrivals[1].wait_recv()
            self.outwards.start()
            self.arrivals[0].wait_recv()
            self.inwards.start()

    def total(self):
        self.arrivals[2].wait_recv()
        return self.own[1].astype(f32) + self.z_recv[2].astype(f32)

    def wait_send(self):
        for copy in self.y_copies + [self.first]:
            copy.wait_send()

        @pl.when(self.inner)
        def _():
            self.outwards.wait_send()
            self.inwards.wait_send()


def back_kernel(
    exchange,
    buckets,
    tokens,
    small,
    grad_h1,
    qkv,
    mixed,
    lse,
    w_query,
    w_key,
    w_value,
    grad_mixed,
    out_grad,
    gain_ff_part,
    ff_base,
    first,
    normed_in,
    ff_far,
    down_in,
    gate_in,
    up_in,
    output,
    grad_input,
    stats_out,
    attn_out,
    gate_out,
    up_out,
    down_out,
    normed,
    strip,
    strip_grad,
    key_head,
    value_head,
    query_sum,
    key_sum,
    value_sum,
    grad_qkv,
    own_terms,
    tx,
    rx,
    down_own,
    down_z,
    gate_own,
    gate_y,
    gate_z,
    up_own,
    up_y,
    up_z,
    attn_own,
    attn_send,
    attn_y,
    attn_z,
    attn_sum,
    ff_recv,
    stats,
    stats_recv,
    send,
    recv,
    local,
):
    group = Group()
    me, core, far, diag = group.me, group.core, group.far, group.diag
    rows, width = grad_h1.shape
    half = rows // 2
    length = 4 * rows
    part = width // 4
    heads = strip.shape[0]
    span = 2 * length
    links = Links(send, recv)
    dp = group.dp
    peers = [group.at(core), group.at(far)]
    copies = []

    def load(src, dst):
        copy = pltpu.make_async_copy(src, dst, local.at[len(copies)])
        copies.append(copy)
        return copy

    save_normed = load(normed_in, normed)
    save_normed.start()
    if exchange:
        z, y = dp // 2, lax.rem(dp, 2)
        order = line_order(z)
        down = Line(links, dp, me, down_own, None, down_z)
        gate = LastHalvings(links, down, gate_own, gate_y, gate_z, [gate_in.at[i, 1 - y] for i in range(2)])
        up = Line(links, dp, me, up_own, up_y, up_z, [up_in.at[i, 1 - y] for i in range(4)])
        attn = Line(links, dp, me, attn_own, attn_y, attn_z, [attn_send.at[i] for i in range(4)])
        peers += [down.y_peer, down.near, down.across, down.middle]
        loads = [load(down_in.at[i], down_own.at[i]) for i in range(4)]
        gate_loads = [load(gate_in.at[i, y], gate_own.at[i]) for i in range(2)]
        up_loads = [load(up_in.at[i, y], up_own.at[i]) for i in range(4)]
        for copy in loads + gate_loads + up_loads:
            copy.start()
    else:
        order = [0, 1, 2, 3]
    greet(peers)
    if exchange:
        for copy in gate.y_copies + up.y_copies:
            copy.start()
        for i in range(4):
            loads[i].wait()
            if i < 3:
                down.begin(i)
    scatter = Scatter(links, group, tx, rx, rows, 1)
    ff_copy = links.copy(ff_far, ff_recv, group.at(far))
    ff_copy.start()
    stages = []
    for i, to in enumerate(peers[2:5] + peers[:2]):
        stages.append(links.copy(stats.at[i], stats_recv.at[i], to))

    build_strips(strip, small, buckets)
    strip_grad[...] = jnp.zeros_like(strip_grad)
    query_sum[...] = jnp.zeros_like(query_sum)
    key_sum[...] = jnp.zeros_like(key_sum)
    value_sum[...] = jnp.zeros_like(value_sum)

    def attend_back(dev, h):
        at = block_rows(dev, rows)
        seen = visible_pairs(dev, rows, length, first[0])
        query, grad = qkv[0, at, :], grad_mixed[at, :]
        lanes = head_lanes(query.shape, h)
        zero = jnp.zeros_like(query)
        scores = contract_cols(query, key_head[...])
        scores = jnp.where(seen, add_bias(scores, strip, h, dev, length), masked_score)
        probs = jnp.exp(scores - lse[at, h : h + 1])
        inner = contract_cols(grad, value_head[...])
        center = jnp.sum(probs * inner, axis=-1, keepdims=True)
        score_grad = (probs * (inner - center)).astype(bf16)
        query_sum[at, :] += mm(score_grad, key_head[...])
        key_sum[...] += contract_rows(score_grad, jnp.where(lanes, query, zero))
        value_sum[...] += contract_rows(probs.astype(bf16), jnp.where(lanes, grad, zero))
        count = length // 128
        for i in range(rows // 128):
            start = (count - 1 - i) * 128 - dev * rows
            to = pl.ds(pl.multiple_of(start, 128), length)
            strip_grad[h, :, to] += score_grad[i * 128 : (i + 1) * 128].astype(f32)

    def head_keys(h):
        key, value = qkv[1], qkv[2]
        lanes = head_lanes(key.shape, h)
        key_head[...] = jnp.where(lanes, key, jnp.zeros_like(key))
        value_head[...] = jnp.where(lanes, value, jnp.zeros_like(value))

    def take_gate(i):
        gate_loads[i].wait()
        gate.take_y(i)

    def take_up(i):
        up_loads[i].wait()
        up.take_y(i)

    def down_total():
        down.total(down_out)

    def gate_total():
        gate_out[...] = gate.total()

    head_keys(0)
    between = {
        (0, 1): [lambda: take_gate(0)],
        (0, 2): [lambda: down.relay(0)],
        (1, 2): [lambda: take_gate(1), lambda: down.relay(1)],
        (1, 3): [lambda: down.relay(2)],
        (2, 2): [lambda: take_up(0)],
    } if exchange else {}
    for h in range(heads):
        if h:
            head_keys(h)
        for j, dev in enumerate((diag, far, core, me)):
            attend_back(dev, h)
            for step in between.get((h, j), []):
                step()

    grad_qkv[0] = query_sum[...].astype(bf16)
    grad_qkv[1] = key_sum[...].astype(bf16)
    grad_qkv[2] = value_sum[...].astype(bf16)

    def terms(dev):
        at = block_rows(dev, rows)
        return (
            mm(grad_qkv[0, at, :], w_query[...])
            + mm(grad_qkv[1, at, :], w_key[...])
            + mm(grad_qkv[2, at, :], w_value[...])
        )

    gain_parts = []

    def gain_terms(dev):
        value = terms(dev)
        product = value * normed[block_rows(dev, rows), :].astype(f32)
        gain_parts.append(jnp.sum(product, axis=0, keepdims=True))
        return value

    save_normed.wait()
    scatter.send_diag(0, gain_terms(diag))
    scatter.send_near(gain_terms(core))
    scatter.send_far(0, gain_terms(far))
    own_terms[...] = gain_terms(me)

    index = small[2:3, :]
    lines = []
    for h in range(heads):
        fold = strip_grad[h]
        count = 128
        while count > 1:
            count //= 2
            fold = fold[:count] + pltpu.roll(fold[count:], span - count, 1)
        lines.append(pltpu.roll(fold, 127, 1))
    diagonals = jnp.concatenate(lines + [jnp.zeros((8 - heads, span), f32)], axis=0)
    onehot = (lax.broadcasted_iota(jnp.int32, (buckets, span), 0).astype(f32) == index).astype(f32)
    table_part = lax.dot_general(
        diagonals, onehot, (((1,), (1,)), ((), ())), precision=highest, preferred_element_type=f32
    )
    stats[0] = jnp.zeros_like(stats[0])
    stats[0, 0:1, :] = (gain_parts[0] + gain_parts[1] + gain_parts[2] + gain_parts[3]) / small[0:1, 0:width]
    stats[0, 1:2, :] = gain_ff_part[...]
    stats[0, 2 : 2 + heads, 0:buckets] = table_part[0:heads]
    stages[0].start()
    dp_stages = len(stages) - 2

    def next_stage(i):
        stages[i].wait_recv()
        total = stats[i] + stats_recv[i]
        if i >= dp_stages:
            row = lax.broadcasted_iota(jnp.int32, total.shape, 0)
            total = jnp.where(row < 2, total, stats[i])
        if i + 1 < len(stages):
            stats[i + 1] = total
            stages[i + 1].start()
        else:
            stats_out[...] = total

    cols = mixed.shape[1]
    for i in range(4):
        at = pl.ds(pl.multiple_of(order[i] * part, 128), part)
        for m in range(3):
            block = contract_rows(normed[:, at], grad_qkv[m]).astype(bf16)
            if exchange:
                low, high = block[: part // 2], block[part // 2 :]
                lanes = slice(m * cols, (m + 1) * cols)
                attn_send[i, :, lanes] = jnp.where(y == 0, high, low)
                attn_own[i, :, lanes] = jnp.where(y == 0, low, high)
            else:
                attn_out[m, at, :] = block
        if exchange:
            attn_send[i, :, 3 * cols :] = out_grad[i, 1 - y]
            attn_own[i, :, 3 * cols :] = out_grad[i, y]
            attn.y_copies[i].start()
        else:
            for side in range(2):
                attn_out[3, pl.ds(i * part + side * part // 2, part // 2), :] = out_grad[i, side]

    if exchange:
        take_up(1)
        down_total()
        gate.hand_on()
    ff_copy.wait_recv()
    output[...] = (ff_base[...] + ff_recv[...].astype(f32)).astype(bf16)
    if exchange:
        up.relay(0)
        take_up(2)
    pulled, _ = norm_pull(tokens[...].astype(f32), small[0:1, 0:width], scatter.total(own_terms[...]))
    grad_input[...] = grad_h1[...] + pulled
    if exchange:
        take_up(3)
        next_stage(0)
        up.relay(1)
        attn.take_y(0)
        gate_total()
        up.relay(2)
        next_stage(1)
        attn.take_y(1)
        attn.relay(0)
        next_stage(2)
        attn.take_y(2)
        up.total(up_out)
        attn.relay(1)
        next_stage(3)
        next_stage(4)
        attn.relay(2)
        attn.take_y(3)
        attn.total(attn_sum)
        for m in range(3):
            attn_out[m] = attn_sum[:, m * cols : (m + 1) * cols]
        attn_out[3] = attn_sum[:, 3 * cols :].T
        down.wait_send()
        gate.wait_send()
        up.wait_send()
        attn.wait_send()
    else:
        next_stage(0)
        next_stage(1)
    ff_copy.wait_send()
    scatter.wait_send()
    for stage in stages:
        stage.wait_send()


def attention_backward(
    exchange, table_shape, tokens, small, grad_h1, qkv, mixed, lse, w_query, w_key, w_value, grad_mixed, out_grad,
    gain_ff_part, ff_base, first, normed, ff_far, down_in, gate_in, up_in,
):
    rows, width = grad_h1.shape
    length = 4 * rows
    cols = w_query.shape[0]
    ff = down_in.shape[-1]
    buckets, heads = table_shape
    part = width // 8
    shape = jax.ShapeDtypeStruct
    scratch = [
        pltpu.VMEM((length, width), bf16),
        pltpu.VMEM((heads, 128, 2 * length), f32),
        pltpu.VMEM((heads, 128, 2 * length), f32),
        pltpu.VMEM((length, cols), bf16),
        pltpu.VMEM((length, cols), bf16),
        pltpu.VMEM((length, cols), f32),
        pltpu.VMEM((length, cols), f32),
        pltpu.VMEM((length, cols), f32),
        pltpu.VMEM((3, length, cols), bf16),
        pltpu.VMEM((rows, width), f32),
        pltpu.VMEM((3, rows, width), bf16),
        pltpu.VMEM((3, rows, width), bf16),
    ]
    for count in (4, 5, 2, 2, 3, 4, 4, 5):
        scratch.append(pltpu.VMEM((count, part, ff) if exchange else (8, 128), bf16))
    for count in (4, 4, 4, 5):
        scratch.append(pltpu.VMEM((count, part, 4 * cols) if exchange else (8, 128), bf16))
    stages = 5 if exchange else 2
    scratch += [
        pltpu.VMEM((part, 4 * cols), f32),
        pltpu.VMEM((rows, width), bf16),
        pltpu.VMEM((stages, 8, width), f32),
        pltpu.VMEM((stages, 8, width), f32),
        pltpu.SemaphoreType.DMA((48,)),
        pltpu.SemaphoreType.DMA((48,)),
        pltpu.SemaphoreType.DMA((16,)),
    ]
    ff_out = shape((part, ff) if exchange else (8, 128), f32)
    return pl.pallas_call(
        functools.partial(back_kernel, exchange, buckets),
        out_shape=(
            shape((rows, width), bf16),
            shape((rows, width), f32),
            shape((8, width), f32),
            shape((4, part, cols), f32) if exchange else shape((4, width, cols), bf16),
            ff_out,
            ff_out,
            ff_out,
        ),
        in_specs=[in_vmem()] * 13 + [in_smem()] + [anywhere()] * 5,
        out_specs=[in_vmem()] * 7,
        scratch_shapes=scratch,
        compiler_params=pltpu.CompilerParams(
            collective_id=1, has_side_effects=True, vmem_limit_bytes=VMEM_BYTES
        ),
    )(
        tokens, small, grad_h1, qkv, mixed, lse, w_query, w_key, w_value, grad_mixed, out_grad, gain_ff_part, ff_base,
        first, normed, ff_far, down_in, gate_in, up_in,
    )


def finish_kernel(heads, *refs):
    ins, outs, (attn_held, *held, load, save) = refs[:7], refs[7:19], refs[19:]
    stats, attn = ins[0], ins[1]
    sources = list(ins[2:]) + [attn.at[i] for i in range(4)]
    slots = held + [attn_held.at[i] for i in range(4)]
    targets = list(outs[4:9]) + list(outs[:4])
    loads = [pltpu.make_async_copy(a, b, load.at[i]) for i, (a, b) in enumerate(zip(sources, slots))]
    saves = [pltpu.make_async_copy(a, b, save.at[i]) for i, (a, b) in enumerate(zip(slots, targets))]
    for copy in loads:
        copy.start()
    gain_attn, gain_ff, table = outs[9:]
    gain_attn[...] = stats[0]
    gain_ff[...] = stats[1]
    table[...] = stats[2 : 2 + heads, 0 : table.shape[1]]
    for before, after in zip(loads, saves):
        before.wait()
        after.start()
    for copy in saves:
        copy.wait()


def finish(table_shape, stats, attn, *whole):
    buckets, heads = table_shape
    shape = jax.ShapeDtypeStruct
    outs = [shape(attn.shape[1:], f32)] * 4 + [shape(v.shape, v.dtype) for v in whole]
    small = [shape(stats.shape[1:], f32)] * 2 + [shape((heads, buckets), f32)]
    return pl.pallas_call(
        functools.partial(finish_kernel, heads),
        out_shape=outs + small,
        in_specs=[in_vmem()] + [anywhere()] * 6,
        out_specs=[anywhere()] * 9 + [in_vmem()] * 3,
        scratch_shapes=[pltpu.VMEM(v.shape, v.dtype) for v in (attn, *whole)]
        + [pltpu.SemaphoreType.DMA((9,))] * 2,
        compiler_params=pltpu.CompilerParams(vmem_limit_bytes=VMEM_BYTES),
    )(stats, attn, *whole)


def shards(
    tokens,
    gain_attn,
    w_query,
    w_key,
    w_value,
    w_out,
    bias_table,
    gain_ff,
    w_gate,
    w_up,
    w_down,
    cotangent,
    first_length,
    offset_bucket,
):
    n_dp = lax.axis_size("dp")
    exchange = n_dp == 8
    buckets, heads = bias_table.shape
    width = tokens.shape[1]
    small = pack_small(gain_attn, gain_ff, offset_bucket, bias_table)
    turned = [w_query.T, w_key.T, w_value.T]
    qkv, mixed, lse, ff_far, ff_base, grad_h1, grad_mixed, out_grad, gain_ff_part, normed, down, gate, up = forward(
        exchange, bias_table.shape, tokens, small, first_length, *turned, w_out, w_gate.T, w_up.T, w_down, cotangent
    )
    output, grad_input, stats, attn, gate_sum, up_sum, down_sum = attention_backward(
        exchange, bias_table.shape, tokens, small, grad_h1, qkv, mixed, lse, *turned, grad_mixed, out_grad, gain_ff_part,
        ff_base, first_length, normed, ff_far, down, gate, up,
    )
    if exchange:
        *attn, output, grad_input, gate_sum, up_sum, down_sum, gain_first, gain_second, table = finish(
            bias_table.shape, stats, attn, output, grad_input, gate_sum, up_sum, down_sum
        )
    else:
        def scatter(value):
            value = value.reshape(width, -1).astype(f32)
            return lax.psum_scatter(value, "dp", scatter_dimension=0, tiled=True)

        stats = lax.psum(stats, "dp")
        gate_sum, up_sum, down_sum = scatter(gate), scatter(up), scatter(down)
        attn = [scatter(attn[i]) for i in range(4)]
        attn[3] = attn[3].T
        gain_first, gain_second, table = stats[0], stats[1], stats[2 : 2 + heads, :buckets]
    return (
        output,
        grad_input,
        gain_first,
        attn[0],
        attn[1],
        attn[2],
        attn[3],
        table.T,
        gain_second,
        gate_sum,
        up_sum,
        down_sum.T,
    )


def solution(mesh):
    placed = (
        P(("dp", "mp"), None),
        P(),
        P(None, "mp"),
        P(None, "mp"),
        P(None, "mp"),
        P("mp", None),
        P(None, "mp"),
        P(),
        P(None, "mp"),
        P(None, "mp"),
        P("mp", None),
        P(("dp", "mp"), None),
        P("dp"),
        P(),
    )
    return jax.shard_map(
        shards,
        mesh=mesh,
        in_specs=placed,
        out_specs=(
            P(("dp", "mp"), None),
            P(("dp", "mp"), None),
            P(),
            P("dp", "mp"),
            P("dp", "mp"),
            P("dp", "mp"),
            P("mp", "dp"),
            P(None, "mp"),
            P(),
            P("dp", "mp"),
            P("dp", "mp"),
            P("mp", "dp"),
        ),
        check_vma=False,
    )
```

```python
import functools

import jax
import jax.numpy as jnp
from jax import lax
from jax.experimental import pallas as pl
from jax.experimental.pallas import tpu as pltpu
from jax.sharding import PartitionSpec as P

MESH = pl.DeviceIdType.MESH
DH = 64
epsilon = 1e-06
masked_score = -1000000000.0
highest = lax.Precision.HIGHEST
bf16 = jnp.bfloat16
f32 = jnp.float32
VMEM_BYTES = 62 * 2**20


def mm(left, right):
    return jnp.dot(left, right, preferred_element_type=f32)


def contract_rows(left, right):
    return lax.dot_general(left, right, (((0,), (0,)), ((), ())), preferred_element_type=f32)


def contract_cols(left, right):
    return lax.dot_general(left, right, (((1,), (1,)), ((), ())), preferred_element_type=f32)


def rms(values):
    return values * lax.rsqrt(jnp.mean(values * values, axis=-1, keepdims=True) + epsilon)


class Links:
    def __init__(self, send, recv):
        self.send, self.recv, self.used = send, recv, 0

    def copy(self, src, dst, to):
        at = self.used
        self.used += 1
        return pltpu.make_async_remote_copy(
            src_ref=src,
            dst_ref=dst,
            send_sem=self.send.at[at],
            recv_sem=self.recv.at[at],
            device_id=to,
            device_id_type=MESH,
        )


class Group:
    def __init__(self):
        self.dp, self.me = lax.axis_index("dp"), lax.axis_index("mp")
        self.core = self.me + 1 - 2 * lax.rem(self.me, 2)
        self.far = lax.rem(self.me + 2, 4)
        self.diag = 3 - self.me

    def at(self, mp):
        return (self.dp, mp)


def greet(peers):
    barrier = pltpu.get_barrier_semaphore()
    for peer in peers:
        pl.semaphore_signal(barrier, inc=1, device_id=peer, device_id_type=MESH)
    pl.semaphore_wait(barrier, len(peers))


def block_rows(dev, rows, start=0, size=None):
    return pl.ds(pl.multiple_of(dev * rows + start, 16), rows if size is None else size)


class Gather:
    def __init__(self, links, group, full, rows, chunks, source=None):
        size = rows // chunks
        own = block_rows(group.me, rows)
        self.near = links.copy(full.at[own] if source is None else source, full.at[own], group.at(group.core))
        self.far, self.passed = [], []
        for i in range(chunks):
            mine = block_rows(group.me, rows, i * size, size)
            theirs = block_rows(group.far, rows, i * size, size)
            src = full.at[mine] if source is None else source.at[pl.ds(i * size, size)]
            self.far.append(links.copy(src, full.at[mine], group.at(group.far)))
            self.passed.append(links.copy(full.at[theirs], full.at[theirs], group.at(group.core)))

    def start(self):
        self.near.start()
        for copy in self.far:
            copy.start()

    def forward(self, i):
        self.far[i].wait_recv()
        self.passed[i].start()

    def wait_send(self):
        self.near.wait_send()
        for copy in self.far + self.passed:
            copy.wait_send()


def pack_small(gain_attn, gain_ff, offset_bucket, table):
    width = offset_bucket.shape[0] + 1

    def row(values, fill=0.0):
        values = values.astype(f32).reshape(-1, values.shape[-1])
        return jnp.pad(values, ((0, 0), (0, width - values.shape[1])), constant_values=fill)

    return jnp.concatenate([row(gain_attn), row(gain_ff), row(offset_bucket, -1.0), row(table.T)])


def build_strips(strip, small, buckets):
    index = small[2:3, :]
    heads, _, width = strip.shape
    for h in range(heads):
        row = jnp.zeros(index.shape, f32)
        for b in range(buckets):
            row = jnp.where(index == float(b), small[3 + h : 4 + h, b : b + 1], row)
        strip[h] = pltpu.roll(
            jnp.broadcast_to(row, (128, width)), width - 127, 1, stride=1, stride_axis=0
        )


def add_bias(scores, strip, h, dev, length):
    parts = []
    count = length // 128
    for i in range(scores.shape[0] // 128):
        first = (count - 1 - i) * 128 - dev * scores.shape[0]
        parts.append(
            scores[i * 128 : (i + 1) * 128]
            + strip[h, :, pl.ds(pl.multiple_of(first, 128), length)]
        )
    return jnp.concatenate(parts, axis=0)


def visible_keys(dev, rows, length, first):
    key = lax.broadcasted_iota(jnp.int32, (1, length), 1)
    return (key >= first) == (dev * rows >= first)


def head_lanes(shape, h):
    lane = lax.broadcasted_iota(jnp.int32, shape, len(shape) - 1)
    return (lane >= h * DH) & (lane < (h + 1) * DH)


def norm_pull(values, gain, grad):
    inverse = lax.rsqrt(jnp.mean(values * values, axis=-1, keepdims=True) + epsilon)
    scaled = grad * gain
    along = jnp.mean(values * scaled, axis=-1, keepdims=True)
    gain_grad = jnp.sum(grad * values * inverse, axis=0, keepdims=True)
    return inverse * scaled - values * (along * inverse * inverse * inverse), gain_grad


class Scatter:
    def __init__(self, links, group, tx, rx, rows, parts):
        self.tx, self.rx, self.size = tx, rx, rows // parts
        core, far = group.at(group.core), group.at(group.far)
        self.near = links.copy(tx.at[2], rx.at[2], core)
        self.diag, self.far = [], []
        for i in range(parts):
            at = pl.ds(i * self.size, self.size)
            self.diag.append(links.copy(tx.at[0, at], rx.at[0, at], core))
            self.far.append(links.copy(tx.at[1, at], rx.at[1, at], far))

    def send_diag(self, i, terms):
        self.tx[0, pl.ds(i * self.size, self.size), :] = terms.astype(bf16)
        self.diag[i].start()

    def send_near(self, terms):
        self.tx[2] = terms.astype(bf16)
        self.near.start()

    def send_far(self, i, terms):
        at = pl.ds(i * self.size, self.size)
        self.diag[i].wait_recv()
        self.tx[1, at, :] = (terms + self.rx[0, at, :].astype(f32)).astype(bf16)
        self.far[i].start()

    def total(self, own):
        self.near.wait_recv()
        for copy in self.far:
            copy.wait_recv()
        return own + self.rx[2].astype(f32) + self.rx[1].astype(f32)

    def wait_send(self):
        for copy in [self.near] + self.diag + self.far:
            copy.wait_send()


GELU_SLOPE = 0.7978845608028654
GELU_CUBE = 0.044715


def z_order(z):
    near = z + 1 - 2 * lax.rem(z, 2)
    return [lax.rem(near + 2, 4), lax.rem(z + 2, 4), near, z]


def line_order(z):
    return [
        jnp.where(z < 2, 3, 0),
        jnp.where(z < 2, 2, 1),
        jnp.where(z == 0, 1, jnp.where(z == 1, 0, jnp.where(z == 2, 3, 2))),
        z,
    ]


def forward_kernel(
    exchange,
    buckets,
    tokens,
    small,
    first,
    w_query,
    w_key,
    w_value,
    w_out,
    gate_w,
    up_w,
    down_w,
    cot_in,
    grad_mixed,
    out_grad,
    gain_grad,
    qkv_out,
    mixed_out,
    lse_out,
    ff_far_out,
    own_terms_out,
    grad_h1_out,
    normed_out,
    down_out,
    gate_out,
    up_out,
    qkv,
    mixed,
    lse,
    ff_far,
    own_terms,
    grad_h1,
    normed,
    cot,
    wg,
    wu,
    wd,
    strip,
    hidden,
    gate_act,
    up_act,
    mixed_all,
    mixed_sum,
    far_terms,
    tx,
    rx,
    tx_ff,
    rx_ff,
    down_grad,
    gate_grad,
    up_grad,
    y_recv,
    z_recv,
    send,
    recv,
    local,
    free,
):
    group = Group()
    me, core, far, diag = group.me, group.core, group.far, group.diag
    rows, width = tokens.shape
    half = rows // 2
    length = 4 * rows
    heads = strip.shape[0]
    depth = w_out.shape[0]
    ff = wg.shape[0]
    part = width // 4
    gain_attn, gain_ff = small[0:1, 0:width], small[1:2, 0:width]
    links = Links(send, recv)
    peers = [group.at(core), group.at(far), group.at(diag)]
    z_peers = []
    if exchange:
        z, y = group.dp // 2, lax.rem(group.dp, 2)
        line, order = line_order(z), z_order(z)
        y_peer = (2 * z + 1 - y, me)
        near_peer = (2 * order[2] + y, me)
        z_peers = [(2 * lax.rem(z + t, 4) + y, me) for t in (1, 2, 3)]
        peers += [y_peer] + z_peers
    else:
        line, order, y = [0, 1, 2, 3], [0, 1, 2, 3], 0

    def place(order, t):
        found = jnp.int32(order[3])
        for i in range(3):
            found = jnp.where(t == i, order[i], found)
        return found

    started = []

    def load(src, dst):
        copy = pltpu.make_async_copy(src, dst, local.at[len(started)])
        started.append(copy)
        return copy

    def depth_rows(i):
        return pl.ds(pl.multiple_of(i * depth, 16), depth)

    own = block_rows(me, rows)
    out_own = load(w_out, wu.at[depth_rows(me)])
    out_own.start()
    proj_loads = [load(w, wg.at[depth_rows(i)]) for i, w in enumerate((w_query, w_key, w_value))]
    for copy in proj_loads:
        copy.start()
    cot_own = load(cot_in, cot.at[own])
    cot_own.start()
    down_load = load(down_w, wd)
    down_load.start()
    greet(peers)

    x = tokens[...].astype(f32)
    normed[own, :] = (rms(x) * gain_attn).astype(bf16)
    gather = Gather(links, group, normed, rows, 2)
    gather.start()
    out_own.wait()
    parts = 4 if exchange else 1
    piece = depth // parts

    def out_rows(dev):
        start = dev * depth + (z * piece if exchange else 0)
        return pl.ds(pl.multiple_of(start, 16), piece)

    out_near = links.copy(wu.at[depth_rows(me)], wu.at[depth_rows(me)], group.at(core))
    out_far = links.copy(wu.at[out_rows(me)], wu.at[out_rows(me)], group.at(far))
    out_near.start()
    out_z = [links.copy(wu.at[out_rows(far)], wu.at[out_rows(far)], peer) for peer in z_peers]
    out_pass = links.copy(wu.at[depth_rows(far)], wu.at[depth_rows(far)], group.at(core))
    cot_gather = Gather(links, group, cot, rows, 4, source=cot_in)
    cot_gather.near.start()
    mixed_near = links.copy(mixed.at[block_rows(core, rows)], mixed_all.at[me], group.at(core))
    mixed_far = links.copy(mixed.at[block_rows(far, rows)], mixed_all.at[me], group.at(far))
    mixed_diag = links.copy(mixed.at[block_rows(diag, rows)], mixed_all.at[me], group.at(diag))

    build_strips(strip, small, buckets)
    for copy in proj_loads:
        copy.wait()

    def project(dev):
        at = block_rows(dev, rows)
        block = normed[at, :]
        for i in range(3):
            qkv[i, at, :] = contract_cols(block, wg[i * depth : (i + 1) * depth, :]).astype(bf16)

    project(me)
    gather.near.wait_recv()
    project(core)
    gather.forward(0)
    gather.forward(1)
    out_far.start()
    cot_gather.far[0].start()
    project(far)
    for copy in gather.passed:
        copy.wait_recv()
    normed_save = load(normed, normed_out)
    normed_save.start()
    project(diag)
    gate_load = load(gate_w, wg)
    gate_load.start()

    def attend(dev):
        at = block_rows(dev, rows)
        seen = visible_keys(dev, rows, length, first[0])
        mixed_sum[...] = jnp.zeros_like(mixed_sum)
        lse[at, :] = jnp.zeros((rows, 128), f32)

        def one_head(h, carry):
            query = qkv[0, at, :]
            lanes = head_lanes(query.shape, h)
            scores = contract_cols(jnp.where(lanes, query, jnp.zeros_like(query)), qkv[1])
            scores = jnp.where(seen, add_bias(scores, strip, h, dev, length), masked_score)
            top = jnp.max(scores, axis=-1, keepdims=True)
            expo = jnp.exp(scores - top)
            total = jnp.sum(expo, axis=-1, keepdims=True)
            weights = (expo * (1.0 / total)).astype(bf16)
            mixed_sum[...] = jnp.where(lanes, mm(weights, qkv[2]), mixed_sum[...])
            lane = lax.broadcasted_iota(jnp.int32, (rows, 128), 1)
            lse[at, :] = jnp.where(lane == h, top + jnp.log(total), lse[at, :])
            return carry

        lax.fori_loop(0, heads, one_head, 0)
        mixed[at, :] = mixed_sum[...].astype(bf16)

    attend(far)
    gather.wait_send()
    normed_save.wait()
    mixed_far.start()
    cot_gather.far[1].start()
    out_far.wait_recv()
    for copy in out_z:
        copy.start()
    attend(diag)
    mixed_diag.start()
    cot_gather.far[2].start()
    attend(core)
    mixed_near.start()
    cot_gather.far[3].start()
    for copy in out_z:
        copy.wait_recv()
    out_pass.start()
    cot_gather.forward(0)
    attend(me)
    mixed_all[me] = mixed[own, :]
    out_near.wait_recv()
    attn = mm(mixed_all[me], wu[depth_rows(me), :])
    mixed_near.wait_recv()
    attn = attn + mm(mixed_all[core], wu[depth_rows(core), :])
    mixed_far.wait_recv()
    attn = attn + mm(mixed_all[far], wu[depth_rows(far), :])
    mixed_diag.wait_recv()
    out_pass.wait_recv()
    attn = attn + mm(mixed_all[diag], wu[depth_rows(diag), :])
    residual = x + attn
    grad_h1[...] = residual
    normed[own, :] = (rms(residual) * gain_ff).astype(bf16)
    second = Gather(links, group, normed, rows, 2)
    second.near.start()
    for copy in second.far:
        copy.start()
    for copy in [out_near, out_far, out_pass] + out_z:
        copy.wait_send()
    up_load = load(up_w, wu)
    up_load.start()

    scatter = Scatter(links, group, tx, rx, rows, 2)
    ff_diag = links.copy(tx_ff.at[0], rx_ff.at[0], group.at(core))
    ff_near = links.copy(tx_ff.at[1], rx_ff.at[1], group.at(core))

    def pair(ref, start, after):
        return jnp.concatenate(
            [
                ref[pl.ds(pl.multiple_of(start, 128), half), :],
                ref[pl.ds(pl.multiple_of(after, 128), half), :],
            ],
            axis=0,
        )

    def keep(i, value):
        strip[i, :, 0:ff] = value[:half]
        strip[i, :, length : length + ff] = value[half:]

    def unit(start, after):
        block = pair(normed, start, after)
        keep(0, contract_cols(block, wg[...]))
        keep(1, contract_cols(block, wu[...]))
        keep(2, contract_cols(pair(cot, start, after), wd[...]))
        for offset, lane in ((start, 0), (after, length)):

            def act(i, carry):
                at = pl.ds(pl.multiple_of(i * 16, 16), 16)
                to = pl.ds(pl.multiple_of(offset + i * 16, 16), 16)
                v, u, g = (strip[k, at, lane : lane + ff] for k in range(3))
                square = v * v
                t = jnp.tanh(GELU_SLOPE * v * (1.0 + GELU_CUBE * square))
                lift = 0.5 * (1.0 + t)
                value = v * lift
                slope = lift + 0.5 * v * (1.0 - t * t) * (
                    GELU_SLOPE * (1.0 + 3.0 * GELU_CUBE * square)
                )
                hidden[to, :] = (value * u).astype(bf16)
                gate_act[to, :] = (g * u * slope).astype(bf16)
                up_act[to, :] = (g * value).astype(bf16)
                return carry

            lax.fori_loop(0, half // 16, act, 0)

    def terms(start, after):
        return mm(pair(gate_act, start, after), wg[...]) + mm(
            pair(up_act, start, after), wu[...]
        )

    def weight_block(order, left, right, store, t):
        at = pl.ds(pl.multiple_of(place(order, t) * part, 128), part)
        value = contract_rows(left[:, at], right[...]).astype(bf16)
        store(t, value[: part // 2], value[part // 2 :])

    def weight_blocks(order, left, right, store):
        def one(t, carry):
            weight_block(order, left, right, store, t)
            return carry

        lax.fori_loop(0, 4, one, 0)

    cot_own.wait()
    down_load.wait()
    gate_load.wait()
    up_load.wait()
    unit(me * rows, me * rows + half)
    cot_gather.forward(1)
    cot_gather.near.wait_recv()
    second.near.wait_recv()
    unit(core * rows, core * rows + half)
    second.forward(0)
    second.passed[0].wait_recv()
    for i in (0, 1):
        cot_gather.passed[i].wait_recv()
    unit(far * rows, diag * rows)
    both = terms(far * rows, diag * rows)
    scatter.send_diag(0, both[half:])
    far_terms[pl.ds(0, half), :] = both[:half]
    cot_gather.forward(2)
    cot_gather.forward(3)
    scatter.send_far(0, far_terms[pl.ds(0, half), :])
    second.forward(1)
    for i in (2, 3):
        cot_gather.passed[i].wait_recv()
    second.passed[1].wait_recv()
    unit(far * rows + half, diag * rows + half)

    base = links.used
    links.used += 8

    def y_copy(t):
        return pltpu.make_async_remote_copy(
            src_ref=down_grad.at[t, 1 - y],
            dst_ref=y_recv.at[t],
            send_sem=send.at[base + t],
            recv_sem=recv.at[base + t],
            device_id=y_peer,
            device_id_type=MESH,
        )

    def z_copy(i, side):
        return pltpu.make_async_remote_copy(
            src_ref=gate_grad.at[2 * i, side],
            dst_ref=z_recv.at[i, side],
            send_sem=send.at[base + 4 + 2 * i + side],
            recv_sem=recv.at[base + 4 + 2 * i + side],
            device_id=near_peer,
            device_id_type=MESH,
        )

    spots = len(started) + 1

    def save(src, dst, at):
        return pltpu.make_async_copy(src, dst, local.at[spots + at])

    results = []

    def keep_result(src, dst):
        results.append(save(src, dst, 12 + len(results)))
        results[-1].start()

    keep_result(qkv, qkv_out)
    keep_result(mixed, mixed_out)
    keep_result(lse, lse_out)

    def store_down(t, low, high):
        down_grad[t, 0] = low
        down_grad[t, 1] = high
        if exchange:
            y_copy(t).start()
        else:
            save(down_grad.at[t], down_out.at[t], t).start()

    def store_gate(t, low, high):
        gate_grad[t, 0] = low
        gate_grad[t, 1] = high
        if exchange:

            if t % 2 == 0:
                z_copy(t // 2, 0).start()
                z_copy(t // 2, 1).start()
        else:
            save(gate_grad.at[t], gate_out.at[t], 4 + t).start()

    def store_up(t, low, high):
        slot = lax.rem(t, 2)

        @pl.when(t >= 2)
        def _():
            save(up_grad.at[slot], up_out.at[t - 2], 8 + t - 2).wait()

        up_grad[slot, 0] = low
        up_grad[slot, 1] = high
        save(up_grad.at[slot], up_out.at[t], 8 + t).start()

    def down_block(t):
        weight_block(line, cot, hidden, store_down, t)

    def gate_block(t):
        weight_block(order, normed, gate_act, store_gate, t)

    down_block(0)
    gate_block(0)
    both = terms(far * rows + half, diag * rows + half)
    scatter.send_diag(1, both[half:])
    far_terms[pl.ds(half, half), :] = both[:half]
    scatter.send_near(terms(core * rows, core * rows + half))
    scatter.send_far(1, far_terms[pl.ds(half, half), :])
    for block in (1, 2):
        down_block(block)
    own_terms[...] = terms(me * rows, me * rows + half)
    gate_block(2)
    down_block(3)
    cot_gather.wait_send()
    for peer in (core, far):
        pl.semaphore_signal(free, inc=1, device_id=group.at(peer), device_id_type=MESH)
    residual = grad_h1[...]
    pulled, gain_part = norm_pull(residual, gain_ff, scatter.total(own_terms[...]))
    gain_grad[...] = gain_part
    own_terms[...] = residual
    grad = cot[own, :].astype(f32) + pulled
    grad_h1[...] = grad
    cot[own, :] = grad.astype(bf16)
    third = Gather(links, group, cot, rows, 2)
    pl.semaphore_wait(free, 2)
    third.start()
    keep_result(grad_h1, grad_h1_out)
    gate_block(1)
    gate_block(3)
    scatter.wait_send()
    out_again = pltpu.make_async_copy(w_out, tx.at[0, 0:depth], local.at[spots - 1])
    out_again.start()

    def ff_terms(dev):
        return mm(hidden[block_rows(dev, rows), :], wd[...])

    tx_ff[0] = ff_terms(diag).astype(bf16)
    ff_diag.start()
    tx_ff[1] = ff_terms(core).astype(bf16)
    ff_near.start()
    own_part = ff_terms(far)
    ff_diag.wait_recv()
    ff_far[...] = (own_part + rx_ff[0].astype(f32)).astype(bf16)
    keep_result(ff_far, ff_far_out)
    own_part = ff_terms(me)
    ff_near.wait_recv()
    own_terms[...] += own_part + rx_ff[1].astype(f32)
    keep_result(own_terms, own_terms_out)
    def mix_back(dev):
        at = block_rows(dev, rows)
        grad_mixed[at, :] = contract_cols(cot[at, :], tx[0, 0:depth, :]).astype(bf16)

    weight_blocks(line, normed, up_act, store_up)
    out_again.wait()
    mix_back(me)
    third.near.wait_recv()
    mix_back(core)
    third.forward(0)
    if exchange:

        def sum_down(t, carry):
            y_copy(t).wait_recv()
            down_grad[t, y] = (
                down_grad[t, y].astype(f32) + y_recv[t].astype(f32)
            ).astype(bf16)
            save(down_grad.at[t, y], down_out.at[t], t).start()
            return carry

        lax.fori_loop(0, 3, sum_down, 0)
    third.forward(1)
    mix_back(far)
    for copy in third.passed:
        copy.wait_recv()
    mix_back(diag)

    def store_out(t, low, high):
        out_grad[t, 0] = low
        out_grad[t, 1] = high

    weight_blocks(line, cot, mixed, store_out)
    if exchange:
        sum_down(3, 0)
        for i in range(2):
            for side in range(2):
                z_copy(i, side).wait_recv()
                kept = gate_grad.at[2 * i + 1, side]
                kept[...] = (kept[...].astype(f32) + z_recv[i, side].astype(f32)).astype(bf16)
                save(kept, gate_out.at[i, side], 4 + 2 * i + side).start()

    for t in range(4):
        if exchange:
            save(down_grad.at[t, y], down_out.at[t], t).wait()
            save(gate_grad.at[t // 2 * 2 + 1, t % 2], gate_out.at[t // 2, t % 2], 4 + t).wait()
            y_copy(t).wait_send()
            z_copy(t // 2, t % 2).wait_send()
        else:
            save(down_grad.at[t], down_out.at[t], t).wait()
            save(gate_grad.at[t], gate_out.at[t], 4 + t).wait()
        if t >= 2:
            save(up_grad.at[t % 2], up_out.at[t], 8 + t).wait()
    for copy in (mixed_near, mixed_far, mixed_diag):
        copy.wait_send()
    for copy in results:
        copy.wait()
    second.wait_send()
    third.wait_send()
    ff_diag.wait_send()
    ff_near.wait_send()


def in_vmem():
    return pl.BlockSpec(memory_space=pltpu.VMEM)


def anywhere():
    return pl.BlockSpec(memory_space=pl.ANY)


def in_smem():
    return pl.BlockSpec(memory_space=pltpu.SMEM)


def forward(exchange, table_shape, tokens, small, first, w_query, w_key, w_value, w_out, gate_w, up_w, down_w, cot):
    rows, width = tokens.shape
    length = 4 * rows
    cols = w_query.shape[0]
    ff = gate_w.shape[0]
    buckets, heads = table_shape
    part = width // 8
    shape = jax.ShapeDtypeStruct
    halves = (4, 2, part, ff)
    kept = [
        shape((3, length, cols), bf16),
        shape((length, cols), bf16),
        shape((length, 128), f32),
        shape((rows, width), bf16),
        shape((rows, width), f32),
        shape((rows, width), f32),
    ]
    return pl.pallas_call(
        functools.partial(forward_kernel, exchange, buckets),
        out_shape=(
            shape((length, cols), bf16),
            shape((4, 2, part, cols), bf16),
            shape((1, width), f32),
            *kept,
            shape((length, width), bf16),
            shape((4, part, ff) if exchange else halves, bf16),
            shape((2, 2, part, ff) if exchange else halves, bf16),
            shape(halves, bf16),
        ),
        in_specs=[in_vmem()] * 2 + [in_smem()] + [anywhere()] * 8,
        out_specs=[in_vmem()] * 3 + [anywhere()] * 10,
        scratch_shapes=[pltpu.VMEM(v.shape, v.dtype) for v in kept]
        + [
            pltpu.VMEM((length, width), bf16),
            pltpu.VMEM((length, width), bf16),
            pltpu.VMEM((ff, width), bf16),
            pltpu.VMEM((ff, width), bf16),
            pltpu.VMEM((ff, width), bf16),
            pltpu.VMEM((heads, 128, 2 * length), f32),
            pltpu.VMEM((length, ff), bf16),
            pltpu.VMEM((length, ff), bf16),
            pltpu.VMEM((length, ff), bf16),
            pltpu.VMEM((4, rows, cols), bf16),
            pltpu.VMEM((rows, cols), f32),
            pltpu.VMEM((rows, width), f32),
            pltpu.VMEM((3, rows, width), bf16),
            pltpu.VMEM((3, rows, width), bf16),
            pltpu.VMEM((2, rows, width), bf16),
            pltpu.VMEM((2, rows, width), bf16),
            pltpu.VMEM(halves, bf16),
            pltpu.VMEM(halves, bf16),
            pltpu.VMEM((2, 2, part, ff), bf16),
            pltpu.VMEM((4, part, ff) if exchange else (8, 128), bf16),
            pltpu.VMEM((2, 2, part, ff) if exchange else (8, 128), bf16),
            pltpu.SemaphoreType.DMA((56,)),
            pltpu.SemaphoreType.DMA((56,)),
            pltpu.SemaphoreType.DMA((32,)),
            pltpu.SemaphoreType.REGULAR,
        ],
        compiler_params=pltpu.CompilerParams(
            collective_id=0, has_side_effects=True, vmem_limit_bytes=VMEM_BYTES
        ),
    )(tokens, small, first, w_query, w_key, w_value, w_out, gate_w, up_w, down_w, cot)


class Line:
    def __init__(self, links, dp, mp, own, y_recv, z_recv, sources=()):
        z, y = dp // 2, lax.rem(dp, 2)
        near = z + 1 - 2 * lax.rem(z, 2)
        self.own, self.y_recv, self.z_recv = own, y_recv, z_recv
        self.inner = (z == 1) | (z == 2)
        self.y_peer, self.near, self.across = (2 * z + 1 - y, mp), (2 * near + y, mp), (2 * lax.rem(z + 2, 4) + y, mp)
        self.middle = (2 * (3 - z) + y, mp)
        self.y_copies = [links.copy(src, y_recv.at[i], self.y_peer) for i, src in enumerate(sources)]
        base = links.used
        links.used += 5
        forth = jnp.where(self.inner, self.middle[0], self.near[0])
        step = jnp.where(self.inner, 3, 0)
        self.copies = [
            pltpu.make_async_remote_copy(
                src_ref=own.at[i],
                dst_ref=z_recv.at[slot],
                send_sem=links.send.at[base + i],
                recv_sem=links.recv.at[base + slot],
                device_id=(to, mp),
                device_id_type=MESH,
            )
            for i, (slot, to) in enumerate(((step, forth), (step + 1, forth), (2, self.near[0])))
        ]
        self.arrivals = [
            pltpu.make_async_remote_copy(
                src_ref=own.at[0],
                dst_ref=z_recv.at[slot],
                send_sem=links.send.at[base],
                recv_sem=links.recv.at[base + slot],
                device_id=self.near,
                device_id_type=MESH,
            )
            for slot in range(5)
        ]

    def add(self, i, other):
        self.own[i] = (self.own[i].astype(f32) + other.astype(f32)).astype(bf16)

    def begin(self, i):
        @pl.when(jnp.logical_not(self.inner))
        def _():
            self.copies[i].start()

    def take_y(self, i):
        self.y_copies[i].wait_recv()
        self.add(i, self.y_recv[i])
        if i < 3:
            self.begin(i)

    def relay(self, i):
        slot = (0, 1, 3)[i]

        @pl.when(self.inner)
        def _():
            self.arrivals[slot].wait_recv()
            self.add(i, self.z_recv[slot])
            self.copies[i].start()

    def total(self, out):
        self.arrivals[2].wait_recv()
        out[...] = self.own[3].astype(f32) + self.z_recv[2].astype(f32)

        @pl.when(self.inner)
        def _():
            self.arrivals[4].wait_recv()
            out[...] += self.z_recv[4].astype(f32)

    def wait_send(self):
        for copy in self.y_copies + self.copies:
            copy.wait_send()


class LastHalvings:
    def __init__(self, links, line, own, y_recv, z_recv, sources):
        self.own, self.y_recv, self.z_recv, self.inner = own, y_recv, z_recv, line.inner
        self.y_copies = [
            links.copy(src, y_recv.at[i], line.y_peer) for i, src in enumerate(sources)
        ]
        base = links.used
        links.used += 3

        def copy(i, src, slot, to):
            return pltpu.make_async_remote_copy(
                src_ref=src,
                dst_ref=z_recv.at[slot],
                send_sem=links.send.at[base + i],
                recv_sem=links.recv.at[base + slot],
                device_id=to,
                device_id_type=MESH,
            )

        mp = line.near[1]
        forth = (jnp.where(self.inner, line.middle[0], line.near[0]), mp)
        self.first = copy(0, own.at[0], jnp.where(self.inner, 1, 0), forth)
        self.inwards = copy(1, z_recv.at[0], 2, line.middle)
        self.outwards = copy(2, z_recv.at[1], 2, line.near)
        self.arrivals = [copy(0, own.at[0], slot, line.near) for slot in range(3)]

    def take_y(self, i):
        self.y_copies[i].wait_recv()
        self.own[i] = (self.own[i].astype(f32) + self.y_recv[i].astype(f32)).astype(bf16)
        if i == 0:
            self.first.start()

    def hand_on(self):
        @pl.when(self.inner)
        def _():
            self.arrivals[1].wait_recv()
            self.outwards.start()
            self.arrivals[0].wait_recv()
            self.inwards.start()

    def total(self):
        self.arrivals[2].wait_recv()
        return self.own[1].astype(f32) + self.z_recv[2].astype(f32)

    def wait_send(self):
        for copy in self.y_copies + [self.first]:
            copy.wait_send()

        @pl.when(self.inner)
        def _():
            self.outwards.wait_send()
            self.inwards.wait_send()


def back_kernel(
    exchange,
    buckets,
    small,
    qkv,
    lse,
    grad_mixed,
    out_grad,
    gain_ff_part,
    first,
    tokens_in,
    grad_h1_in,
    w_query_in,
    w_key_in,
    w_value_in,
    ff_base_in,
    normed_in,
    ff_far,
    down_in,
    gate_in,
    up_in,
    stats_out,
    attn_out,
    output,
    grad_input,
    gate_out,
    up_out,
    down_out,
    tokens,
    grad_h1,
    ff_base,
    w_query,
    w_key,
    w_value,
    gate_sum,
    up_sum,
    down_sum,
    normed,
    strip,
    strip_grad,
    key_head,
    value_head,
    query_sum,
    key_sum,
    value_sum,
    grad_qkv,
    own_terms,
    tx,
    rx,
    down_own,
    down_z,
    gate_own,
    gate_y,
    gate_z,
    up_own,
    up_y,
    up_z,
    attn_own,
    attn_send,
    attn_y,
    attn_z,
    attn_sum,
    ff_recv,
    stats,
    stats_recv,
    send,
    recv,
    local,
):
    group = Group()
    me, core, far, diag = group.me, group.core, group.far, group.diag
    rows, width = grad_h1.shape
    half = rows // 2
    length = 4 * rows
    part = width // 4
    heads = strip.shape[0]
    span = 2 * length
    links = Links(send, recv)
    dp = group.dp
    peers = [group.at(core), group.at(far)]
    copies = []

    def load(src, dst):
        copy = pltpu.make_async_copy(src, dst, local.at[len(copies)])
        copies.append(copy)
        return copy

    save_normed = load(normed_in, normed)
    late = [
        load(src, dst)
        for src, dst in (
            (tokens_in, tokens),
            (grad_h1_in, grad_h1),
            (ff_base_in, ff_base),
            (w_query_in, w_query),
            (w_key_in, w_key),
            (w_value_in, w_value),
        )
    ]
    if exchange:
        z, y = dp // 2, lax.rem(dp, 2)
        order = line_order(z)
        down = Line(links, dp, me, down_own, None, down_z)
        gate = LastHalvings(links, down, gate_own, gate_y, gate_z, [gate_in.at[i, 1 - y] for i in range(2)])
        up = Line(links, dp, me, up_own, up_y, up_z, [up_in.at[i, 1 - y] for i in range(4)])
        attn = Line(links, dp, me, attn_own, attn_y, attn_z, [attn_send.at[i] for i in range(4)])
        peers += [down.y_peer, down.near, down.across, down.middle]
        loads = [load(down_in.at[i], down_own.at[i]) for i in range(4)]
        gate_loads = [load(gate_in.at[i, y], gate_own.at[i]) for i in range(2)]
        up_loads = [load(up_in.at[i, y], up_own.at[i]) for i in range(4)]
        for copy in loads:
            copy.start()
    else:
        order = [0, 1, 2, 3]
    greet(peers)
    if exchange:
        for copy in gate.y_copies + up.y_copies:
            copy.start()
        for i in range(4):
            loads[i].wait()
            if i < 3:
                down.begin(i)
        for copy in gate_loads + up_loads:
            copy.start()
    for copy in [save_normed] + late:
        copy.start()
    scatter = Scatter(links, group, tx, rx, rows, 1)
    ff_copy = links.copy(ff_far, ff_recv, group.at(far))
    ff_copy.start()
    stages = []
    for i, to in enumerate(peers[2:5] + peers[:2]):
        stages.append(links.copy(stats.at[i], stats_recv.at[i], to))

    build_strips(strip, small, buckets)
    strip_grad[...] = jnp.zeros_like(strip_grad)
    query_sum[...] = jnp.zeros_like(query_sum)
    key_sum[...] = jnp.zeros_like(key_sum)
    value_sum[...] = jnp.zeros_like(value_sum)

    def attend_back(dev, h):
        at = block_rows(dev, rows)
        seen = visible_keys(dev, rows, length, first[0])
        query, grad = qkv[0, at, :], grad_mixed[at, :]
        lanes = head_lanes(query.shape, h)
        zero = jnp.zeros_like(query)
        scores = contract_cols(query, key_head[...])
        scores = jnp.where(seen, add_bias(scores, strip, h, dev, length), masked_score)
        probs = jnp.exp(scores - lse[at, h : h + 1])
        inner = contract_cols(grad, value_head[...])
        center = jnp.sum(probs * inner, axis=-1, keepdims=True)
        score_grad = (probs * (inner - center)).astype(bf16)
        query_sum[at, :] += mm(score_grad, key_head[...])
        key_sum[...] += contract_rows(score_grad, jnp.where(lanes, query, zero))
        value_sum[...] += contract_rows(probs.astype(bf16), jnp.where(lanes, grad, zero))
        count = length // 128
        for i in range(rows // 128):
            start = (count - 1 - i) * 128 - dev * rows
            to = pl.ds(pl.multiple_of(start, 128), length)
            strip_grad[h, :, to] += score_grad[i * 128 : (i + 1) * 128].astype(f32)

    def head_keys(h):
        key, value = qkv[1], qkv[2]
        lanes = head_lanes(key.shape, h)
        key_head[...] = jnp.where(lanes, key, jnp.zeros_like(key))
        value_head[...] = jnp.where(lanes, value, jnp.zeros_like(value))

    def take_gate(i):
        gate_loads[i].wait()
        gate.take_y(i)

    def take_up(i):
        up_loads[i].wait()
        up.take_y(i)

    def down_total():
        down.total(down_sum)
        save(down_sum, down_out)

    def gate_total():
        gate_sum[...] = gate.total()
        save(gate_sum, gate_out)

    head_keys(0)
    between = {
        (0, 1): [lambda: take_gate(0)],
        (0, 2): [lambda: down.relay(0)],
        (1, 2): [lambda: take_gate(1), lambda: down.relay(1)],
        (1, 3): [lambda: down.relay(2)],
        (2, 2): [lambda: take_up(0)],
    } if exchange else {}
    for h in range(heads):
        if h:
            head_keys(h)
        for j, dev in enumerate((diag, far, core, me)):
            attend_back(dev, h)
            for step in between.get((h, j), []):
                step()

    grad_qkv[0] = query_sum[...].astype(bf16)
    grad_qkv[1] = key_sum[...].astype(bf16)
    grad_qkv[2] = value_sum[...].astype(bf16)

    def terms(dev):
        at = block_rows(dev, rows)
        return (
            mm(grad_qkv[0, at, :], w_query[...])
            + mm(grad_qkv[1, at, :], w_key[...])
            + mm(grad_qkv[2, at, :], w_value[...])
        )

    gain_parts = []

    def gain_terms(dev):
        value = terms(dev)
        product = value * normed[block_rows(dev, rows), :].astype(f32)
        gain_parts.append(jnp.sum(product, axis=0, keepdims=True))
        return value

    for copy in [save_normed] + late:
        copy.wait()
    saves = []

    def save(src, dst):
        saves.append(load(src, dst))
        saves[-1].start()

    scatter.send_diag(0, gain_terms(diag))
    scatter.send_near(gain_terms(core))
    scatter.send_far(0, gain_terms(far))
    own_terms[...] = gain_terms(me)

    index = small[2:3, :]
    lines = []
    for h in range(heads):
        fold = strip_grad[h]
        count = 128
        while count > 1:
            count //= 2
            fold = fold[:count] + pltpu.roll(fold[count:], span - count, 1)
        lines.append(pltpu.roll(fold, 127, 1))
    diagonals = jnp.concatenate(lines + [jnp.zeros((8 - heads, span), f32)], axis=0)
    onehot = (lax.broadcasted_iota(jnp.int32, (buckets, span), 0).astype(f32) == index).astype(f32)
    table_part = lax.dot_general(
        diagonals, onehot, (((1,), (1,)), ((), ())), precision=highest, preferred_element_type=f32
    )
    stats[0] = jnp.zeros_like(stats[0])
    stats[0, 0:1, :] = (gain_parts[0] + gain_parts[1] + gain_parts[2] + gain_parts[3]) / small[0:1, 0:width]
    stats[0, 1:2, :] = gain_ff_part[...]
    stats[0, 2 : 2 + heads, 0:buckets] = table_part[0:heads]
    stages[0].start()
    dp_stages = len(stages) - 2

    def next_stage(i):
        stages[i].wait_recv()
        total = stats[i] + stats_recv[i]
        if i >= dp_stages:
            row = lax.broadcasted_iota(jnp.int32, total.shape, 0)
            total = jnp.where(row < 2, total, stats[i])
        if i + 1 < len(stages):
            stats[i + 1] = total
            stages[i + 1].start()
        else:
            stats_out[...] = total

    cols = w_query.shape[0]
    for i in range(4):
        at = pl.ds(pl.multiple_of(order[i] * part, 128), part)
        for m in range(3):
            block = contract_rows(normed[:, at], grad_qkv[m]).astype(bf16)
            if exchange:
                low, high = block[: part // 2], block[part // 2 :]
                lanes = slice(m * cols, (m + 1) * cols)
                attn_send[i, :, lanes] = jnp.where(y == 0, high, low)
                attn_own[i, :, lanes] = jnp.where(y == 0, low, high)
            else:
                attn_out[m, at, :] = block
        if exchange:
            attn_send[i, :, 3 * cols :] = out_grad[i, 1 - y]
            attn_own[i, :, 3 * cols :] = out_grad[i, y]
            attn.y_copies[i].start()
        else:
            for side in range(2):
                attn_out[3, pl.ds(i * part + side * part // 2, part // 2), :] = out_grad[i, side]

    if exchange:
        take_up(1)
        down_total()
        gate.hand_on()
    ff_copy.wait_recv()
    ff_recv[...] = (ff_base[...] + ff_recv[...].astype(f32)).astype(bf16)
    save(ff_recv, output)

    def input_total():
        pulled, _ = norm_pull(tokens[...].astype(f32), small[0:1, 0:width], scatter.total(own_terms[...]))
        grad_h1[...] += pulled
        save(grad_h1, grad_input)

    if exchange:
        up.relay(0)
        take_up(2)
        take_up(3)
        next_stage(0)
        up.relay(1)
        attn.take_y(0)
        gate_total()
        input_total()
        up.relay(2)
        next_stage(1)
        attn.take_y(1)
        attn.relay(0)
        next_stage(2)
        attn.take_y(2)
        up.total(up_sum)
        save(up_sum, up_out)
        attn.relay(1)
        next_stage(3)
        next_stage(4)
        attn.relay(2)
        attn.take_y(3)
        attn.total(attn_sum)
        for m in range(3):
            attn_out[m] = attn_sum[:, m * cols : (m + 1) * cols]
        attn_out[3] = attn_sum[:, 3 * cols :].T
        down.wait_send()
        gate.wait_send()
        up.wait_send()
        attn.wait_send()
    else:
        input_total()
        next_stage(0)
        next_stage(1)
    for copy in saves:
        copy.wait()
    ff_copy.wait_send()
    scatter.wait_send()
    for stage in stages:
        stage.wait_send()


def attention_backward(
    exchange, table_shape, tokens, small, grad_h1, qkv, lse, w_query, w_key, w_value, grad_mixed, out_grad,
    gain_ff_part, ff_base, first, normed, ff_far, down_in, gate_in, up_in,
):
    rows, width = grad_h1.shape
    length = 4 * rows
    cols = w_query.shape[0]
    ff = down_in.shape[-1]
    buckets, heads = table_shape
    part = width // 8
    shape = jax.ShapeDtypeStruct
    ff_scratch = pltpu.VMEM((part, ff) if exchange else (8, 128), f32)
    scratch = [
        pltpu.VMEM((rows, width), bf16),
        pltpu.VMEM((rows, width), f32),
        pltpu.VMEM((rows, width), f32),
        pltpu.VMEM((cols, width), bf16),
        pltpu.VMEM((cols, width), bf16),
        pltpu.VMEM((cols, width), bf16),
        ff_scratch,
        ff_scratch,
        ff_scratch,
        pltpu.VMEM((length, width), bf16),
        pltpu.VMEM((heads, 128, 2 * length), f32),
        pltpu.VMEM((heads, 128, 2 * length), f32),
        pltpu.VMEM((length, cols), bf16),
        pltpu.VMEM((length, cols), bf16),
        pltpu.VMEM((length, cols), f32),
        pltpu.VMEM((length, cols), f32),
        pltpu.VMEM((length, cols), f32),
        pltpu.VMEM((3, length, cols), bf16),
        pltpu.VMEM((rows, width), f32),
        pltpu.VMEM((3, rows, width), bf16),
        pltpu.VMEM((3, rows, width), bf16),
    ]
    for count in (4, 5, 2, 2, 3, 4, 4, 5):
        scratch.append(pltpu.VMEM((count, part, ff) if exchange else (8, 128), bf16))
    for count in (4, 4, 4, 5):
        scratch.append(pltpu.VMEM((count, part, 4 * cols) if exchange else (8, 128), bf16))
    stages = 5 if exchange else 2
    scratch += [
        pltpu.VMEM((part, 4 * cols), f32),
        pltpu.VMEM((rows, width), bf16),
        pltpu.VMEM((stages, 8, width), f32),
        pltpu.VMEM((stages, 8, width), f32),
        pltpu.SemaphoreType.DMA((48,)),
        pltpu.SemaphoreType.DMA((48,)),
        pltpu.SemaphoreType.DMA((24,)),
    ]
    ff_out = shape((part, ff) if exchange else (8, 128), f32)
    return pl.pallas_call(
        functools.partial(back_kernel, exchange, buckets),
        out_shape=(
            shape((8, width), f32),
            shape((4, part, cols), f32) if exchange else shape((4, width, cols), bf16),
            shape((rows, width), bf16),
            shape((rows, width), f32),
            ff_out,
            ff_out,
            ff_out,
        ),
        in_specs=[in_vmem()] * 6 + [in_smem()] + [anywhere()] * 11,
        out_specs=[in_vmem()] * 2 + [anywhere()] * 5,
        scratch_shapes=scratch,
        compiler_params=pltpu.CompilerParams(
            collective_id=1, has_side_effects=True, vmem_limit_bytes=VMEM_BYTES
        ),
    )(
        small, qkv, lse, grad_mixed, out_grad, gain_ff_part, first, tokens, grad_h1, w_query, w_key, w_value,
        ff_base, normed, ff_far, down_in, gate_in, up_in,
    )


def finish_kernel(heads, *refs):
    ins, outs, (attn_held, *held, load, save) = refs[:7], refs[7:19], refs[19:]
    stats, attn = ins[0], ins[1]
    sources = list(ins[2:]) + [attn.at[i] for i in range(4)]
    slots = held + [attn_held.at[i] for i in range(4)]
    targets = list(outs[4:9]) + list(outs[:4])
    loads = [pltpu.make_async_copy(a, b, load.at[i]) for i, (a, b) in enumerate(zip(sources, slots))]
    saves = [pltpu.make_async_copy(a, b, save.at[i]) for i, (a, b) in enumerate(zip(slots, targets))]
    for copy in loads:
        copy.start()
    gain_attn, gain_ff, table = outs[9:]
    gain_attn[...] = stats[0]
    gain_ff[...] = stats[1]
    table[...] = stats[2 : 2 + heads, 0 : table.shape[1]]
    for before, after in zip(loads, saves):
        before.wait()
        after.start()
    for copy in saves:
        copy.wait()


def finish(table_shape, stats, attn, *whole):
    buckets, heads = table_shape
    shape = jax.ShapeDtypeStruct
    outs = [shape(attn.shape[1:], f32)] * 4 + [shape(v.shape, v.dtype) for v in whole]
    small = [shape(stats.shape[1:], f32)] * 2 + [shape((heads, buckets), f32)]
    return pl.pallas_call(
        functools.partial(finish_kernel, heads),
        out_shape=outs + small,
        in_specs=[in_vmem()] + [anywhere()] * 6,
        out_specs=[anywhere()] * 9 + [in_vmem()] * 3,
        scratch_shapes=[pltpu.VMEM(v.shape, v.dtype) for v in (attn, *whole)]
        + [pltpu.SemaphoreType.DMA((9,))] * 2,
        compiler_params=pltpu.CompilerParams(vmem_limit_bytes=VMEM_BYTES),
    )(stats, attn, *whole)


def shards(
    tokens,
    gain_attn,
    w_query,
    w_key,
    w_value,
    w_out,
    bias_table,
    gain_ff,
    w_gate,
    w_up,
    w_down,
    cotangent,
    first_length,
    offset_bucket,
):
    n_dp = lax.axis_size("dp")
    exchange = n_dp == 8
    buckets, heads = bias_table.shape
    width = tokens.shape[1]
    small = pack_small(gain_attn, gain_ff, offset_bucket, bias_table)
    turned = [w_query.T, w_key.T, w_value.T]
    grad_mixed, out_grad, gain_ff_part, qkv, mixed, lse, ff_far, ff_base, grad_h1, normed, down, gate, up = forward(
        exchange, bias_table.shape, tokens, small, first_length, *turned, w_out, w_gate.T, w_up.T, w_down, cotangent
    )
    stats, attn, output, grad_input, gate_sum, up_sum, down_sum = attention_backward(
        exchange, bias_table.shape, tokens, small, grad_h1, qkv, lse, *turned, grad_mixed, out_grad, gain_ff_part,
        ff_base, first_length, normed, ff_far, down, gate, up,
    )
    if exchange:
        *attn, output, grad_input, gate_sum, up_sum, down_sum, gain_first, gain_second, table = finish(
            bias_table.shape, stats, attn, output, grad_input, gate_sum, up_sum, down_sum
        )
    else:
        def scatter(value):
            value = value.reshape(width, -1).astype(f32)
            return lax.psum_scatter(value, "dp", scatter_dimension=0, tiled=True)

        stats = lax.psum(stats, "dp")
        gate_sum, up_sum, down_sum = scatter(gate), scatter(up), scatter(down)
        attn = [scatter(attn[i]) for i in range(4)]
        attn[3] = attn[3].T
        gain_first, gain_second, table = stats[0], stats[1], stats[2 : 2 + heads, :buckets]
    return (
        output,
        grad_input,
        gain_first,
        attn[0],
        attn[1],
        attn[2],
        attn[3],
        table.T,
        gain_second,
        gate_sum,
        up_sum,
        down_sum.T,
    )


def solution(mesh):
    placed = (
        P(("dp", "mp"), None),
        P(),
        P(None, "mp"),
        P(None, "mp"),
        P(None, "mp"),
        P("mp", None),
        P(None, "mp"),
        P(),
        P(None, "mp"),
        P(None, "mp"),
        P("mp", None),
        P(("dp", "mp"), None),
        P("dp"),
        P(),
    )
    return jax.shard_map(
        shards,
        mesh=mesh,
        in_specs=placed,
        out_specs=(
            P(("dp", "mp"), None),
            P(("dp", "mp"), None),
            P(),
            P("dp", "mp"),
            P("dp", "mp"),
            P("dp", "mp"),
            P("mp", "dp"),
            P(None, "mp"),
            P(),
            P("dp", "mp"),
            P("dp", "mp"),
            P("mp", "dp"),
        ),
        check_vma=False,
    )
```

```python
import functools

import jax
import jax.numpy as jnp
from jax import lax
from jax.experimental import pallas as pl
from jax.experimental.pallas import tpu as pltpu
from jax.sharding import PartitionSpec as P

MESH = pl.DeviceIdType.MESH
DH = 64
epsilon = 1e-06
masked_score = -1000000000.0
highest = lax.Precision.HIGHEST
bf16 = jnp.bfloat16
f32 = jnp.float32
VMEM_BYTES = 62 * 2**20


def mm(left, right):
    return jnp.dot(left, right, preferred_element_type=f32)


def contract_rows(left, right):
    return lax.dot_general(left, right, (((0,), (0,)), ((), ())), preferred_element_type=f32)


def contract_cols(left, right):
    return lax.dot_general(left, right, (((1,), (1,)), ((), ())), preferred_element_type=f32)


def rms(values):
    return values * lax.rsqrt(jnp.mean(values * values, axis=-1, keepdims=True) + epsilon)


class Links:
    def __init__(self, send, recv):
        self.send, self.recv, self.used = send, recv, 0

    def copy(self, src, dst, to):
        at = self.used
        self.used += 1
        return pltpu.make_async_remote_copy(
            src_ref=src,
            dst_ref=dst,
            send_sem=self.send.at[at],
            recv_sem=self.recv.at[at],
            device_id=to,
            device_id_type=MESH,
        )


class Group:
    def __init__(self):
        self.dp, self.me = lax.axis_index("dp"), lax.axis_index("mp")
        self.core = self.me + 1 - 2 * lax.rem(self.me, 2)
        self.far = lax.rem(self.me + 2, 4)
        self.diag = 3 - self.me

    def at(self, mp):
        return (self.dp, mp)


def greet(peers):
    barrier = pltpu.get_barrier_semaphore()
    for peer in peers:
        pl.semaphore_signal(barrier, inc=1, device_id=peer, device_id_type=MESH)
    pl.semaphore_wait(barrier, len(peers))


def block_rows(dev, rows, start=0, size=None):
    return pl.ds(pl.multiple_of(dev * rows + start, 16), rows if size is None else size)


class Gather:
    def __init__(self, links, group, full, rows, chunks, source=None):
        size = rows // chunks
        own = block_rows(group.me, rows)
        self.near = links.copy(full.at[own] if source is None else source, full.at[own], group.at(group.core))
        self.far, self.passed = [], []
        for i in range(chunks):
            mine = block_rows(group.me, rows, i * size, size)
            theirs = block_rows(group.far, rows, i * size, size)
            src = full.at[mine] if source is None else source.at[pl.ds(i * size, size)]
            self.far.append(links.copy(src, full.at[mine], group.at(group.far)))
            self.passed.append(links.copy(full.at[theirs], full.at[theirs], group.at(group.core)))

    def start(self):
        self.near.start()
        for copy in self.far:
            copy.start()

    def forward(self, i):
        self.far[i].wait_recv()
        self.passed[i].start()

    def wait_send(self):
        self.near.wait_send()
        for copy in self.far + self.passed:
            copy.wait_send()


def pack_small(small, gain_attn, gain_ff, offset_bucket, table):
    width, offsets = gain_attn.shape[0], offset_bucket.shape[0]
    heads, buckets = table.shape
    small[...] = jnp.full(small.shape, -1.0, f32)
    small[0:1, 0:width] = gain_attn[...].reshape(1, width)
    small[1:2, 0:width] = gain_ff[...].reshape(1, width)
    small[2:3, 0:offsets] = offset_bucket[...].astype(f32).reshape(1, offsets)
    small[3 : 3 + heads, 0:buckets] = table[...]


def build_strips(strip, small, buckets):
    index = small[2:3, :]
    heads, _, width = strip.shape
    for h in range(heads):
        row = jnp.zeros(index.shape, f32)
        for b in range(buckets):
            row = jnp.where(index == float(b), small[3 + h : 4 + h, b : b + 1], row)
        strip[h] = pltpu.roll(
            jnp.broadcast_to(row, (128, width)), width - 127, 1, stride=1, stride_axis=0
        )


def add_bias(scores, strip, h, dev, length):
    parts = []
    count = length // 128
    for i in range(scores.shape[0] // 128):
        first = (count - 1 - i) * 128 - dev * scores.shape[0]
        parts.append(
            scores[i * 128 : (i + 1) * 128]
            + strip[h, :, pl.ds(pl.multiple_of(first, 128), length)]
        )
    return jnp.concatenate(parts, axis=0)


def visible_keys(dev, rows, length, first):
    key = lax.broadcasted_iota(jnp.int32, (1, length), 1)
    return (key >= first) == (dev * rows >= first)


def head_lanes(shape, h):
    lane = lax.broadcasted_iota(jnp.int32, shape, len(shape) - 1)
    return (lane >= h * DH) & (lane < (h + 1) * DH)


def norm_pull(values, gain, grad):
    inverse = lax.rsqrt(jnp.mean(values * values, axis=-1, keepdims=True) + epsilon)
    scaled = grad * gain
    along = jnp.mean(values * scaled, axis=-1, keepdims=True)
    gain_grad = jnp.sum(grad * values * inverse, axis=0, keepdims=True)
    return inverse * scaled - values * (along * inverse * inverse * inverse), gain_grad


class Scatter:
    def __init__(self, links, group, tx, rx, rows, parts):
        self.tx, self.rx, self.size = tx, rx, rows // parts
        core, far = group.at(group.core), group.at(group.far)
        self.near = links.copy(tx.at[2], rx.at[2], core)
        self.diag, self.far = [], []
        for i in range(parts):
            at = pl.ds(i * self.size, self.size)
            self.diag.append(links.copy(tx.at[0, at], rx.at[0, at], core))
            self.far.append(links.copy(tx.at[1, at], rx.at[1, at], far))

    def send_diag(self, i, terms):
        self.tx[0, pl.ds(i * self.size, self.size), :] = terms.astype(bf16)
        self.diag[i].start()

    def send_near(self, terms):
        self.tx[2] = terms.astype(bf16)
        self.near.start()

    def send_far(self, i, terms):
        at = pl.ds(i * self.size, self.size)
        self.diag[i].wait_recv()
        self.tx[1, at, :] = (terms + self.rx[0, at, :].astype(f32)).astype(bf16)
        self.far[i].start()

    def total(self, own):
        self.near.wait_recv()
        for copy in self.far:
            copy.wait_recv()
        return own + self.rx[2].astype(f32) + self.rx[1].astype(f32)

    def wait_send(self):
        for copy in [self.near] + self.diag + self.far:
            copy.wait_send()


GELU_SLOPE = 0.7978845608028654
GELU_CUBE = 0.044715


def z_order(z):
    near = z + 1 - 2 * lax.rem(z, 2)
    return [lax.rem(near + 2, 4), lax.rem(z + 2, 4), near, z]


def line_order(z):
    return [
        jnp.where(z < 2, 3, 0),
        jnp.where(z < 2, 2, 1),
        jnp.where(z == 0, 1, jnp.where(z == 1, 0, jnp.where(z == 2, 3, 2))),
        z,
    ]


def forward_kernel(
    exchange,
    buckets,
    tokens,
    gain_attn_in,
    gain_ff_in,
    offset_bucket,
    table,
    first,
    w_query,
    w_key,
    w_value,
    w_out,
    gate_w,
    up_w,
    down_w,
    cot_in,
    grad_mixed,
    out_grad,
    gain_grad,
    small,
    qkv_out,
    mixed_out,
    lse_out,
    ff_far_out,
    own_terms_out,
    grad_h1_out,
    normed_out,
    down_out,
    gate_out,
    up_out,
    qkv,
    mixed,
    lse,
    ff_far,
    own_terms,
    grad_h1,
    normed,
    cot,
    wg,
    wu,
    wd,
    strip,
    hidden,
    gate_act,
    up_act,
    mixed_all,
    mixed_sum,
    far_terms,
    tx,
    rx,
    tx_ff,
    rx_ff,
    down_grad,
    gate_grad,
    up_grad,
    y_recv,
    z_recv,
    send,
    recv,
    local,
    free,
):
    group = Group()
    me, core, far, diag = group.me, group.core, group.far, group.diag
    rows, width = tokens.shape
    half = rows // 2
    length = 4 * rows
    heads = strip.shape[0]
    depth = w_out.shape[0]
    ff = wg.shape[0]
    part = width // 4
    pack_small(small, gain_attn_in, gain_ff_in, offset_bucket, table)
    gain_attn, gain_ff = small[0:1, 0:width], small[1:2, 0:width]
    links = Links(send, recv)
    peers = [group.at(core), group.at(far), group.at(diag)]
    z_peers = []
    if exchange:
        z, y = group.dp // 2, lax.rem(group.dp, 2)
        line, order = line_order(z), z_order(z)
        y_peer = (2 * z + 1 - y, me)
        near_peer = (2 * order[2] + y, me)
        z_peers = [(2 * lax.rem(z + t, 4) + y, me) for t in (1, 2, 3)]
        peers += [y_peer] + z_peers
    else:
        line, order, y = [0, 1, 2, 3], [0, 1, 2, 3], 0

    def place(order, t):
        found = jnp.int32(order[3])
        for i in range(3):
            found = jnp.where(t == i, order[i], found)
        return found

    started = []

    def load(src, dst):
        copy = pltpu.make_async_copy(src, dst, local.at[len(started)])
        started.append(copy)
        return copy

    def depth_rows(i):
        return pl.ds(pl.multiple_of(i * depth, 16), depth)

    own = block_rows(me, rows)
    out_own = load(w_out, wu.at[depth_rows(me)])
    out_own.start()
    proj_loads = [load(w, wg.at[depth_rows(i)]) for i, w in enumerate((w_query, w_key, w_value))]
    for copy in proj_loads:
        copy.start()
    cot_own = load(cot_in, cot.at[own])
    cot_own.start()
    down_load = load(down_w, wd)
    down_load.start()
    greet(peers)

    x = tokens[...].astype(f32)
    normed[own, :] = (rms(x) * gain_attn).astype(bf16)
    gather = Gather(links, group, normed, rows, 2)
    gather.start()
    out_own.wait()
    parts = 4 if exchange else 1
    piece = depth // parts

    def out_rows(dev):
        start = dev * depth + (z * piece if exchange else 0)
        return pl.ds(pl.multiple_of(start, 16), piece)

    out_near = links.copy(wu.at[depth_rows(me)], wu.at[depth_rows(me)], group.at(core))
    out_far = links.copy(wu.at[out_rows(me)], wu.at[out_rows(me)], group.at(far))
    out_near.start()
    out_z = [links.copy(wu.at[out_rows(far)], wu.at[out_rows(far)], peer) for peer in z_peers]
    out_pass = links.copy(wu.at[depth_rows(far)], wu.at[depth_rows(far)], group.at(core))
    cot_gather = Gather(links, group, cot, rows, 4, source=cot_in)
    cot_gather.near.start()
    mixed_near = links.copy(mixed.at[block_rows(core, rows)], mixed_all.at[me], group.at(core))
    mixed_far = links.copy(mixed.at[block_rows(far, rows)], mixed_all.at[me], group.at(far))
    mixed_diag = links.copy(mixed.at[block_rows(diag, rows)], mixed_all.at[me], group.at(diag))

    build_strips(strip, small, buckets)
    for copy in proj_loads:
        copy.wait()

    def project(dev):
        at = block_rows(dev, rows)
        block = normed[at, :]
        for i in range(3):
            qkv[i, at, :] = contract_cols(block, wg[i * depth : (i + 1) * depth, :]).astype(bf16)

    project(me)
    gather.near.wait_recv()
    project(core)
    gather.forward(0)
    gather.forward(1)
    out_far.start()
    cot_gather.far[0].start()
    project(far)
    for copy in gather.passed:
        copy.wait_recv()
    normed_save = load(normed, normed_out)
    normed_save.start()
    project(diag)
    gate_load = load(gate_w, wg)
    gate_load.start()

    def attend(dev):
        at = block_rows(dev, rows)
        seen = visible_keys(dev, rows, length, first[0])
        mixed_sum[...] = jnp.zeros_like(mixed_sum)
        lse[at, :] = jnp.zeros((rows, 128), f32)

        def one_head(h, carry):
            query = qkv[0, at, :]
            lanes = head_lanes(query.shape, h)
            scores = contract_cols(jnp.where(lanes, query, jnp.zeros_like(query)), qkv[1])
            scores = jnp.where(seen, add_bias(scores, strip, h, dev, length), masked_score)
            top = jnp.max(scores, axis=-1, keepdims=True)
            expo = jnp.exp(scores - top)
            total = jnp.sum(expo, axis=-1, keepdims=True)
            weights = (expo * (1.0 / total)).astype(bf16)
            mixed_sum[...] = jnp.where(lanes, mm(weights, qkv[2]), mixed_sum[...])
            lane = lax.broadcasted_iota(jnp.int32, (rows, 128), 1)
            lse[at, :] = jnp.where(lane == h, top + jnp.log(total), lse[at, :])
            return carry

        lax.fori_loop(0, heads, one_head, 0)
        mixed[at, :] = mixed_sum[...].astype(bf16)

    attend(far)
    gather.wait_send()
    normed_save.wait()
    mixed_far.start()
    cot_gather.far[1].start()
    out_far.wait_recv()
    for copy in out_z:
        copy.start()
    attend(diag)
    mixed_diag.start()
    cot_gather.far[2].start()
    attend(core)
    mixed_near.start()
    cot_gather.far[3].start()
    for copy in out_z:
        copy.wait_recv()
    out_pass.start()
    cot_gather.forward(0)
    attend(me)
    mixed_all[me] = mixed[own, :]
    out_near.wait_recv()
    attn = mm(mixed_all[me], wu[depth_rows(me), :])
    mixed_near.wait_recv()
    attn = attn + mm(mixed_all[core], wu[depth_rows(core), :])
    mixed_far.wait_recv()
    attn = attn + mm(mixed_all[far], wu[depth_rows(far), :])
    mixed_diag.wait_recv()
    out_pass.wait_recv()
    attn = attn + mm(mixed_all[diag], wu[depth_rows(diag), :])
    residual = x + attn
    grad_h1[...] = residual
    normed[own, :] = (rms(residual) * gain_ff).astype(bf16)
    second = Gather(links, group, normed, rows, 2)
    second.near.start()
    for copy in second.far:
        copy.start()
    for copy in [out_near, out_far, out_pass] + out_z:
        copy.wait_send()
    up_load = load(up_w, wu)
    up_load.start()

    scatter = Scatter(links, group, tx, rx, rows, 2)
    ff_diag = links.copy(tx_ff.at[0], rx_ff.at[0], group.at(core))
    ff_near = links.copy(tx_ff.at[1], rx_ff.at[1], group.at(core))

    def pair(ref, start, after):
        return jnp.concatenate(
            [
                ref[pl.ds(pl.multiple_of(start, 128), half), :],
                ref[pl.ds(pl.multiple_of(after, 128), half), :],
            ],
            axis=0,
        )

    def keep(i, value):
        strip[i, :, 0:ff] = value[:half]
        strip[i, :, length : length + ff] = value[half:]

    def unit(start, after):
        block = pair(normed, start, after)
        keep(0, contract_cols(block, wg[...]))
        keep(1, contract_cols(block, wu[...]))
        keep(2, contract_cols(pair(cot, start, after), wd[...]))
        for offset, lane in ((start, 0), (after, length)):

            def act(i, carry):
                at = pl.ds(pl.multiple_of(i * 16, 16), 16)
                to = pl.ds(pl.multiple_of(offset + i * 16, 16), 16)
                v, u, g = (strip[k, at, lane : lane + ff] for k in range(3))
                square = v * v
                t = jnp.tanh(GELU_SLOPE * v * (1.0 + GELU_CUBE * square))
                lift = 0.5 * (1.0 + t)
                value = v * lift
                slope = lift + 0.5 * v * (1.0 - t * t) * (
                    GELU_SLOPE * (1.0 + 3.0 * GELU_CUBE * square)
                )
                hidden[to, :] = (value * u).astype(bf16)
                gate_act[to, :] = (g * u * slope).astype(bf16)
                up_act[to, :] = (g * value).astype(bf16)
                return carry

            lax.fori_loop(0, half // 16, act, 0)

    def terms(start, after):
        return mm(pair(gate_act, start, after), wg[...]) + mm(
            pair(up_act, start, after), wu[...]
        )

    def weight_block(order, left, right, store, t):
        at = pl.ds(pl.multiple_of(place(order, t) * part, 128), part)
        value = contract_rows(left[:, at], right[...]).astype(bf16)
        store(t, value[: part // 2], value[part // 2 :])

    def weight_blocks(order, left, right, store):
        def one(t, carry):
            weight_block(order, left, right, store, t)
            return carry

        lax.fori_loop(0, 4, one, 0)

    cot_own.wait()
    down_load.wait()
    gate_load.wait()
    up_load.wait()
    unit(me * rows, me * rows + half)
    cot_gather.forward(1)
    cot_gather.near.wait_recv()
    second.near.wait_recv()
    unit(core * rows, core * rows + half)
    second.forward(0)
    second.passed[0].wait_recv()
    for i in (0, 1):
        cot_gather.passed[i].wait_recv()
    unit(far * rows, diag * rows)
    both = terms(far * rows, diag * rows)
    scatter.send_diag(0, both[half:])
    far_terms[pl.ds(0, half), :] = both[:half]
    cot_gather.forward(2)
    cot_gather.forward(3)
    scatter.send_far(0, far_terms[pl.ds(0, half), :])
    second.forward(1)
    for i in (2, 3):
        cot_gather.passed[i].wait_recv()
    second.passed[1].wait_recv()
    unit(far * rows + half, diag * rows + half)

    base = links.used
    links.used += 8

    def y_copy(t):
        return pltpu.make_async_remote_copy(
            src_ref=down_grad.at[t, 1 - y],
            dst_ref=y_recv.at[t],
            send_sem=send.at[base + t],
            recv_sem=recv.at[base + t],
            device_id=y_peer,
            device_id_type=MESH,
        )

    def z_copy(i, side):
        return pltpu.make_async_remote_copy(
            src_ref=gate_grad.at[2 * i, side],
            dst_ref=z_recv.at[i, side],
            send_sem=send.at[base + 4 + 2 * i + side],
            recv_sem=recv.at[base + 4 + 2 * i + side],
            device_id=near_peer,
            device_id_type=MESH,
        )

    spots = len(started) + 1

    def save(src, dst, at):
        return pltpu.make_async_copy(src, dst, local.at[spots + at])

    results = []

    def keep_result(src, dst):
        results.append(save(src, dst, 12 + len(results)))
        results[-1].start()

    keep_result(qkv, qkv_out)
    keep_result(mixed, mixed_out)
    keep_result(lse, lse_out)

    def store_down(t, low, high):
        down_grad[t, 0] = low
        down_grad[t, 1] = high
        if exchange:
            y_copy(t).start()
        else:
            save(down_grad.at[t], down_out.at[t], t).start()

    def store_gate(t, low, high):
        gate_grad[t, 0] = low
        gate_grad[t, 1] = high
        if exchange:

            if t % 2 == 0:
                z_copy(t // 2, 0).start()
                z_copy(t // 2, 1).start()
        else:
            save(gate_grad.at[t], gate_out.at[t], 4 + t).start()

    def store_up(t, low, high):
        slot = lax.rem(t, 2)

        @pl.when(t >= 2)
        def _():
            save(up_grad.at[slot], up_out.at[t - 2], 8 + t - 2).wait()

        up_grad[slot, 0] = low
        up_grad[slot, 1] = high
        save(up_grad.at[slot], up_out.at[t], 8 + t).start()

    def down_block(t):
        weight_block(line, cot, hidden, store_down, t)

    def gate_block(t):
        weight_block(order, normed, gate_act, store_gate, t)

    down_block(0)
    gate_block(0)
    both = terms(far * rows + half, diag * rows + half)
    scatter.send_diag(1, both[half:])
    far_terms[pl.ds(half, half), :] = both[:half]
    scatter.send_near(terms(core * rows, core * rows + half))
    scatter.send_far(1, far_terms[pl.ds(half, half), :])
    for block in (1, 2):
        down_block(block)
    own_terms[...] = terms(me * rows, me * rows + half)
    gate_block(2)
    down_block(3)
    cot_gather.wait_send()
    for peer in (core, far):
        pl.semaphore_signal(free, inc=1, device_id=group.at(peer), device_id_type=MESH)
    residual = grad_h1[...]
    pulled, gain_part = norm_pull(residual, gain_ff, scatter.total(own_terms[...]))
    gain_grad[...] = gain_part
    own_terms[...] = residual
    grad = cot[own, :].astype(f32) + pulled
    grad_h1[...] = grad
    cot[own, :] = grad.astype(bf16)
    third = Gather(links, group, cot, rows, 2)
    pl.semaphore_wait(free, 2)
    third.start()
    keep_result(grad_h1, grad_h1_out)
    gate_block(1)
    gate_block(3)
    scatter.wait_send()
    out_again = pltpu.make_async_copy(w_out, tx.at[0, 0:depth], local.at[spots - 1])
    out_again.start()

    def ff_terms(dev):
        return mm(hidden[block_rows(dev, rows), :], wd[...])

    tx_ff[0] = ff_terms(diag).astype(bf16)
    ff_diag.start()
    tx_ff[1] = ff_terms(core).astype(bf16)
    ff_near.start()
    own_part = ff_terms(far)
    ff_diag.wait_recv()
    ff_far[...] = (own_part + rx_ff[0].astype(f32)).astype(bf16)
    keep_result(ff_far, ff_far_out)
    own_part = ff_terms(me)
    ff_near.wait_recv()
    own_terms[...] += own_part + rx_ff[1].astype(f32)
    keep_result(own_terms, own_terms_out)
    def mix_back(dev):
        at = block_rows(dev, rows)
        grad_mixed[at, :] = contract_cols(cot[at, :], tx[0, 0:depth, :]).astype(bf16)

    weight_blocks(line, normed, up_act, store_up)
    out_again.wait()
    mix_back(me)
    third.near.wait_recv()
    mix_back(core)
    third.forward(0)

    def sum_down(t):
        y_copy(t).wait_recv()
        down_grad[t, y] = (
            down_grad[t, y].astype(f32) + y_recv[t].astype(f32)
        ).astype(bf16)
        save(down_grad.at[t, y], down_out.at[t], t).start()

    def sum_gate(i):
        for side in range(2):
            z_copy(i, side).wait_recv()
            kept = gate_grad.at[2 * i + 1, side]
            kept[...] = (kept[...].astype(f32) + z_recv[i, side].astype(f32)).astype(bf16)
            save(kept, gate_out.at[i, side], 4 + 2 * i + side).start()

    if exchange:
        sum_down(0)
        sum_down(1)
        sum_gate(0)
        sum_down(2)
    third.forward(1)
    mix_back(far)
    for copy in third.passed:
        copy.wait_recv()
    mix_back(diag)

    def store_out(t, low, high):
        out_grad[t, 0] = low
        out_grad[t, 1] = high

    weight_blocks(line, cot, mixed, store_out)
    if exchange:
        sum_down(3)
        sum_gate(1)

    for t in range(4):
        if exchange:
            save(down_grad.at[t, y], down_out.at[t], t).wait()
            save(gate_grad.at[t // 2 * 2 + 1, t % 2], gate_out.at[t // 2, t % 2], 4 + t).wait()
            y_copy(t).wait_send()
            z_copy(t // 2, t % 2).wait_send()
        else:
            save(down_grad.at[t], down_out.at[t], t).wait()
            save(gate_grad.at[t], gate_out.at[t], 4 + t).wait()
        if t >= 2:
            save(up_grad.at[t % 2], up_out.at[t], 8 + t).wait()
    for copy in (mixed_near, mixed_far, mixed_diag):
        copy.wait_send()
    for copy in results:
        copy.wait()
    second.wait_send()
    third.wait_send()
    ff_diag.wait_send()
    ff_near.wait_send()


def in_vmem():
    return pl.BlockSpec(memory_space=pltpu.VMEM)


def anywhere():
    return pl.BlockSpec(memory_space=pl.ANY)


def in_smem():
    return pl.BlockSpec(memory_space=pltpu.SMEM)


def forward(exchange, tokens, gain_attn, gain_ff, offset_bucket, table, first, w_query, w_key, w_value, w_out, gate_w, up_w, down_w, cot):
    rows, width = tokens.shape
    length = 4 * rows
    cols = w_query.shape[0]
    ff = gate_w.shape[0]
    heads, buckets = table.shape
    part = width // 8
    shape = jax.ShapeDtypeStruct
    halves = (4, 2, part, ff)
    kept = [
        shape((3, length, cols), bf16),
        shape((length, cols), bf16),
        shape((length, 128), f32),
        shape((rows, width), bf16),
        shape((rows, width), f32),
        shape((rows, width), f32),
    ]
    return pl.pallas_call(
        functools.partial(forward_kernel, exchange, buckets),
        out_shape=(
            shape((length, cols), bf16),
            shape((4, 2, part, cols), bf16),
            shape((1, width), f32),
            shape((8, 2 * length), f32),
            *kept,
            shape((length, width), bf16),
            shape((4, part, ff) if exchange else halves, bf16),
            shape((2, 2, part, ff) if exchange else halves, bf16),
            shape(halves, bf16),
        ),
        in_specs=[in_vmem()] * 5 + [in_smem()] + [anywhere()] * 8,
        out_specs=[in_vmem()] * 4 + [anywhere()] * 10,
        scratch_shapes=[pltpu.VMEM(v.shape, v.dtype) for v in kept]
        + [
            pltpu.VMEM((length, width), bf16),
            pltpu.VMEM((length, width), bf16),
            pltpu.VMEM((ff, width), bf16),
            pltpu.VMEM((ff, width), bf16),
            pltpu.VMEM((ff, width), bf16),
            pltpu.VMEM((heads, 128, 2 * length), f32),
            pltpu.VMEM((length, ff), bf16),
            pltpu.VMEM((length, ff), bf16),
            pltpu.VMEM((length, ff), bf16),
            pltpu.VMEM((4, rows, cols), bf16),
            pltpu.VMEM((rows, cols), f32),
            pltpu.VMEM((rows, width), f32),
            pltpu.VMEM((3, rows, width), bf16),
            pltpu.VMEM((3, rows, width), bf16),
            pltpu.VMEM((2, rows, width), bf16),
            pltpu.VMEM((2, rows, width), bf16),
            pltpu.VMEM(halves, bf16),
            pltpu.VMEM(halves, bf16),
            pltpu.VMEM((2, 2, part, ff), bf16),
            pltpu.VMEM((4, part, ff) if exchange else (8, 128), bf16),
            pltpu.VMEM((2, 2, part, ff) if exchange else (8, 128), bf16),
            pltpu.SemaphoreType.DMA((56,)),
            pltpu.SemaphoreType.DMA((56,)),
            pltpu.SemaphoreType.DMA((32,)),
            pltpu.SemaphoreType.REGULAR,
        ],
        compiler_params=pltpu.CompilerParams(
            collective_id=0, has_side_effects=True, vmem_limit_bytes=VMEM_BYTES
        ),
    )(tokens, gain_attn, gain_ff, offset_bucket, table, first, w_query, w_key, w_value, w_out, gate_w, up_w, down_w, cot)


class Line:
    def __init__(self, links, dp, mp, own, y_recv, z_recv, sources=()):
        z, y = dp // 2, lax.rem(dp, 2)
        near = z + 1 - 2 * lax.rem(z, 2)
        self.own, self.y_recv, self.z_recv = own, y_recv, z_recv
        self.inner = (z == 1) | (z == 2)
        self.y_peer, self.near, self.across = (2 * z + 1 - y, mp), (2 * near + y, mp), (2 * lax.rem(z + 2, 4) + y, mp)
        self.middle = (2 * (3 - z) + y, mp)
        self.y_copies = [links.copy(src, y_recv.at[i], self.y_peer) for i, src in enumerate(sources)]
        base = links.used
        links.used += 5
        forth = jnp.where(self.inner, self.middle[0], self.near[0])
        step = jnp.where(self.inner, 3, 0)
        self.copies = [
            pltpu.make_async_remote_copy(
                src_ref=own.at[i],
                dst_ref=z_recv.at[slot],
                send_sem=links.send.at[base + i],
                recv_sem=links.recv.at[base + slot],
                device_id=(to, mp),
                device_id_type=MESH,
            )
            for i, (slot, to) in enumerate(((step, forth), (step + 1, forth), (2, self.near[0])))
        ]
        self.arrivals = [
            pltpu.make_async_remote_copy(
                src_ref=own.at[0],
                dst_ref=z_recv.at[slot],
                send_sem=links.send.at[base],
                recv_sem=links.recv.at[base + slot],
                device_id=self.near,
                device_id_type=MESH,
            )
            for slot in range(5)
        ]

    def add(self, i, other):
        self.own[i] = (self.own[i].astype(f32) + other.astype(f32)).astype(bf16)

    def begin(self, i):
        @pl.when(jnp.logical_not(self.inner))
        def _():
            self.copies[i].start()

    def take_y(self, i):
        self.y_copies[i].wait_recv()
        self.add(i, self.y_recv[i])
        if i < 3:
            self.begin(i)

    def relay(self, i):
        slot = (0, 1, 3)[i]

        @pl.when(self.inner)
        def _():
            self.arrivals[slot].wait_recv()
            self.add(i, self.z_recv[slot])
            self.copies[i].start()

    def total(self, out):
        self.arrivals[2].wait_recv()
        out[...] = self.own[3].astype(f32) + self.z_recv[2].astype(f32)

        @pl.when(self.inner)
        def _():
            self.arrivals[4].wait_recv()
            out[...] += self.z_recv[4].astype(f32)

    def wait_send(self):
        for copy in self.y_copies + self.copies:
            copy.wait_send()


class LastHalvings:
    def __init__(self, links, line, own, y_recv, z_recv, sources):
        self.own, self.y_recv, self.z_recv, self.inner = own, y_recv, z_recv, line.inner
        self.y_copies = [
            links.copy(src, y_recv.at[i], line.y_peer) for i, src in enumerate(sources)
        ]
        base = links.used
        links.used += 3

        def copy(i, src, slot, to):
            return pltpu.make_async_remote_copy(
                src_ref=src,
                dst_ref=z_recv.at[slot],
                send_sem=links.send.at[base + i],
                recv_sem=links.recv.at[base + slot],
                device_id=to,
                device_id_type=MESH,
            )

        mp = line.near[1]
        forth = (jnp.where(self.inner, line.middle[0], line.near[0]), mp)
        self.first = copy(0, own.at[0], jnp.where(self.inner, 1, 0), forth)
        self.inwards = copy(1, z_recv.at[0], 2, line.middle)
        self.outwards = copy(2, z_recv.at[1], 2, line.near)
        self.arrivals = [copy(0, own.at[0], slot, line.near) for slot in range(3)]

    def take_y(self, i):
        self.y_copies[i].wait_recv()
        self.own[i] = (self.own[i].astype(f32) + self.y_recv[i].astype(f32)).astype(bf16)
        if i == 0:
            self.first.start()

    def hand_on(self):
        @pl.when(self.inner)
        def _():
            self.arrivals[1].wait_recv()
            self.outwards.start()
            self.arrivals[0].wait_recv()
            self.inwards.start()

    def total(self):
        self.arrivals[2].wait_recv()
        return self.own[1].astype(f32) + self.z_recv[2].astype(f32)

    def wait_send(self):
        for copy in self.y_copies + [self.first]:
            copy.wait_send()

        @pl.when(self.inner)
        def _():
            self.outwards.wait_send()
            self.inwards.wait_send()


def back_kernel(
    exchange,
    buckets,
    small,
    qkv,
    lse,
    grad_mixed,
    out_grad,
    gain_ff_part,
    first,
    tokens_in,
    grad_h1_in,
    w_query_in,
    w_key_in,
    w_value_in,
    ff_base_in,
    normed_in,
    ff_far,
    down_in,
    gate_in,
    up_in,
    stats_out,
    attn_out,
    output,
    grad_input,
    gate_out,
    up_out,
    down_out,
    tokens,
    grad_h1,
    ff_base,
    w_query,
    w_key,
    w_value,
    gate_sum,
    up_sum,
    down_sum,
    normed,
    strip,
    strip_grad,
    key_head,
    value_head,
    query_sum,
    key_sum,
    value_sum,
    grad_qkv,
    own_terms,
    tx,
    rx,
    down_own,
    down_z,
    gate_own,
    gate_y,
    gate_z,
    up_own,
    up_y,
    up_z,
    attn_own,
    attn_send,
    attn_y,
    attn_z,
    attn_sum,
    ff_recv,
    stats,
    stats_recv,
    send,
    recv,
    local,
):
    group = Group()
    me, core, far, diag = group.me, group.core, group.far, group.diag
    rows, width = grad_h1.shape
    half = rows // 2
    length = 4 * rows
    part = width // 4
    heads = strip.shape[0]
    span = 2 * length
    links = Links(send, recv)
    dp = group.dp
    peers = [group.at(core), group.at(far)]
    copies = []

    def load(src, dst):
        copy = pltpu.make_async_copy(src, dst, local.at[len(copies)])
        copies.append(copy)
        return copy

    save_normed = load(normed_in, normed)
    late = [
        load(src, dst)
        for src, dst in (
            (tokens_in, tokens),
            (grad_h1_in, grad_h1),
            (ff_base_in, ff_base),
            (w_query_in, w_query),
            (w_key_in, w_key),
            (w_value_in, w_value),
        )
    ]
    if exchange:
        z, y = dp // 2, lax.rem(dp, 2)
        order = line_order(z)
        down = Line(links, dp, me, down_own, None, down_z)
        gate = LastHalvings(links, down, gate_own, gate_y, gate_z, [gate_in.at[i, 1 - y] for i in range(2)])
        up = Line(links, dp, me, up_own, up_y, up_z, [up_in.at[i, 1 - y] for i in range(4)])
        attn = Line(links, dp, me, attn_own, attn_y, attn_z, [attn_send.at[i] for i in range(4)])
        peers += [down.y_peer, down.near, down.across, down.middle]
        loads = [load(down_in.at[i], down_own.at[i]) for i in range(4)]
        gate_loads = [load(gate_in.at[i, y], gate_own.at[i]) for i in range(2)]
        up_loads = [load(up_in.at[i, y], up_own.at[i]) for i in range(4)]
        for copy in loads:
            copy.start()
    else:
        order = [0, 1, 2, 3]
    greet(peers)
    if exchange:
        for copy in gate.y_copies + up.y_copies:
            copy.start()
        for i in range(4):
            loads[i].wait()
            if i < 3:
                down.begin(i)
        for copy in gate_loads + up_loads:
            copy.start()
    for copy in [save_normed] + late:
        copy.start()
    scatter = Scatter(links, group, tx, rx, rows, 1)
    ff_copy = links.copy(ff_far, ff_recv, group.at(far))
    ff_copy.start()
    stages = []
    for i, to in enumerate(peers[2:5] + peers[:2]):
        stages.append(links.copy(stats.at[i], stats_recv.at[i], to))

    build_strips(strip, small, buckets)
    strip_grad[...] = jnp.zeros_like(strip_grad)
    query_sum[...] = jnp.zeros_like(query_sum)
    key_sum[...] = jnp.zeros_like(key_sum)
    value_sum[...] = jnp.zeros_like(value_sum)

    def attend_back(dev, h):
        at = block_rows(dev, rows)
        seen = visible_keys(dev, rows, length, first[0])
        query, grad = qkv[0, at, :], grad_mixed[at, :]
        lanes = head_lanes(query.shape, h)
        zero = jnp.zeros_like(query)
        scores = contract_cols(query, key_head[...])
        scores = jnp.where(seen, add_bias(scores, strip, h, dev, length), masked_score)
        probs = jnp.exp(scores - lse[at, h : h + 1])
        inner = contract_cols(grad, value_head[...])
        center = jnp.sum(probs * inner, axis=-1, keepdims=True)
        score_grad = (probs * (inner - center)).astype(bf16)
        query_sum[at, :] += mm(score_grad, key_head[...])
        key_sum[...] += contract_rows(score_grad, jnp.where(lanes, query, zero))
        value_sum[...] += contract_rows(probs.astype(bf16), jnp.where(lanes, grad, zero))
        count = length // 128
        for i in range(rows // 128):
            start = (count - 1 - i) * 128 - dev * rows
            to = pl.ds(pl.multiple_of(start, 128), length)
            strip_grad[h, :, to] += score_grad[i * 128 : (i + 1) * 128].astype(f32)

    def head_keys(h):
        key, value = qkv[1], qkv[2]
        lanes = head_lanes(key.shape, h)
        key_head[...] = jnp.where(lanes, key, jnp.zeros_like(key))
        value_head[...] = jnp.where(lanes, value, jnp.zeros_like(value))

    def take_gate(i):
        gate_loads[i].wait()
        gate.take_y(i)

    def take_up(i):
        up_loads[i].wait()
        up.take_y(i)

    def down_total():
        down.total(down_sum)
        save(down_sum, down_out)

    def gate_total():
        gate_sum[...] = gate.total()
        save(gate_sum, gate_out)

    head_keys(0)
    between = {
        (0, 1): [lambda: take_gate(0)],
        (0, 2): [lambda: down.relay(0)],
        (1, 2): [lambda: take_gate(1), lambda: down.relay(1)],
        (1, 3): [lambda: down.relay(2)],
        (2, 2): [lambda: take_up(0)],
    } if exchange else {}
    for h in range(heads):
        if h:
            head_keys(h)
        for j, dev in enumerate((diag, far, core, me)):
            attend_back(dev, h)
            for step in between.get((h, j), []):
                step()

    grad_qkv[0] = query_sum[...].astype(bf16)
    grad_qkv[1] = key_sum[...].astype(bf16)
    grad_qkv[2] = value_sum[...].astype(bf16)

    def terms(dev):
        at = block_rows(dev, rows)
        return (
            mm(grad_qkv[0, at, :], w_query[...])
            + mm(grad_qkv[1, at, :], w_key[...])
            + mm(grad_qkv[2, at, :], w_value[...])
        )

    gain_parts = []

    def gain_terms(dev):
        value = terms(dev)
        product = value * normed[block_rows(dev, rows), :].astype(f32)
        gain_parts.append(jnp.sum(product, axis=0, keepdims=True))
        return value

    for copy in [save_normed] + late:
        copy.wait()
    saves = []

    def save(src, dst):
        saves.append(load(src, dst))
        saves[-1].start()

    scatter.send_diag(0, gain_terms(diag))
    scatter.send_near(gain_terms(core))
    scatter.send_far(0, gain_terms(far))
    own_terms[...] = gain_terms(me)

    index = small[2:3, :]
    lines = []
    for h in range(heads):
        fold = strip_grad[h]
        count = 128
        while count > 1:
            count //= 2
            fold = fold[:count] + pltpu.roll(fold[count:], span - count, 1)
        lines.append(pltpu.roll(fold, 127, 1))
    diagonals = jnp.concatenate(lines + [jnp.zeros((8 - heads, span), f32)], axis=0)
    onehot = (lax.broadcasted_iota(jnp.int32, (buckets, span), 0).astype(f32) == index).astype(f32)
    table_part = lax.dot_general(
        diagonals, onehot, (((1,), (1,)), ((), ())), precision=highest, preferred_element_type=f32
    )
    stats[0] = jnp.zeros_like(stats[0])
    stats[0, 0:1, :] = (gain_parts[0] + gain_parts[1] + gain_parts[2] + gain_parts[3]) / small[0:1, 0:width]
    stats[0, 1:2, :] = gain_ff_part[...]
    stats[0, 2 : 2 + heads, 0:buckets] = table_part[0:heads]
    stages[0].start()
    dp_stages = len(stages) - 2

    def next_stage(i):
        stages[i].wait_recv()
        total = stats[i] + stats_recv[i]
        if i >= dp_stages:
            row = lax.broadcasted_iota(jnp.int32, total.shape, 0)
            total = jnp.where(row < 2, total, stats[i])
        if i + 1 < len(stages):
            stats[i + 1] = total
            stages[i + 1].start()
        else:
            stats_out[...] = total

    cols = w_query.shape[0]
    for i in range(4):
        at = pl.ds(pl.multiple_of(order[i] * part, 128), part)
        for m in range(3):
            block = contract_rows(normed[:, at], grad_qkv[m]).astype(bf16)
            if exchange:
                low, high = block[: part // 2], block[part // 2 :]
                lanes = slice(m * cols, (m + 1) * cols)
                attn_send[i, :, lanes] = jnp.where(y == 0, high, low)
                attn_own[i, :, lanes] = jnp.where(y == 0, low, high)
            else:
                attn_out[m, at, :] = block
        if exchange:
            attn_send[i, :, 3 * cols :] = out_grad[i, 1 - y]
            attn_own[i, :, 3 * cols :] = out_grad[i, y]
            attn.y_copies[i].start()
        else:
            for side in range(2):
                attn_out[3, pl.ds(i * part + side * part // 2, part // 2), :] = out_grad[i, side]

    if exchange:
        take_up(1)
        down_total()
        gate.hand_on()
    ff_copy.wait_recv()
    ff_recv[...] = (ff_base[...] + ff_recv[...].astype(f32)).astype(bf16)
    save(ff_recv, output)

    def input_total():
        pulled, _ = norm_pull(tokens[...].astype(f32), small[0:1, 0:width], scatter.total(own_terms[...]))
        grad_h1[...] += pulled
        save(grad_h1, grad_input)

    if exchange:
        up.relay(0)
        take_up(2)
        take_up(3)
        next_stage(0)
        up.relay(1)
        attn.take_y(0)
        gate_total()
        input_total()
        up.relay(2)
        next_stage(1)
        attn.take_y(1)
        attn.relay(0)
        up.total(up_sum)
        save(up_sum, up_out)
        attn.take_y(2)
        attn.relay(1)
        attn.relay(2)
        next_stage(2)
        attn.take_y(3)
        next_stage(3)
        next_stage(4)
        attn.total(attn_sum)
        for m in range(3):
            attn_out[m] = attn_sum[:, m * cols : (m + 1) * cols]
        attn_out[3] = attn_sum[:, 3 * cols :].T
        down.wait_send()
        gate.wait_send()
        up.wait_send()
        attn.wait_send()
    else:
        input_total()
        next_stage(0)
        next_stage(1)
    for copy in saves:
        copy.wait()
    ff_copy.wait_send()
    scatter.wait_send()
    for stage in stages:
        stage.wait_send()


def attention_backward(
    exchange, table_shape, tokens, small, grad_h1, qkv, lse, w_query, w_key, w_value, grad_mixed, out_grad,
    gain_ff_part, ff_base, first, normed, ff_far, down_in, gate_in, up_in,
):
    rows, width = grad_h1.shape
    length = 4 * rows
    cols = w_query.shape[0]
    ff = down_in.shape[-1]
    buckets, heads = table_shape
    part = width // 8
    shape = jax.ShapeDtypeStruct
    ff_scratch = pltpu.VMEM((part, ff) if exchange else (8, 128), f32)
    scratch = [
        pltpu.VMEM((rows, width), bf16),
        pltpu.VMEM((rows, width), f32),
        pltpu.VMEM((rows, width), f32),
        pltpu.VMEM((cols, width), bf16),
        pltpu.VMEM((cols, width), bf16),
        pltpu.VMEM((cols, width), bf16),
        ff_scratch,
        ff_scratch,
        ff_scratch,
        pltpu.VMEM((length, width), bf16),
        pltpu.VMEM((heads, 128, 2 * length), f32),
        pltpu.VMEM((heads, 128, 2 * length), f32),
        pltpu.VMEM((length, cols), bf16),
        pltpu.VMEM((length, cols), bf16),
        pltpu.VMEM((length, cols), f32),
        pltpu.VMEM((length, cols), f32),
        pltpu.VMEM((length, cols), f32),
        pltpu.VMEM((3, length, cols), bf16),
        pltpu.VMEM((rows, width), f32),
        pltpu.VMEM((3, rows, width), bf16),
        pltpu.VMEM((3, rows, width), bf16),
    ]
    for count in (4, 5, 2, 2, 3, 4, 4, 5):
        scratch.append(pltpu.VMEM((count, part, ff) if exchange else (8, 128), bf16))
    for count in (4, 4, 4, 5):
        scratch.append(pltpu.VMEM((count, part, 4 * cols) if exchange else (8, 128), bf16))
    stages = 5 if exchange else 2
    scratch += [
        pltpu.VMEM((part, 4 * cols), f32),
        pltpu.VMEM((rows, width), bf16),
        pltpu.VMEM((stages, 8, width), f32),
        pltpu.VMEM((stages, 8, width), f32),
        pltpu.SemaphoreType.DMA((48,)),
        pltpu.SemaphoreType.DMA((48,)),
        pltpu.SemaphoreType.DMA((24,)),
    ]
    ff_out = shape((part, ff) if exchange else (8, 128), f32)
    return pl.pallas_call(
        functools.partial(back_kernel, exchange, buckets),
        out_shape=(
            shape((8, width), f32),
            shape((4, part, cols), f32) if exchange else shape((4, width, cols), bf16),
            shape((rows, width), bf16),
            shape((rows, width), f32),
            ff_out,
            ff_out,
            ff_out,
        ),
        in_specs=[in_vmem()] * 6 + [in_smem()] + [anywhere()] * 11,
        out_specs=[in_vmem()] * 2 + [anywhere()] * 5,
        scratch_shapes=scratch,
        compiler_params=pltpu.CompilerParams(
            collective_id=1, has_side_effects=True, vmem_limit_bytes=VMEM_BYTES
        ),
    )(
        small, qkv, lse, grad_mixed, out_grad, gain_ff_part, first, tokens, grad_h1, w_query, w_key, w_value,
        ff_base, normed, ff_far, down_in, gate_in, up_in,
    )


def finish_kernel(heads, *refs):
    ins, outs, (attn_held, *held, load, save) = refs[:7], refs[7:19], refs[19:]
    stats, attn = ins[0], ins[1]
    sources = list(ins[2:]) + [attn.at[i] for i in range(4)]
    slots = held + [attn_held.at[i] for i in range(4)]
    targets = list(outs[4:9]) + list(outs[:4])
    loads = [pltpu.make_async_copy(a, b, load.at[i]) for i, (a, b) in enumerate(zip(sources, slots))]
    saves = [pltpu.make_async_copy(a, b, save.at[i]) for i, (a, b) in enumerate(zip(slots, targets))]
    for copy in loads:
        copy.start()
    gain_attn, gain_ff, table = outs[9:]
    gain_attn[...] = stats[0]
    gain_ff[...] = stats[1]
    table[...] = stats[2 : 2 + heads, 0 : table.shape[1]]
    for before, after in zip(loads, saves):
        before.wait()
        after.start()
    for copy in saves:
        copy.wait()


def finish(table_shape, stats, attn, *whole):
    buckets, heads = table_shape
    shape = jax.ShapeDtypeStruct
    outs = [shape(attn.shape[1:], f32)] * 4 + [shape(v.shape, v.dtype) for v in whole]
    small = [shape(stats.shape[1:], f32)] * 2 + [shape((heads, buckets), f32)]
    return pl.pallas_call(
        functools.partial(finish_kernel, heads),
        out_shape=outs + small,
        in_specs=[in_vmem()] + [anywhere()] * 6,
        out_specs=[anywhere()] * 9 + [in_vmem()] * 3,
        scratch_shapes=[pltpu.VMEM(v.shape, v.dtype) for v in (attn, *whole)]
        + [pltpu.SemaphoreType.DMA((9,))] * 2,
        compiler_params=pltpu.CompilerParams(vmem_limit_bytes=VMEM_BYTES),
    )(stats, attn, *whole)


def shards(
    tokens,
    gain_attn,
    w_query,
    w_key,
    w_value,
    w_out,
    bias_table,
    gain_ff,
    w_gate,
    w_up,
    w_down,
    cotangent,
    first_length,
    offset_bucket,
):
    n_dp = lax.axis_size("dp")
    exchange = n_dp == 8
    buckets, heads = bias_table.shape
    width = tokens.shape[1]
    turned = [w_query.T, w_key.T, w_value.T]
    grad_mixed, out_grad, gain_ff_part, small, qkv, mixed, lse, ff_far, ff_base, grad_h1, normed, down, gate, up = forward(
        exchange, tokens, gain_attn, gain_ff, offset_bucket, bias_table.T, first_length, *turned, w_out, w_gate.T, w_up.T, w_down, cotangent
    )
    stats, attn, output, grad_input, gate_sum, up_sum, down_sum = attention_backward(
        exchange, bias_table.shape, tokens, small, grad_h1, qkv, lse, *turned, grad_mixed, out_grad, gain_ff_part,
        ff_base, first_length, normed, ff_far, down, gate, up,
    )
    if exchange:
        *attn, output, grad_input, gate_sum, up_sum, down_sum, gain_first, gain_second, table = finish(
            bias_table.shape, stats, attn, output, grad_input, gate_sum, up_sum, down_sum
        )
    else:
        def scatter(value):
            value = value.reshape(width, -1).astype(f32)
            return lax.psum_scatter(value, "dp", scatter_dimension=0, tiled=True)

        stats = lax.psum(stats, "dp")
        gate_sum, up_sum, down_sum = scatter(gate), scatter(up), scatter(down)
        attn = [scatter(attn[i]) for i in range(4)]
        attn[3] = attn[3].T
        gain_first, gain_second, table = stats[0], stats[1], stats[2 : 2 + heads, :buckets]
    return (
        output,
        grad_input,
        gain_first,
        attn[0],
        attn[1],
        attn[2],
        attn[3],
        table.T,
        gain_second,
        gate_sum,
        up_sum,
        down_sum.T,
    )


def solution(mesh):
    placed = (
        P(("dp", "mp"), None),
        P(),
        P(None, "mp"),
        P(None, "mp"),
        P(None, "mp"),
        P("mp", None),
        P(None, "mp"),
        P(),
        P(None, "mp"),
        P(None, "mp"),
        P("mp", None),
        P(("dp", "mp"), None),
        P("dp"),
        P(),
    )
    return jax.shard_map(
        shards,
        mesh=mesh,
        in_specs=placed,
        out_specs=(
            P(("dp", "mp"), None),
            P(("dp", "mp"), None),
            P(),
            P("dp", "mp"),
            P("dp", "mp"),
            P("dp", "mp"),
            P("mp", "dp"),
            P(None, "mp"),
            P(),
            P("dp", "mp"),
            P("dp", "mp"),
            P("mp", "dp"),
        ),
        check_vma=False,
    )
```

```python
import functools

import jax
import jax.numpy as jnp
from jax import lax
from jax.experimental import pallas as pl
from jax.experimental.pallas import tpu as pltpu
from jax.sharding import PartitionSpec as P

MESH = pl.DeviceIdType.MESH
DH = 64
epsilon = 1e-06
masked_score = -1000000000.0
highest = lax.Precision.HIGHEST
bf16 = jnp.bfloat16
f32 = jnp.float32
VMEM_BYTES = 62 * 2**20


def mm(left, right):
    return jnp.dot(left, right, preferred_element_type=f32)


def contract_rows(left, right):
    return lax.dot_general(left, right, (((0,), (0,)), ((), ())), preferred_element_type=f32)


def contract_cols(left, right):
    return lax.dot_general(left, right, (((1,), (1,)), ((), ())), preferred_element_type=f32)


def rms(values):
    return values * lax.rsqrt(jnp.mean(values * values, axis=-1, keepdims=True) + epsilon)


class Links:
    def __init__(self, send, recv):
        self.send, self.recv, self.used = send, recv, 0

    def copy(self, src, dst, to):
        at = self.used
        self.used += 1
        return pltpu.make_async_remote_copy(
            src_ref=src,
            dst_ref=dst,
            send_sem=self.send.at[at],
            recv_sem=self.recv.at[at],
            device_id=to,
            device_id_type=MESH,
        )


class Group:
    def __init__(self):
        self.dp, self.me = lax.axis_index("dp"), lax.axis_index("mp")
        self.core = self.me + 1 - 2 * lax.rem(self.me, 2)
        self.far = lax.rem(self.me + 2, 4)
        self.diag = 3 - self.me

    def at(self, mp):
        return (self.dp, mp)


def greet(peers):
    barrier = pltpu.get_barrier_semaphore()
    for peer in peers:
        pl.semaphore_signal(barrier, inc=1, device_id=peer, device_id_type=MESH)


def meet(peers):
    pl.semaphore_wait(pltpu.get_barrier_semaphore(), len(peers))


def block_rows(dev, rows, start=0, size=None):
    return pl.ds(pl.multiple_of(dev * rows + start, 16), rows if size is None else size)


class Gather:
    def __init__(self, links, group, full, rows, chunks, source=None):
        size = rows // chunks
        own = block_rows(group.me, rows)
        self.near = links.copy(full.at[own] if source is None else source, full.at[own], group.at(group.core))
        self.far, self.passed = [], []
        for i in range(chunks):
            mine = block_rows(group.me, rows, i * size, size)
            theirs = block_rows(group.far, rows, i * size, size)
            src = full.at[mine] if source is None else source.at[pl.ds(i * size, size)]
            self.far.append(links.copy(src, full.at[mine], group.at(group.far)))
            self.passed.append(links.copy(full.at[theirs], full.at[theirs], group.at(group.core)))

    def start(self):
        self.near.start()
        for copy in self.far:
            copy.start()

    def forward(self, i):
        self.far[i].wait_recv()
        self.passed[i].start()

    def wait_send(self):
        self.near.wait_send()
        for copy in self.far + self.passed:
            copy.wait_send()


def pack_small(small, gain_attn, gain_ff, offset_bucket, table):
    width, offsets = gain_attn.shape[0], offset_bucket.shape[0]
    heads, buckets = table.shape
    small[...] = jnp.full(small.shape, -1.0, f32)
    small[0:1, 0:width] = gain_attn[...].reshape(1, width)
    small[1:2, 0:width] = gain_ff[...].reshape(1, width)
    small[2:3, 0:offsets] = offset_bucket[...].astype(f32).reshape(1, offsets)
    small[3 : 3 + heads, 0:buckets] = table[...]


def build_strips(strip, small, buckets):
    index = small[2:3, :]
    heads, _, width = strip.shape
    for h in range(heads):
        row = jnp.zeros(index.shape, f32)
        for b in range(buckets):
            row = jnp.where(index == float(b), small[3 + h : 4 + h, b : b + 1], row)
        strip[h] = pltpu.roll(
            jnp.broadcast_to(row, (128, width)), width - 127, 1, stride=1, stride_axis=0
        )


def add_bias(scores, strip, h, dev, length):
    parts = []
    count = length // 128
    for i in range(scores.shape[0] // 128):
        first = (count - 1 - i) * 128 - dev * scores.shape[0]
        parts.append(
            scores[i * 128 : (i + 1) * 128]
            + strip[h, :, pl.ds(pl.multiple_of(first, 128), length)]
        )
    return jnp.concatenate(parts, axis=0)


def visible_keys(dev, rows, length, first):
    key = lax.broadcasted_iota(jnp.int32, (1, length), 1)
    return (key >= first) == (dev * rows >= first)


def head_lanes(shape, h):
    lane = lax.broadcasted_iota(jnp.int32, shape, len(shape) - 1)
    return (lane >= h * DH) & (lane < (h + 1) * DH)


def norm_pull(values, gain, grad):
    inverse = lax.rsqrt(jnp.mean(values * values, axis=-1, keepdims=True) + epsilon)
    scaled = grad * gain
    along = jnp.mean(values * scaled, axis=-1, keepdims=True)
    gain_grad = jnp.sum(grad * values * inverse, axis=0, keepdims=True)
    return inverse * scaled - values * (along * inverse * inverse * inverse), gain_grad


class Scatter:
    def __init__(self, links, group, tx, rx, rows, parts):
        self.tx, self.rx, self.size = tx, rx, rows // parts
        core, far = group.at(group.core), group.at(group.far)
        self.near = links.copy(tx.at[2], rx.at[2], core)
        self.diag, self.far = [], []
        for i in range(parts):
            at = pl.ds(i * self.size, self.size)
            self.diag.append(links.copy(tx.at[0, at], rx.at[0, at], core))
            self.far.append(links.copy(tx.at[1, at], rx.at[1, at], far))

    def send_diag(self, i, terms):
        self.tx[0, pl.ds(i * self.size, self.size), :] = terms.astype(bf16)
        self.diag[i].start()

    def send_near(self, terms):
        self.tx[2] = terms.astype(bf16)
        self.near.start()

    def send_far(self, i, terms):
        at = pl.ds(i * self.size, self.size)
        self.diag[i].wait_recv()
        self.tx[1, at, :] = (terms + self.rx[0, at, :].astype(f32)).astype(bf16)
        self.far[i].start()

    def total(self, own):
        self.near.wait_recv()
        for copy in self.far:
            copy.wait_recv()
        return own + self.rx[2].astype(f32) + self.rx[1].astype(f32)

    def wait_send(self):
        for copy in [self.near] + self.diag + self.far:
            copy.wait_send()


GELU_SLOPE = 0.7978845608028654
GELU_CUBE = 0.044715


def z_order(z):
    near = z + 1 - 2 * lax.rem(z, 2)
    return [lax.rem(near + 2, 4), lax.rem(z + 2, 4), near, z]


def line_order(z):
    return [
        jnp.where(z < 2, 3, 0),
        jnp.where(z < 2, 2, 1),
        jnp.where(z == 0, 1, jnp.where(z == 1, 0, jnp.where(z == 2, 3, 2))),
        z,
    ]


def forward_kernel(
    exchange,
    buckets,
    tokens,
    gain_attn_in,
    gain_ff_in,
    offset_bucket,
    table,
    first,
    w_query,
    w_key,
    w_value,
    w_out,
    gate_w,
    up_w,
    down_w,
    cot_in,
    grad_mixed,
    out_grad,
    gain_grad,
    small,
    qkv_out,
    mixed_out,
    lse_out,
    ff_far_out,
    own_terms_out,
    grad_h1_out,
    normed_out,
    down_out,
    gate_out,
    up_out,
    qkv,
    mixed,
    lse,
    ff_far,
    own_terms,
    grad_h1,
    normed,
    cot,
    wg,
    wu,
    wd,
    strip,
    hidden,
    gate_act,
    up_act,
    mixed_all,
    mixed_sum,
    far_terms,
    tx,
    rx,
    tx_ff,
    rx_ff,
    down_grad,
    gate_grad,
    up_grad,
    y_recv,
    z_recv,
    send,
    recv,
    local,
    free,
):
    group = Group()
    me, core, far, diag = group.me, group.core, group.far, group.diag
    rows, width = tokens.shape
    half = rows // 2
    length = 4 * rows
    heads = strip.shape[0]
    depth = w_out.shape[0]
    ff = wg.shape[0]
    part = width // 4
    links = Links(send, recv)
    peers = [group.at(core), group.at(far), group.at(diag)]
    z_peers = []
    if exchange:
        z, y = group.dp // 2, lax.rem(group.dp, 2)
        line, order = line_order(z), z_order(z)
        y_peer = (2 * z + 1 - y, me)
        near_peer = (2 * order[2] + y, me)
        z_peers = [(2 * lax.rem(z + t, 4) + y, me) for t in (1, 2, 3)]
        peers += [y_peer] + z_peers
    else:
        line, order, y = [0, 1, 2, 3], [0, 1, 2, 3], 0
    greet(peers)

    def place(order, t):
        found = jnp.int32(order[3])
        for i in range(3):
            found = jnp.where(t == i, order[i], found)
        return found

    started = []

    def load(src, dst):
        copy = pltpu.make_async_copy(src, dst, local.at[len(started)])
        started.append(copy)
        return copy

    def depth_rows(i):
        return pl.ds(pl.multiple_of(i * depth, 16), depth)

    own = block_rows(me, rows)
    out_own = load(w_out, wu.at[depth_rows(me)])
    out_own.start()
    proj_loads = [load(w, wg.at[depth_rows(i)]) for i, w in enumerate((w_query, w_key, w_value))]
    for copy in proj_loads:
        copy.start()
    cot_own = load(cot_in, cot.at[own])
    cot_own.start()
    down_load = load(down_w, wd)
    down_load.start()
    pack_small(small, gain_attn_in, gain_ff_in, offset_bucket, table)
    gain_attn, gain_ff = small[0:1, 0:width], small[1:2, 0:width]
    x = tokens[...].astype(f32)
    normed[own, :] = (rms(x) * gain_attn).astype(bf16)
    meet(peers)
    gather = Gather(links, group, normed, rows, 2)
    gather.start()
    out_own.wait()
    parts = 4 if exchange else 1
    piece = depth // parts

    def out_rows(dev):
        start = dev * depth + (z * piece if exchange else 0)
        return pl.ds(pl.multiple_of(start, 16), piece)

    out_near = links.copy(wu.at[depth_rows(me)], wu.at[depth_rows(me)], group.at(core))
    out_far = links.copy(wu.at[out_rows(me)], wu.at[out_rows(me)], group.at(far))
    out_near.start()
    out_z = [links.copy(wu.at[out_rows(far)], wu.at[out_rows(far)], peer) for peer in z_peers]
    out_pass = links.copy(wu.at[depth_rows(far)], wu.at[depth_rows(far)], group.at(core))
    cot_gather = Gather(links, group, cot, rows, 4, source=cot_in)
    cot_gather.near.start()
    mixed_near = links.copy(mixed.at[block_rows(core, rows)], mixed_all.at[me], group.at(core))
    mixed_far = links.copy(mixed.at[block_rows(far, rows)], mixed_all.at[me], group.at(far))
    mixed_diag = links.copy(mixed.at[block_rows(diag, rows)], mixed_all.at[me], group.at(diag))

    build_strips(strip, small, buckets)
    for copy in proj_loads:
        copy.wait()

    def project(dev):
        at = block_rows(dev, rows)
        block = normed[at, :]
        for i in range(3):
            qkv[i, at, :] = contract_cols(block, wg[i * depth : (i + 1) * depth, :]).astype(bf16)

    project(me)
    gather.near.wait_recv()
    project(core)
    gather.forward(0)
    gather.forward(1)
    out_far.start()
    cot_gather.far[0].start()
    project(far)
    for copy in gather.passed:
        copy.wait_recv()
    normed_save = load(normed, normed_out)
    normed_save.start()
    project(diag)
    gate_load = load(gate_w, wg)
    gate_load.start()

    def attend(dev):
        at = block_rows(dev, rows)
        seen = visible_keys(dev, rows, length, first[0])
        mixed_sum[...] = jnp.zeros_like(mixed_sum)
        lse[at, :] = jnp.zeros((rows, 128), f32)

        def one_head(h, carry):
            query = qkv[0, at, :]
            lanes = head_lanes(query.shape, h)
            scores = contract_cols(jnp.where(lanes, query, jnp.zeros_like(query)), qkv[1])
            scores = jnp.where(seen, add_bias(scores, strip, h, dev, length), masked_score)
            top = jnp.max(scores, axis=-1, keepdims=True)
            expo = jnp.exp(scores - top)
            total = jnp.sum(expo, axis=-1, keepdims=True)
            weights = (expo * (1.0 / total)).astype(bf16)
            mixed_sum[...] = jnp.where(lanes, mm(weights, qkv[2]), mixed_sum[...])
            lane = lax.broadcasted_iota(jnp.int32, (rows, 128), 1)
            lse[at, :] = jnp.where(lane == h, top + jnp.log(total), lse[at, :])
            return carry

        lax.fori_loop(0, heads, one_head, 0)
        mixed[at, :] = mixed_sum[...].astype(bf16)

    attend(far)
    gather.wait_send()
    normed_save.wait()
    mixed_far.start()
    cot_gather.far[1].start()
    out_far.wait_recv()
    for copy in out_z:
        copy.start()
    attend(diag)
    mixed_diag.start()
    cot_gather.far[2].start()
    attend(core)
    mixed_near.start()
    cot_gather.far[3].start()
    for copy in out_z:
        copy.wait_recv()
    out_pass.start()
    cot_gather.forward(0)
    attend(me)
    mixed_all[me] = mixed[own, :]
    out_near.wait_recv()
    attn = mm(mixed_all[me], wu[depth_rows(me), :])
    mixed_near.wait_recv()
    attn = attn + mm(mixed_all[core], wu[depth_rows(core), :])
    mixed_far.wait_recv()
    attn = attn + mm(mixed_all[far], wu[depth_rows(far), :])
    mixed_diag.wait_recv()
    out_pass.wait_recv()
    attn = attn + mm(mixed_all[diag], wu[depth_rows(diag), :])
    residual = x + attn
    grad_h1[...] = residual
    normed[own, :] = (rms(residual) * gain_ff).astype(bf16)
    second = Gather(links, group, normed, rows, 2)
    second.near.start()
    for copy in second.far:
        copy.start()
    for copy in [out_near, out_far, out_pass] + out_z:
        copy.wait_send()
    up_load = load(up_w, wu)
    up_load.start()

    scatter = Scatter(links, group, tx, rx, rows, 2)
    ff_diag = links.copy(tx_ff.at[0], rx_ff.at[0], group.at(core))
    ff_near = links.copy(tx_ff.at[1], rx_ff.at[1], group.at(core))

    def pair(ref, start, after):
        return jnp.concatenate(
            [
                ref[pl.ds(pl.multiple_of(start, 128), half), :],
                ref[pl.ds(pl.multiple_of(after, 128), half), :],
            ],
            axis=0,
        )

    def keep(i, value):
        strip[i, :, 0:ff] = value[:half]
        strip[i, :, length : length + ff] = value[half:]

    def unit(start, after):
        block = pair(normed, start, after)
        keep(0, contract_cols(block, wg[...]))
        keep(1, contract_cols(block, wu[...]))
        keep(2, contract_cols(pair(cot, start, after), wd[...]))
        for offset, lane in ((start, 0), (after, length)):

            def act(i, carry):
                at = pl.ds(pl.multiple_of(i * 16, 16), 16)
                to = pl.ds(pl.multiple_of(offset + i * 16, 16), 16)
                v, u, g = (strip[k, at, lane : lane + ff] for k in range(3))
                square = v * v
                t = jnp.tanh(GELU_SLOPE * v * (1.0 + GELU_CUBE * square))
                lift = 0.5 * (1.0 + t)
                value = v * lift
                slope = lift + 0.5 * v * (1.0 - t * t) * (
                    GELU_SLOPE * (1.0 + 3.0 * GELU_CUBE * square)
                )
                hidden[to, :] = (value * u).astype(bf16)
                gate_act[to, :] = (g * u * slope).astype(bf16)
                up_act[to, :] = (g * value).astype(bf16)
                return carry

            lax.fori_loop(0, half // 16, act, 0)

    def terms(start, after):
        return mm(pair(gate_act, start, after), wg[...]) + mm(
            pair(up_act, start, after), wu[...]
        )

    def weight_block(order, left, right, store, t):
        at = pl.ds(pl.multiple_of(place(order, t) * part, 128), part)
        value = contract_rows(left[:, at], right[...]).astype(bf16)
        store(t, value[: part // 2], value[part // 2 :])

    def weight_blocks(order, left, right, store):
        def one(t, carry):
            weight_block(order, left, right, store, t)
            return carry

        lax.fori_loop(0, 4, one, 0)

    cot_own.wait()
    down_load.wait()
    gate_load.wait()
    up_load.wait()
    unit(me * rows, me * rows + half)
    cot_gather.forward(1)
    cot_gather.near.wait_recv()
    second.near.wait_recv()
    unit(core * rows, core * rows + half)
    second.forward(0)
    second.passed[0].wait_recv()
    for i in (0, 1):
        cot_gather.passed[i].wait_recv()
    unit(far * rows, diag * rows)
    both = terms(far * rows, diag * rows)
    scatter.send_diag(0, both[half:])
    far_terms[pl.ds(0, half), :] = both[:half]
    cot_gather.forward(2)
    cot_gather.forward(3)
    scatter.send_far(0, far_terms[pl.ds(0, half), :])
    second.forward(1)
    for i in (2, 3):
        cot_gather.passed[i].wait_recv()
    second.passed[1].wait_recv()
    unit(far * rows + half, diag * rows + half)

    base = links.used
    links.used += 8

    def y_copy(t):
        return pltpu.make_async_remote_copy(
            src_ref=down_grad.at[t, 1 - y],
            dst_ref=y_recv.at[t],
            send_sem=send.at[base + t],
            recv_sem=recv.at[base + t],
            device_id=y_peer,
            device_id_type=MESH,
        )

    def z_copy(i, side):
        return pltpu.make_async_remote_copy(
            src_ref=gate_grad.at[2 * i, side],
            dst_ref=z_recv.at[i, side],
            send_sem=send.at[base + 4 + 2 * i + side],
            recv_sem=recv.at[base + 4 + 2 * i + side],
            device_id=near_peer,
            device_id_type=MESH,
        )

    spots = len(started) + 1

    def save(src, dst, at):
        return pltpu.make_async_copy(src, dst, local.at[spots + at])

    results = []

    def keep_result(src, dst):
        results.append(save(src, dst, 12 + len(results)))
        results[-1].start()

    keep_result(qkv, qkv_out)
    keep_result(mixed, mixed_out)
    keep_result(lse, lse_out)

    def store_down(t, low, high):
        down_grad[t, 0] = low
        down_grad[t, 1] = high
        if exchange:
            y_copy(t).start()
        else:
            save(down_grad.at[t], down_out.at[t], t).start()

    def store_gate(t, low, high):
        gate_grad[t, 0] = low
        gate_grad[t, 1] = high
        if exchange:

            if t % 2 == 0:
                z_copy(t // 2, 0).start()
                z_copy(t // 2, 1).start()
        else:
            save(gate_grad.at[t], gate_out.at[t], 4 + t).start()

    def store_up(t, low, high):
        slot = lax.rem(t, 2)

        @pl.when(t >= 2)
        def _():
            save(up_grad.at[slot], up_out.at[t - 2], 8 + t - 2).wait()

        up_grad[slot, 0] = low
        up_grad[slot, 1] = high
        save(up_grad.at[slot], up_out.at[t], 8 + t).start()

    def down_block(t):
        weight_block(line, cot, hidden, store_down, t)

    def gate_block(t):
        weight_block(order, normed, gate_act, store_gate, t)

    down_block(0)
    gate_block(0)
    both = terms(far * rows + half, diag * rows + half)
    scatter.send_diag(1, both[half:])
    far_terms[pl.ds(half, half), :] = both[:half]
    scatter.send_near(terms(core * rows, core * rows + half))
    scatter.send_far(1, far_terms[pl.ds(half, half), :])
    for block in (1, 2):
        down_block(block)
    own_terms[...] = terms(me * rows, me * rows + half)
    gate_block(2)
    down_block(3)
    cot_gather.wait_send()
    for peer in (core, far):
        pl.semaphore_signal(free, inc=1, device_id=group.at(peer), device_id_type=MESH)
    residual = grad_h1[...]
    pulled, gain_part = norm_pull(residual, gain_ff, scatter.total(own_terms[...]))
    gain_grad[...] = gain_part
    own_terms[...] = residual
    grad = cot[own, :].astype(f32) + pulled
    grad_h1[...] = grad
    cot[own, :] = grad.astype(bf16)
    third = Gather(links, group, cot, rows, 2)
    pl.semaphore_wait(free, 2)
    third.start()
    keep_result(grad_h1, grad_h1_out)
    gate_block(1)
    gate_block(3)
    scatter.wait_send()
    out_again = pltpu.make_async_copy(w_out, tx.at[0, 0:depth], local.at[spots - 1])
    out_again.start()

    def ff_terms(dev):
        return mm(hidden[block_rows(dev, rows), :], wd[...])

    tx_ff[0] = ff_terms(diag).astype(bf16)
    ff_diag.start()
    tx_ff[1] = ff_terms(core).astype(bf16)
    ff_near.start()
    own_part = ff_terms(far)
    ff_diag.wait_recv()
    ff_far[...] = (own_part + rx_ff[0].astype(f32)).astype(bf16)
    keep_result(ff_far, ff_far_out)
    own_part = ff_terms(me)
    ff_near.wait_recv()
    own_terms[...] += own_part + rx_ff[1].astype(f32)
    keep_result(own_terms, own_terms_out)
    def mix_back(dev):
        at = block_rows(dev, rows)
        grad_mixed[at, :] = contract_cols(cot[at, :], tx[0, 0:depth, :]).astype(bf16)

    weight_blocks(line, normed, up_act, store_up)
    out_again.wait()
    mix_back(me)
    third.near.wait_recv()
    mix_back(core)
    third.forward(0)

    def sum_down(t):
        y_copy(t).wait_recv()
        down_grad[t, y] = (
            down_grad[t, y].astype(f32) + y_recv[t].astype(f32)
        ).astype(bf16)
        save(down_grad.at[t, y], down_out.at[t], t).start()

    def sum_gate(i):
        for side in range(2):
            z_copy(i, side).wait_recv()
            kept = gate_grad.at[2 * i + 1, side]
            kept[...] = (kept[...].astype(f32) + z_recv[i, side].astype(f32)).astype(bf16)
            save(kept, gate_out.at[i, side], 4 + 2 * i + side).start()

    if exchange:
        sum_down(0)
        sum_down(1)
        sum_gate(0)
        sum_down(2)
    third.forward(1)
    mix_back(far)
    for copy in third.passed:
        copy.wait_recv()
    mix_back(diag)

    def store_out(t, low, high):
        out_grad[t, 0] = low
        out_grad[t, 1] = high

    weight_blocks(line, cot, mixed, store_out)
    if exchange:
        sum_down(3)
        sum_gate(1)

    for t in range(4):
        if exchange:
            save(down_grad.at[t, y], down_out.at[t], t).wait()
            save(gate_grad.at[t // 2 * 2 + 1, t % 2], gate_out.at[t // 2, t % 2], 4 + t).wait()
            y_copy(t).wait_send()
            z_copy(t // 2, t % 2).wait_send()
        else:
            save(down_grad.at[t], down_out.at[t], t).wait()
            save(gate_grad.at[t], gate_out.at[t], 4 + t).wait()
        if t >= 2:
            save(up_grad.at[t % 2], up_out.at[t], 8 + t).wait()
    for copy in (mixed_near, mixed_far, mixed_diag):
        copy.wait_send()
    for copy in results:
        copy.wait()
    second.wait_send()
    third.wait_send()
    ff_diag.wait_send()
    ff_near.wait_send()


def in_vmem():
    return pl.BlockSpec(memory_space=pltpu.VMEM)


def anywhere():
    return pl.BlockSpec(memory_space=pl.ANY)


def in_smem():
    return pl.BlockSpec(memory_space=pltpu.SMEM)


def forward(exchange, tokens, gain_attn, gain_ff, offset_bucket, table, first, w_query, w_key, w_value, w_out, gate_w, up_w, down_w, cot):
    rows, width = tokens.shape
    length = 4 * rows
    cols = w_query.shape[0]
    ff = gate_w.shape[0]
    heads, buckets = table.shape
    part = width // 8
    shape = jax.ShapeDtypeStruct
    halves = (4, 2, part, ff)
    kept = [
        shape((3, length, cols), bf16),
        shape((length, cols), bf16),
        shape((length, 128), f32),
        shape((rows, width), bf16),
        shape((rows, width), f32),
        shape((rows, width), f32),
    ]
    return pl.pallas_call(
        functools.partial(forward_kernel, exchange, buckets),
        out_shape=(
            shape((length, cols), bf16),
            shape((4, 2, part, cols), bf16),
            shape((1, width), f32),
            shape((8, 2 * length), f32),
            *kept,
            shape((length, width), bf16),
            shape((4, part, ff) if exchange else halves, bf16),
            shape((2, 2, part, ff) if exchange else halves, bf16),
            shape(halves, bf16),
        ),
        in_specs=[in_vmem()] * 5 + [in_smem()] + [anywhere()] * 8,
        out_specs=[in_vmem()] * 4 + [anywhere()] * 10,
        scratch_shapes=[pltpu.VMEM(v.shape, v.dtype) for v in kept]
        + [
            pltpu.VMEM((length, width), bf16),
            pltpu.VMEM((length, width), bf16),
            pltpu.VMEM((ff, width), bf16),
            pltpu.VMEM((ff, width), bf16),
            pltpu.VMEM((ff, width), bf16),
            pltpu.VMEM((heads, 128, 2 * length), f32),
            pltpu.VMEM((length, ff), bf16),
            pltpu.VMEM((length, ff), bf16),
            pltpu.VMEM((length, ff), bf16),
            pltpu.VMEM((4, rows, cols), bf16),
            pltpu.VMEM((rows, cols), f32),
            pltpu.VMEM((rows, width), f32),
            pltpu.VMEM((3, rows, width), bf16),
            pltpu.VMEM((3, rows, width), bf16),
            pltpu.VMEM((2, rows, width), bf16),
            pltpu.VMEM((2, rows, width), bf16),
            pltpu.VMEM(halves, bf16),
            pltpu.VMEM(halves, bf16),
            pltpu.VMEM((2, 2, part, ff), bf16),
            pltpu.VMEM((4, part, ff) if exchange else (8, 128), bf16),
            pltpu.VMEM((2, 2, part, ff) if exchange else (8, 128), bf16),
            pltpu.SemaphoreType.DMA((56,)),
            pltpu.SemaphoreType.DMA((56,)),
            pltpu.SemaphoreType.DMA((32,)),
            pltpu.SemaphoreType.REGULAR,
        ],
        compiler_params=pltpu.CompilerParams(
            collective_id=0, has_side_effects=True, vmem_limit_bytes=VMEM_BYTES
        ),
    )(tokens, gain_attn, gain_ff, offset_bucket, table, first, w_query, w_key, w_value, w_out, gate_w, up_w, down_w, cot)


class Line:
    def __init__(self, links, dp, mp, own, y_recv, z_recv, sources=()):
        z, y = dp // 2, lax.rem(dp, 2)
        near = z + 1 - 2 * lax.rem(z, 2)
        self.own, self.y_recv, self.z_recv = own, y_recv, z_recv
        self.inner = (z == 1) | (z == 2)
        self.y_peer, self.near, self.across = (2 * z + 1 - y, mp), (2 * near + y, mp), (2 * lax.rem(z + 2, 4) + y, mp)
        self.middle = (2 * (3 - z) + y, mp)
        self.y_copies = [links.copy(src, y_recv.at[i], self.y_peer) for i, src in enumerate(sources)]
        base = links.used
        links.used += 5
        forth = jnp.where(self.inner, self.middle[0], self.near[0])
        step = jnp.where(self.inner, 3, 0)
        self.copies = [
            pltpu.make_async_remote_copy(
                src_ref=own.at[i],
                dst_ref=z_recv.at[slot],
                send_sem=links.send.at[base + i],
                recv_sem=links.recv.at[base + slot],
                device_id=(to, mp),
                device_id_type=MESH,
            )
            for i, (slot, to) in enumerate(((step, forth), (step + 1, forth), (2, self.near[0])))
        ]
        self.arrivals = [
            pltpu.make_async_remote_copy(
                src_ref=own.at[0],
                dst_ref=z_recv.at[slot],
                send_sem=links.send.at[base],
                recv_sem=links.recv.at[base + slot],
                device_id=self.near,
                device_id_type=MESH,
            )
            for slot in range(5)
        ]

    def add(self, i, other):
        self.own[i] = (self.own[i].astype(f32) + other.astype(f32)).astype(bf16)

    def begin(self, i):
        @pl.when(jnp.logical_not(self.inner))
        def _():
            self.copies[i].start()

    def take_y(self, i):
        self.y_copies[i].wait_recv()
        self.add(i, self.y_recv[i])
        if i < 3:
            self.begin(i)

    def relay(self, i):
        slot = (0, 1, 3)[i]

        @pl.when(self.inner)
        def _():
            self.arrivals[slot].wait_recv()
            self.add(i, self.z_recv[slot])
            self.copies[i].start()

    def total(self, out):
        self.arrivals[2].wait_recv()
        out[...] = self.own[3].astype(f32) + self.z_recv[2].astype(f32)

        @pl.when(self.inner)
        def _():
            self.arrivals[4].wait_recv()
            out[...] += self.z_recv[4].astype(f32)

    def wait_send(self):
        for copy in self.y_copies + self.copies:
            copy.wait_send()


class LastHalvings:
    def __init__(self, links, line, own, y_recv, z_recv, sources):
        self.own, self.y_recv, self.z_recv, self.inner = own, y_recv, z_recv, line.inner
        self.y_copies = [
            links.copy(src, y_recv.at[i], line.y_peer) for i, src in enumerate(sources)
        ]
        base = links.used
        links.used += 3

        def copy(i, src, slot, to):
            return pltpu.make_async_remote_copy(
                src_ref=src,
                dst_ref=z_recv.at[slot],
                send_sem=links.send.at[base + i],
                recv_sem=links.recv.at[base + slot],
                device_id=to,
                device_id_type=MESH,
            )

        mp = line.near[1]
        forth = (jnp.where(self.inner, line.middle[0], line.near[0]), mp)
        self.first = copy(0, own.at[0], jnp.where(self.inner, 1, 0), forth)
        self.inwards = copy(1, z_recv.at[0], 2, line.middle)
        self.outwards = copy(2, z_recv.at[1], 2, line.near)
        self.arrivals = [copy(0, own.at[0], slot, line.near) for slot in range(3)]

    def take_y(self, i):
        self.y_copies[i].wait_recv()
        self.own[i] = (self.own[i].astype(f32) + self.y_recv[i].astype(f32)).astype(bf16)
        if i == 0:
            self.first.start()

    def hand_on(self):
        @pl.when(self.inner)
        def _():
            self.arrivals[1].wait_recv()
            self.outwards.start()
            self.arrivals[0].wait_recv()
            self.inwards.start()

    def total(self):
        self.arrivals[2].wait_recv()
        return self.own[1].astype(f32) + self.z_recv[2].astype(f32)

    def wait_send(self):
        for copy in self.y_copies + [self.first]:
            copy.wait_send()

        @pl.when(self.inner)
        def _():
            self.outwards.wait_send()
            self.inwards.wait_send()


def back_kernel(
    exchange,
    buckets,
    small,
    qkv,
    lse,
    grad_mixed,
    out_grad,
    gain_ff_part,
    first,
    tokens_in,
    grad_h1_in,
    w_query_in,
    w_key_in,
    w_value_in,
    ff_base_in,
    normed_in,
    ff_far,
    down_in,
    gate_in,
    up_in,
    stats_out,
    attn_out,
    output,
    grad_input,
    gate_out,
    up_out,
    down_out,
    tokens,
    grad_h1,
    ff_base,
    w_query,
    w_key,
    w_value,
    gate_sum,
    up_sum,
    down_sum,
    normed,
    strip,
    strip_grad,
    key_head,
    value_head,
    query_sum,
    key_sum,
    value_sum,
    grad_qkv,
    own_terms,
    tx,
    rx,
    down_own,
    down_z,
    gate_own,
    gate_y,
    gate_z,
    up_own,
    up_y,
    up_z,
    attn_own,
    attn_send,
    attn_y,
    attn_z,
    attn_sum,
    ff_recv,
    stats,
    stats_recv,
    send,
    recv,
    local,
):
    group = Group()
    me, core, far, diag = group.me, group.core, group.far, group.diag
    rows, width = grad_h1.shape
    half = rows // 2
    length = 4 * rows
    part = width // 4
    heads = strip.shape[0]
    span = 2 * length
    links = Links(send, recv)
    dp = group.dp
    peers = [group.at(core), group.at(far)]
    copies = []

    def load(src, dst):
        copy = pltpu.make_async_copy(src, dst, local.at[len(copies)])
        copies.append(copy)
        return copy

    save_normed = load(normed_in, normed)
    late = [
        load(src, dst)
        for src, dst in (
            (tokens_in, tokens),
            (grad_h1_in, grad_h1),
            (ff_base_in, ff_base),
            (w_query_in, w_query),
            (w_key_in, w_key),
            (w_value_in, w_value),
        )
    ]
    if exchange:
        z, y = dp // 2, lax.rem(dp, 2)
        order = line_order(z)
        down = Line(links, dp, me, down_own, None, down_z)
        gate = LastHalvings(links, down, gate_own, gate_y, gate_z, [gate_in.at[i, 1 - y] for i in range(2)])
        up = Line(links, dp, me, up_own, up_y, up_z, [up_in.at[i, 1 - y] for i in range(4)])
        attn = Line(links, dp, me, attn_own, attn_y, attn_z, [attn_send.at[i] for i in range(4)])
        peers += [down.y_peer, down.near, down.across, down.middle]
        loads = [load(down_in.at[i], down_own.at[i]) for i in range(4)]
        gate_loads = [load(gate_in.at[i, y], gate_own.at[i]) for i in range(2)]
        up_loads = [load(up_in.at[i, y], up_own.at[i]) for i in range(4)]
        for copy in loads:
            copy.start()
    else:
        order = [0, 1, 2, 3]
    greet(peers)
    meet(peers)
    if exchange:
        for copy in gate.y_copies + up.y_copies:
            copy.start()
        for i in range(4):
            loads[i].wait()
            if i < 3:
                down.begin(i)
        for copy in gate_loads + up_loads:
            copy.start()
    for copy in [save_normed] + late:
        copy.start()
    scatter = Scatter(links, group, tx, rx, rows, 1)
    ff_copy = links.copy(ff_far, ff_recv, group.at(far))
    ff_copy.start()
    stages = []
    for i, to in enumerate(peers[2:5] + peers[:2]):
        stages.append(links.copy(stats.at[i], stats_recv.at[i], to))

    build_strips(strip, small, buckets)
    strip_grad[...] = jnp.zeros_like(strip_grad)
    query_sum[...] = jnp.zeros_like(query_sum)
    key_sum[...] = jnp.zeros_like(key_sum)
    value_sum[...] = jnp.zeros_like(value_sum)

    def attend_back(dev, h):
        at = block_rows(dev, rows)
        seen = visible_keys(dev, rows, length, first[0])
        query, grad = qkv[0, at, :], grad_mixed[at, :]
        lanes = head_lanes(query.shape, h)
        zero = jnp.zeros_like(query)
        scores = contract_cols(query, key_head[...])
        scores = jnp.where(seen, add_bias(scores, strip, h, dev, length), masked_score)
        probs = jnp.exp(scores - lse[at, h : h + 1])
        inner = contract_cols(grad, value_head[...])
        center = jnp.sum(probs * inner, axis=-1, keepdims=True)
        score_grad = (probs * (inner - center)).astype(bf16)
        query_sum[at, :] += mm(score_grad, key_head[...])
        key_sum[...] += contract_rows(score_grad, jnp.where(lanes, query, zero))
        value_sum[...] += contract_rows(probs.astype(bf16), jnp.where(lanes, grad, zero))
        count = length // 128
        for i in range(rows // 128):
            start = (count - 1 - i) * 128 - dev * rows
            to = pl.ds(pl.multiple_of(start, 128), length)
            strip_grad[h, :, to] += score_grad[i * 128 : (i + 1) * 128].astype(f32)

    def head_keys(h):
        key, value = qkv[1], qkv[2]
        lanes = head_lanes(key.shape, h)
        key_head[...] = jnp.where(lanes, key, jnp.zeros_like(key))
        value_head[...] = jnp.where(lanes, value, jnp.zeros_like(value))

    def take_gate(i):
        gate_loads[i].wait()
        gate.take_y(i)

    def take_up(i):
        up_loads[i].wait()
        up.take_y(i)

    def down_total():
        down.total(down_sum)
        save(down_sum, down_out)

    def gate_total():
        gate_sum[...] = gate.total()
        save(gate_sum, gate_out)

    head_keys(0)
    between = {
        (0, 1): [lambda: take_gate(0)],
        (0, 2): [lambda: down.relay(0)],
        (1, 2): [lambda: take_gate(1), lambda: down.relay(1)],
        (1, 3): [lambda: down.relay(2)],
        (2, 2): [lambda: take_up(0)],
    } if exchange else {}
    for h in range(heads):
        if h:
            head_keys(h)
        for j, dev in enumerate((diag, far, core, me)):
            attend_back(dev, h)
            for step in between.get((h, j), []):
                step()

    grad_qkv[0] = query_sum[...].astype(bf16)
    grad_qkv[1] = key_sum[...].astype(bf16)
    grad_qkv[2] = value_sum[...].astype(bf16)

    def terms(dev):
        at = block_rows(dev, rows)
        return (
            mm(grad_qkv[0, at, :], w_query[...])
            + mm(grad_qkv[1, at, :], w_key[...])
            + mm(grad_qkv[2, at, :], w_value[...])
        )

    gain_parts = []

    def gain_terms(dev):
        value = terms(dev)
        product = value * normed[block_rows(dev, rows), :].astype(f32)
        gain_parts.append(jnp.sum(product, axis=0, keepdims=True))
        return value

    for copy in [save_normed] + late:
        copy.wait()
    saves = []

    def save(src, dst):
        saves.append(load(src, dst))
        saves[-1].start()

    scatter.send_diag(0, gain_terms(diag))
    scatter.send_near(gain_terms(core))
    scatter.send_far(0, gain_terms(far))
    own_terms[...] = gain_terms(me)

    index = small[2:3, :]
    lines = []
    for h in range(heads):
        fold = strip_grad[h]
        count = 128
        while count > 1:
            count //= 2
            fold = fold[:count] + pltpu.roll(fold[count:], span - count, 1)
        lines.append(pltpu.roll(fold, 127, 1))
    diagonals = jnp.concatenate(lines + [jnp.zeros((8 - heads, span), f32)], axis=0)
    onehot = (lax.broadcasted_iota(jnp.int32, (buckets, span), 0).astype(f32) == index).astype(f32)
    table_part = lax.dot_general(
        diagonals, onehot, (((1,), (1,)), ((), ())), precision=highest, preferred_element_type=f32
    )
    stats[0] = jnp.zeros_like(stats[0])
    stats[0, 0:1, :] = (gain_parts[0] + gain_parts[1] + gain_parts[2] + gain_parts[3]) / small[0:1, 0:width]
    stats[0, 1:2, :] = gain_ff_part[...]
    stats[0, 2 : 2 + heads, 0:buckets] = table_part[0:heads]
    stages[0].start()
    dp_stages = len(stages) - 2

    def next_stage(i):
        stages[i].wait_recv()
        total = stats[i] + stats_recv[i]
        if i >= dp_stages:
            row = lax.broadcasted_iota(jnp.int32, total.shape, 0)
            total = jnp.where(row < 2, total, stats[i])
        if i + 1 < len(stages):
            stats[i + 1] = total
            stages[i + 1].start()
        else:
            stats_out[...] = total

    cols = w_query.shape[0]
    for i in range(4):
        at = pl.ds(pl.multiple_of(order[i] * part, 128), part)
        for m in range(3):
            block = contract_rows(normed[:, at], grad_qkv[m]).astype(bf16)
            if exchange:
                low, high = block[: part // 2], block[part // 2 :]
                lanes = slice(m * cols, (m + 1) * cols)
                attn_send[i, :, lanes] = jnp.where(y == 0, high, low)
                attn_own[i, :, lanes] = jnp.where(y == 0, low, high)
            else:
                attn_out[m, at, :] = block
        if exchange:
            attn_send[i, :, 3 * cols :] = out_grad[i, 1 - y]
            attn_own[i, :, 3 * cols :] = out_grad[i, y]
            attn.y_copies[i].start()
        else:
            for side in range(2):
                attn_out[3, pl.ds(i * part + side * part // 2, part // 2), :] = out_grad[i, side]

    if exchange:
        take_up(1)
        down_total()
        gate.hand_on()
    ff_copy.wait_recv()
    ff_recv[...] = (ff_base[...] + ff_recv[...].astype(f32)).astype(bf16)
    save(ff_recv, output)

    def input_total():
        pulled, _ = norm_pull(tokens[...].astype(f32), small[0:1, 0:width], scatter.total(own_terms[...]))
        grad_h1[...] += pulled
        save(grad_h1, grad_input)

    if exchange:
        up.relay(0)
        take_up(2)
        take_up(3)
        next_stage(0)
        up.relay(1)
        attn.take_y(0)
        gate_total()
        input_total()
        up.relay(2)
        next_stage(1)
        attn.take_y(1)
        attn.relay(0)
        up.total(up_sum)
        save(up_sum, up_out)
        attn.take_y(2)
        attn.relay(1)
        attn.relay(2)
        next_stage(2)
        attn.take_y(3)
        next_stage(3)
        next_stage(4)
        attn.total(attn_sum)
        for m in range(3):
            attn_out[m] = attn_sum[:, m * cols : (m + 1) * cols]
        attn_out[3] = attn_sum[:, 3 * cols :].T
        down.wait_send()
        gate.wait_send()
        up.wait_send()
        attn.wait_send()
    else:
        input_total()
        next_stage(0)
        next_stage(1)
    for copy in saves:
        copy.wait()
    ff_copy.wait_send()
    scatter.wait_send()
    for stage in stages:
        stage.wait_send()


def attention_backward(
    exchange, table_shape, tokens, small, grad_h1, qkv, lse, w_query, w_key, w_value, grad_mixed, out_grad,
    gain_ff_part, ff_base, first, normed, ff_far, down_in, gate_in, up_in,
):
    rows, width = grad_h1.shape
    length = 4 * rows
    cols = w_query.shape[0]
    ff = down_in.shape[-1]
    buckets, heads = table_shape
    part = width // 8
    shape = jax.ShapeDtypeStruct
    ff_scratch = pltpu.VMEM((part, ff) if exchange else (8, 128), f32)
    scratch = [
        pltpu.VMEM((rows, width), bf16),
        pltpu.VMEM((rows, width), f32),
        pltpu.VMEM((rows, width), f32),
        pltpu.VMEM((cols, width), bf16),
        pltpu.VMEM((cols, width), bf16),
        pltpu.VMEM((cols, width), bf16),
        ff_scratch,
        ff_scratch,
        ff_scratch,
        pltpu.VMEM((length, width), bf16),
        pltpu.VMEM((heads, 128, 2 * length), f32),
        pltpu.VMEM((heads, 128, 2 * length), f32),
        pltpu.VMEM((length, cols), bf16),
        pltpu.VMEM((length, cols), bf16),
        pltpu.VMEM((length, cols), f32),
        pltpu.VMEM((length, cols), f32),
        pltpu.VMEM((length, cols), f32),
        pltpu.VMEM((3, length, cols), bf16),
        pltpu.VMEM((rows, width), f32),
        pltpu.VMEM((3, rows, width), bf16),
        pltpu.VMEM((3, rows, width), bf16),
    ]
    for count in (4, 5, 2, 2, 3, 4, 4, 5):
        scratch.append(pltpu.VMEM((count, part, ff) if exchange else (8, 128), bf16))
    for count in (4, 4, 4, 5):
        scratch.append(pltpu.VMEM((count, part, 4 * cols) if exchange else (8, 128), bf16))
    stages = 5 if exchange else 2
    scratch += [
        pltpu.VMEM((part, 4 * cols), f32),
        pltpu.VMEM((rows, width), bf16),
        pltpu.VMEM((stages, 8, width), f32),
        pltpu.VMEM((stages, 8, width), f32),
        pltpu.SemaphoreType.DMA((48,)),
        pltpu.SemaphoreType.DMA((48,)),
        pltpu.SemaphoreType.DMA((24,)),
    ]
    ff_out = shape((part, ff) if exchange else (8, 128), f32)
    return pl.pallas_call(
        functools.partial(back_kernel, exchange, buckets),
        out_shape=(
            shape((8, width), f32),
            shape((4, part, cols), f32) if exchange else shape((4, width, cols), bf16),
            shape((rows, width), bf16),
            shape((rows, width), f32),
            ff_out,
            ff_out,
            ff_out,
        ),
        in_specs=[in_vmem()] * 6 + [in_smem()] + [anywhere()] * 11,
        out_specs=[in_vmem()] * 2 + [anywhere()] * 5,
        scratch_shapes=scratch,
        compiler_params=pltpu.CompilerParams(
            collective_id=1, has_side_effects=True, vmem_limit_bytes=VMEM_BYTES
        ),
    )(
        small, qkv, lse, grad_mixed, out_grad, gain_ff_part, first, tokens, grad_h1, w_query, w_key, w_value,
        ff_base, normed, ff_far, down_in, gate_in, up_in,
    )


def finish_kernel(heads, *refs):
    ins, outs, (attn_held, *held, load, save) = refs[:7], refs[7:19], refs[19:]
    stats, attn = ins[0], ins[1]
    sources = list(ins[2:]) + [attn.at[i] for i in range(4)]
    slots = held + [attn_held.at[i] for i in range(4)]
    targets = list(outs[4:9]) + list(outs[:4])
    loads = [pltpu.make_async_copy(a, b, load.at[i]) for i, (a, b) in enumerate(zip(sources, slots))]
    saves = [pltpu.make_async_copy(a, b, save.at[i]) for i, (a, b) in enumerate(zip(slots, targets))]
    for copy in loads:
        copy.start()
    gain_attn, gain_ff, table = outs[9:]
    gain_attn[...] = stats[0]
    gain_ff[...] = stats[1]
    table[...] = stats[2 : 2 + heads, 0 : table.shape[1]]
    for before, after in zip(loads, saves):
        before.wait()
        after.start()
    for copy in saves:
        copy.wait()


def finish(table_shape, stats, attn, *whole):
    buckets, heads = table_shape
    shape = jax.ShapeDtypeStruct
    outs = [shape(attn.shape[1:], f32)] * 4 + [shape(v.shape, v.dtype) for v in whole]
    small = [shape(stats.shape[1:], f32)] * 2 + [shape((heads, buckets), f32)]
    return pl.pallas_call(
        functools.partial(finish_kernel, heads),
        out_shape=outs + small,
        in_specs=[in_vmem()] + [anywhere()] * 6,
        out_specs=[anywhere()] * 9 + [in_vmem()] * 3,
        scratch_shapes=[pltpu.VMEM(v.shape, v.dtype) for v in (attn, *whole)]
        + [pltpu.SemaphoreType.DMA((9,))] * 2,
        compiler_params=pltpu.CompilerParams(vmem_limit_bytes=VMEM_BYTES),
    )(stats, attn, *whole)


def shards(
    tokens,
    gain_attn,
    w_query,
    w_key,
    w_value,
    w_out,
    bias_table,
    gain_ff,
    w_gate,
    w_up,
    w_down,
    cotangent,
    first_length,
    offset_bucket,
):
    n_dp = lax.axis_size("dp")
    exchange = n_dp == 8
    buckets, heads = bias_table.shape
    width = tokens.shape[1]
    turned = [w_query.T, w_key.T, w_value.T]
    grad_mixed, out_grad, gain_ff_part, small, qkv, mixed, lse, ff_far, ff_base, grad_h1, normed, down, gate, up = forward(
        exchange, tokens, gain_attn, gain_ff, offset_bucket, bias_table.T, first_length, *turned, w_out, w_gate.T, w_up.T, w_down, cotangent
    )
    stats, attn, output, grad_input, gate_sum, up_sum, down_sum = attention_backward(
        exchange, bias_table.shape, tokens, small, grad_h1, qkv, lse, *turned, grad_mixed, out_grad, gain_ff_part,
        ff_base, first_length, normed, ff_far, down, gate, up,
    )
    if exchange:
        *attn, output, grad_input, gate_sum, up_sum, down_sum, gain_first, gain_second, table = finish(
            bias_table.shape, stats, attn, output, grad_input, gate_sum, up_sum, down_sum
        )
    else:
        def scatter(value):
            value = value.reshape(width, -1).astype(f32)
            return lax.psum_scatter(value, "dp", scatter_dimension=0, tiled=True)

        stats = lax.psum(stats, "dp")
        gate_sum, up_sum, down_sum = scatter(gate), scatter(up), scatter(down)
        attn = [scatter(attn[i]) for i in range(4)]
        attn[3] = attn[3].T
        gain_first, gain_second, table = stats[0], stats[1], stats[2 : 2 + heads, :buckets]
    return (
        output,
        grad_input,
        gain_first,
        attn[0],
        attn[1],
        attn[2],
        attn[3],
        table.T,
        gain_second,
        gate_sum,
        up_sum,
        down_sum.T,
    )


def solution(mesh):
    placed = (
        P(("dp", "mp"), None),
        P(),
        P(None, "mp"),
        P(None, "mp"),
        P(None, "mp"),
        P("mp", None),
        P(None, "mp"),
        P(),
        P(None, "mp"),
        P(None, "mp"),
        P("mp", None),
        P(("dp", "mp"), None),
        P("dp"),
        P(),
    )
    return jax.shard_map(
        shards,
        mesh=mesh,
        in_specs=placed,
        out_specs=(
            P(("dp", "mp"), None),
            P(("dp", "mp"), None),
            P(),
            P("dp", "mp"),
            P("dp", "mp"),
            P("dp", "mp"),
            P("mp", "dp"),
            P(None, "mp"),
            P(),
            P("dp", "mp"),
            P("dp", "mp"),
            P("mp", "dp"),
        ),
        check_vma=False,
    )
```
